256 devices in a mesh: grp: 8 (over y, core), box: 32 (over x, z).
Axes of the slice: x: 4, y: 4, z: 8, core: 2. Of those that a mesh axis runs over, the one named last changes fastest.
Arguments:
- source: float32 [128, 256, 256], P('grp', 'box'), may hold values from -16 to 30
- alpha: float32 [128, 256, 256], P('grp', 'box'), may hold values from 0.02 to 0.4
- beta: float32 [128, 256, 256], P('grp', 'box'), may hold values from 0.3 to 3
Outputs:
- correction: float32 [128, 256, 256], P('grp', 'box')
The draws below stay inside these ranges and needn't reach their ends.
All inputs are finite; a program needn't handle non-finite values.
Results may differ from the reference program's by a relative error of at most 0.00002.
Values sent between devices are 32-bit elements; how exact they have to be, the bound alone decides.
A program may use at most 128 MiB of HBM per device.

```python
import math
from functools import partial
import jax
import jax.numpy as jnp

CZ = 256
SMOOTH = 4
BOTTOM = 16
NX = 128
NY = 256


def smooth_field(key, amplitude):
    phases = jax.random.uniform(key, (3,), jnp.float32, 0.0, 2.0 * math.pi)
    first = jnp.sin(2.0 * math.pi * jnp.arange(NX, dtype=jnp.float32) / NX + phases[0])
    second = jnp.cos(2.0 * math.pi * jnp.arange(NY, dtype=jnp.float32) / NY + phases[1])
    third = jnp.cos(2.0 * math.pi * jnp.arange(CZ, dtype=jnp.float32) / CZ + phases[2])
    product = first[:, None, None] * second[None, :, None] * third[None, None, :]
    return amplitude * (1.5 + product)


def draw_source(key, part):
    key = jax.random.fold_in(key, 7)
    rough_key, smooth_key = jax.random.split(key, 2)
    rough = jnp.clip(4.0 * jax.random.normal(rough_key, (NX, NY, CZ), jnp.float32), -16.0, 16.0)
    amplitude = 4.0
    return (rough + smooth_field(smooth_key, amplitude)).astype(jnp.float32)


def steps_of(key, shape, shards, low, high):
    loudness = 1.0
    for axis_at, blocks in shards:
        heights = jax.random.uniform(jax.random.fold_in(jax.random.fold_in(key, 6), axis_at), (blocks,), jnp.float32, low / len(shards), high / len(shards))
        loudness = loudness * jnp.repeat(jnp.exp(heights), shape[axis_at] // blocks).reshape((-1,) + (1,) * (len(shape) - 1 - axis_at))
    return loudness


def setup_inputs(seed: int = 0) -> dict:
    key_list = jax.random.split(jax.random.key(seed), 4)
    source = draw_source(jax.random.fold_in(key_list[3], 71), 0)
    alpha = jnp.clip(jnp.exp(math.log(0.4) - 2.9957323 * jax.random.uniform(key_list[1], (NX, NY, CZ), jnp.float32) ** steps_of(key_list[1], (NX, NY, CZ), ((0, 8), (1, 32)), -0.2, 0.2)), 0.02, 0.4)
    beta = jnp.clip(jnp.exp(math.log(3.0) - 2.3025851 * jax.random.uniform(key_list[2], (NX, NY, CZ), jnp.float32) ** steps_of(key_list[2], (NX, NY, CZ), ((0, 8), (1, 32)), -0.2, 0.2)), 0.3, 3.0)
    return {"source": source, "alpha": alpha, "beta": beta}


SMOOTH_LOW = 0.25
BOTTOM_LOW = 0.02
UPPER_BOUND = 2.0


def whole_pad(field):
    return jnp.pad(field, 1)


def couplings(alpha, beta, scale, padder):
    padded = padder(beta)
    east = scale * 0.5 * (beta + padded[2:, 1:-1, 1:-1])
    west = scale * 0.5 * (beta + padded[:-2, 1:-1, 1:-1])
    north = scale * 0.5 * (beta + padded[1:-1, 2:, 1:-1])
    south = scale * 0.5 * (beta + padded[1:-1, :-2, 1:-1])
    above = scale * 0.5 * (beta + padded[1:-1, 1:-1, 2:])
    below = scale * 0.5 * (beta + padded[1:-1, 1:-1, :-2])
    diagonal = alpha + east + west + north + south + above + below
    return (diagonal, east, west, north, south, above, below)


def operate(field, table, padder):
    padded = padder(field)
    result = table[0] * field - table[1] * padded[2:, 1:-1, 1:-1] - table[2] * padded[:-2, 1:-1, 1:-1]
    result = result - table[3] * padded[1:-1, 2:, 1:-1] - table[4] * padded[1:-1, :-2, 1:-1]
    return result - table[5] * padded[1:-1, 1:-1, 2:] - table[6] * padded[1:-1, 1:-1, :-2]


def restrict(field):
    sizes = field.shape
    return field.reshape(sizes[0] // 2, 2, sizes[1] // 2, 2, sizes[2] // 2, 2).mean(axis=(1, 3, 5))


def prolong(field):
    return jnp.repeat(jnp.repeat(jnp.repeat(field, 2, 0), 2, 1), 2, 2)


def chebyshev(operator, diagonal, source, guess, degree, lower):
    middle = (UPPER_BOUND + lower) / 2.0
    spread = (UPPER_BOUND - lower) / 2.0
    ratio_base = middle / spread
    factor_now = 1.0 / ratio_base
    if guess is None:
        residual = source
        approx = jnp.zeros_like(source)
    else:
        residual = source - operator(guess)
        approx = guess
    update = residual / (diagonal * middle)
    approx = approx + update
    for k in range(degree - 1):
        residual = source - operator(approx)
        factor_next = 1.0 / (2.0 * ratio_base - factor_now)
        update = factor_next * factor_now * update + (2.0 * factor_next / spread) * residual / diagonal
        approx = approx + update
        factor_now = factor_next
    return approx


def reference(source, alpha, beta):
    fine = couplings(alpha, beta, 1.0, whole_pad)
    fine_op = partial(operate, table=fine, padder=whole_pad)
    approx_three = chebyshev(fine_op, fine[0], source, None, SMOOTH, SMOOTH_LOW)
    source_four = restrict(source - fine_op(approx_three))
    alpha_four = restrict(alpha)
    beta_four = restrict(beta)
    middle_table = couplings(alpha_four, beta_four, 0.25, whole_pad)
    middle_op = partial(operate, table=middle_table, padder=whole_pad)
    approx_four = chebyshev(middle_op, middle_table[0], source_four, None, SMOOTH, SMOOTH_LOW)
    source_five = restrict(source_four - middle_op(approx_four))
    coarse = couplings(restrict(alpha_four), restrict(beta_four), 0.0625, whole_pad)
    coarse_op = partial(operate, table=coarse, padder=whole_pad)
    approx_five = chebyshev(coarse_op, coarse[0], source_five, None, BOTTOM, BOTTOM_LOW)
    approx_four = chebyshev(middle_op, middle_table[0], source_four, approx_four + prolong(approx_five), SMOOTH, SMOOTH_LOW)
    return chebyshev(fine_op, fine[0], source, approx_three + prolong(approx_four), SMOOTH, SMOOTH_LOW)
```

```python
import jax
import jax.numpy as jnp
from jax import lax
from jax.experimental import pallas as pl
from jax.experimental.pallas import tpu as pltpu
from jax.sharding import PartitionSpec as P

SMOOTH = 4
BOTTOM = 16
SMOOTH_LOW = 0.25
BOTTOM_LOW = 0.02
UPPER_BOUND = 2.0

MESH = pl.DeviceIdType.MESH
F32 = jnp.float32
NG, NB = 8, 32
N0, N1, N2 = 16, 8, 256
REACH = 9
MID = REACH + 1
SPAN = 2 * MID + 1

FACES = [(dg, db) for db in (-1, 1, 0) for dg in (0, -1, 1) if (dg, db) != (0, 0)]
WIDE = [(dg, db) for db in (-2, 2, -1, 1, 0) for dg in (0, -1, 1) if (dg, db) != (0, 0)]


def coefficients(degree, lower):
    middle = (UPPER_BOUND + lower) / 2.0
    spread = (UPPER_BOUND - lower) / 2.0
    base = middle / spread
    now = 1.0 / base
    pairs = []
    for _ in range(degree - 1):
        after = 1.0 / (2.0 * base - now)
        pairs.append((after * now, 2.0 * after / spread))
        now = after
    return middle, pairs


def part(step, size, width, origin):
    if step == 0:
        return 0, origin, size
    if step == 2:
        return size - (width - size), origin - width, width - size
    if step == -2:
        return 0, origin + 2 * size, width - size
    width = min(width, size)
    if step == 1:
        return size - width, origin - width, width
    return 0, origin + size, width


def kernel(
    source, alpha, beta, out,
    f3, a3, b3, t3, d3, fd3, x3a, x3b, h3,
    ab4, f4, p4, t4, inv4, d4, fd4, x4a, x4b, w4,
    z5, g5ab, g5f, t5, inv5, fd5, x5a, x5b, q4, w3, u4,
    own_sem, ends,
    s_p1, r_p1, s_ab4, r_ab4, s_f4, r_f4, s_x3, r_x3, s_p4, r_p4,
    s_aba, r_aba, s_abb, r_abb, s_abc, r_abc, s_fa, r_fa, s_fb, r_fb, s_fc, r_fc,
):
    g, b = lax.axis_index("grp"), lax.axis_index("box")
    core, chip = lax.rem(g, 2), g // 2
    sub = 4 * core + chip

    def device(dg, db):
        return (lax.rem(g + dg + NG, NG), lax.rem(b + db + NB, NB))

    def remote(src, dst, send, recv, target):
        copy = pltpu.make_async_remote_copy(
            src_ref=src, dst_ref=dst, send_sem=send, recv_sem=recv, device_id=target, device_id_type=MESH
        )
        copy.start()
        return copy

    started = []

    own = [
        pltpu.make_async_copy(beta, b3.at[pl.ds(5, N0), pl.ds(8, N1), :], own_sem.at[0]),
        pltpu.make_async_copy(alpha, a3.at[pl.ds(4, N0), pl.ds(4, N1), :], own_sem.at[1]),
        pltpu.make_async_copy(source, f3.at[pl.ds(4, N0), pl.ds(4, N1), :], own_sem.at[2]),
    ]
    for copy in own:
        copy.start()

    f4[...] = jnp.zeros_like(f4)

    partners = set(FACES) | set(WIDE) | {(2, 0), (4, 0), (6, 0)}
    partners |= {(0, k) for k in range(-MID, MID + 1) if k}
    partners = sorted(partners, key=lambda p: -abs(p[1]))
    barrier = pltpu.get_barrier_semaphore()
    for dg, db in partners:
        pl.semaphore_signal(barrier, inc=1, device_id=device(dg, db), device_id_type=MESH)

    x3a[...] = jnp.zeros_like(x3a)
    x4a[...] = jnp.zeros_like(x4a)
    x5a[...] = jnp.zeros_like(x5a)
    x5b[...] = jnp.zeros_like(x5b)

    pl.semaphore_wait(barrier, len(partners))

    def halo(src, dst, dg, db, w0, w1, o0, o1, size, send, recv):
        s0, t0, l0 = part(dg, size[0], w0, o0)
        s1, t1, l1 = part(db, size[1], w1, o1)
        return remote(
            src(s0, l0, s1, l1), dst(t0, l0, t1, l1), send, recv, device(dg, db)
        )

    def window(ref):
        return lambda i, n, j, m: ref.at[pl.ds(i, n), pl.ds(j, m), :]

    def window2(ref):
        return lambda i, n, j, m: ref.at[:, pl.ds(i, n), pl.ds(j, m), :]

    def inner(ref, o0, o1):
        return lambda i, n, j, m: ref.at[pl.ds(o0 + i, n), pl.ds(o1 + j, m), :]

    def inner2(ref, o0, o1):
        return lambda i, n, j, m: ref.at[:, pl.ds(o0 + i, n), pl.ds(o1 + j, m), :]

    p1 = []
    for n, (src, dst, w, o0, o1) in enumerate(
        ((beta, b3, 5, 5, 8), (alpha, a3, 4, 4, 4), (source, f3, 4, 4, 4))
    ):
        for k, (dg, db) in enumerate(FACES):
            p1.append(
                halo(window(src), window(dst), dg, db, w, w, o0, o1, (N0, N1), s_p1.at[n, k], r_p1.at[n, k])
            )
    started += p1

    rows256 = lax.broadcasted_iota(jnp.int32, (256, 128), 0)
    cols128 = lax.broadcasted_iota(jnp.int32, (256, 128), 1)
    gather = jnp.where(lax.shift_right_logical(rows256, 1) == cols128, 1.0, 0.0).astype(F32)
    rows128 = lax.broadcasted_iota(jnp.int32, (128, 256), 0)
    cols256 = lax.broadcasted_iota(jnp.int32, (128, 256), 1)
    spread = jnp.where(lax.shift_right_logical(cols256, 1) == rows128, 1.0, 0.0).astype(F32)

    def dot(x, matrix):
        return jnp.dot(x, matrix, precision=lax.Precision.HIGHEST, preferred_element_type=F32)

    def halve(pairs, o1):
        n = pairs.shape[1]
        w4[:, 0:n, :] = dot(pairs.reshape(8 * n, 256), gather).reshape(8, n, 128)
        return 0.125 * (w4[:, pl.ds(o1, 4, stride=2), :] + w4[:, pl.ds(o1 + 1, 4, stride=2), :])

    def pack(get, row):
        for i in range(4):
            t = get(2 * i) + get(2 * i + 1)
            z5[pl.ds(row + i, 1), 0:128] = t[0:1] + t[1:2]
            z5[pl.ds(row + i, 1), 128:256] = t[2:3] + t[3:4]

    for copy in own[:2]:
        copy.wait()
    ab4[0, 6:14, 6:10, :] = halve(
        jnp.stack([a3[4 + 2 * i, 4:12, :] + a3[5 + 2 * i, 4:12, :] for i in range(8)]), 0
    )
    ab4[1, 6:14, 6:10, :] = halve(
        jnp.stack([b3[5 + 2 * i, 8:16, :] + b3[6 + 2 * i, 8:16, :] for i in range(8)]), 0
    )
    ab4_copies = []
    for k, (dg, db) in enumerate(WIDE):
        ab4_copies.append(
            halo(inner2(ab4, 6, 6), window2(ab4), dg, db, 6, 6, 6, 6, (8, 4), s_ab4.at[k], r_ab4.at[k])
        )
    started += ab4_copies
    for n in range(2):
        pack(lambda r, n=n: ab4[n, 6 + r, 6:10, :], 4 * n)
    packed = 0.125 * dot(z5[...], gather)
    for n in range(2):
        for i in range(4):
            g5ab[n, MID, i, pl.ds(sub, 1), :] = packed[4 * n + i : 4 * n + i + 1]
    abb = []
    for k, db in enumerate([s * d for d in range(MID, 0, -1) for s in (-1, 1)]):
        abb.append(
            remote(
                g5ab.at[:, MID, :, pl.ds(sub, 1), :],
                g5ab.at[:, MID - db, :, pl.ds(sub, 1), :],
                s_abb.at[k], r_abb.at[k], device(0, db),
            )
        )
    started += abb

    own[2].wait()
    for copy in p1:
        copy.wait_recv()

    def inside(start, shape, axis, count):
        at = lax.broadcasted_iota(jnp.int32, shape, axis) + start
        return (at >= 0) & (at < count)

    lanes3 = lax.broadcasted_iota(jnp.int32, (16, 256), 1)
    m3c = inside(N1 * b - 4, (16, 256), 0, N1 * NB)
    m3n = inside(N1 * b - 3, (16, 256), 0, N1 * NB)
    m3s = inside(N1 * b - 5, (16, 256), 0, N1 * NB)

    def row_in(r, size, origin):
        at = size * g + r - origin
        return jnp.where((at >= 0) & (at < size * NG), 1.0, 0.0).astype(F32)

    def table3(r, carry):
        here = row_in(r, N0, 4)
        bc = jnp.where(m3c, b3[r + 1, pl.ds(4, 16), :], 0.0) * here
        be = jnp.where(m3c, b3[r + 2, pl.ds(4, 16), :], 0.0) * row_in(r + 1, N0, 4)
        bw = jnp.where(m3c, b3[r, pl.ds(4, 16), :], 0.0) * row_in(r - 1, N0, 4)
        bn = jnp.where(m3n, b3[r + 1, pl.ds(5, 16), :], 0.0) * here
        bs = jnp.where(m3s, b3[r + 1, pl.ds(3, 16), :], 0.0) * here
        bu = jnp.where(lanes3 == 255, 0.0, pltpu.roll(bc, 255, 1))
        bd = jnp.where(lanes3 == 0, 0.0, pltpu.roll(bc, 1, 1))
        c = [0.5 * (bc + v) for v in (be, bw, bn, bs, bu, bd)]
        diag = a3[r] + c[0] + c[1] + c[2] + c[3] + c[4] + c[5]
        inv = jnp.where(m3c, 1.0 / diag, 0.0) * here
        for n in range(4):
            t3[n, r] = c[n] * inv
        t3[4, r] = jnp.where(lanes3 == 255, 0.0, c[4] * inv)
        t3[5, r] = jnp.where(lanes3 == 0, 0.0, c[5] * inv)
        d3[r] = diag
        fd = f3[r] * inv
        fd3[r] = fd
        x3b[r] = fd * (1.0 / smooth_middle)
        return carry

    smooth_middle, smooth_pairs = coefficients(SMOOTH, SMOOTH_LOW)
    lax.fori_loop(0, 24, table3, 0, unroll=4)

    def scaled_residual(t, fd, x, r):
        here = x[r]
        n, m = here.shape
        total = fd[r] - here
        total = total + t[0, r] * x[r + 1] + t[1, r] * x[r - 1]
        total = total + t[2, r] * pltpu.roll(here, n - 1, 0) + t[3, r] * pltpu.roll(here, 1, 0)
        return total + t[4, r] * pltpu.roll(here, m - 1, 1) + t[5, r] * pltpu.roll(here, 1, 1)

    def sweep(t, fd, now, old, lo, hi, chunk, pair):
        def rows(k, carry):
            for i in range(chunk):
                r = lo + k * chunk + i
                total = scaled_residual(t, fd, now, r)
                here = now[r]
                if len(pair) == 1:
                    old[r] = here + pair[0] * total
                else:
                    old[r] = here + pair[0] * (here - old[r]) + pair[1] * total
            return carry

        lax.fori_loop(0, (hi - lo) // chunk, rows, 0)

    sweep(t3, fd3, x3b, x3a, 1, 23, 11, smooth_pairs[0])
    sweep(t3, fd3, x3a, x3b, 2, 22, 10, smooth_pairs[1])
    sweep(t3, fd3, x3b, x3a, 3, 21, 9, smooth_pairs[2])

    def fine_residual(i):
        return d3[i] * scaled_residual(t3, fd3, x3a, i)

    for i in range(8):
        w3[i] = fine_residual(4 + 2 * i) + fine_residual(5 + 2 * i)
    f4[6:14, 6:10, :] = halve(w3[...], 4)
    f4_copies = []
    for k, (dg, db) in enumerate(FACES):
        f4_copies.append(
            halo(inner(f4, 6, 6), window(f4), dg, db, 4, 4, 6, 6, (8, 4), s_f4.at[k], r_f4.at[k])
        )
    started += f4_copies
    for i in range(16):
        h3[4 + i, 4:12, :] = x3a[4 + i, 4:12, :]
    x3_copies = []
    for k, (dg, db) in enumerate(FACES):
        x3_copies.append(
            halo(inner(h3, 4, 4), window(h3), dg, db, 4, 4, 4, 4, (N0, N1), s_x3.at[k], r_x3.at[k])
        )
    started += x3_copies

    for copy in abb:
        copy.wait_recv()
    aba = []
    for k, dg in enumerate((2, 4, 6)):
        aba.append(
            remote(
                g5ab.at[:, :, :, pl.ds(sub, 1), :], g5ab.at[:, :, :, pl.ds(sub, 1), :],
                s_aba.at[k], r_aba.at[k], device(dg, 0),
            )
        )
    started += aba

    for copy in ab4_copies:
        copy.wait_recv()
    lanes4 = lax.broadcasted_iota(jnp.int32, (16, 128), 1)
    m4 = inside(4 * b - 6, (16, 128), 0, 4 * NB)

    def masked4(r):
        return jnp.where(m4, ab4[1, r], 0.0) * row_in(r, 8, 6)

    def table4(r, carry):
        bc = masked4(r)
        be, bw = masked4(r + 1), masked4(r - 1)
        bn, bs = pltpu.roll(bc, 15, 0), pltpu.roll(bc, 1, 0)
        bu = jnp.where(lanes4 == 127, 0.0, pltpu.roll(bc, 127, 1))
        bd = jnp.where(lanes4 == 0, 0.0, pltpu.roll(bc, 1, 1))
        c = [0.125 * (bc + v) for v in (be, bw, bn, bs, bu, bd)]
        diag = ab4[0, r] + c[0] + c[1] + c[2] + c[3] + c[4] + c[5]
        inv = jnp.where(m4, 1.0 / diag, 0.0) * row_in(r, 8, 6)
        for n in range(4):
            t4[n, r] = c[n] * inv
        t4[4, r] = jnp.where(lanes4 == 127, 0.0, c[4] * inv)
        t4[5, r] = jnp.where(lanes4 == 0, 0.0, c[5] * inv)
        d4[r] = diag
        inv4[r] = inv
        return carry

    lax.fori_loop(1, 19, table4, 0, unroll=6)

    mine = pl.ds(pl.multiple_of(4 * core, 4), 4)
    partner = (g + 1 - 2 * core, b)
    for copy in aba:
        copy.wait_recv()
    abc = remote(
        g5ab.at[:, :, :, mine, :], g5ab.at[:, :, :, mine, :], s_abc.at[0], r_abc.at[0], partner
    )
    started.append(abc)

    for copy in f4_copies:
        copy.wait_recv()
    for r in range(2, 18):
        fd = f4[r] * inv4[r]
        fd4[r] = fd
        x4b[r] = fd * (1.0 / smooth_middle)
    sweep(t4, fd4, x4b, x4a, 3, 17, 14, smooth_pairs[0])
    sweep(t4, fd4, x4a, x4b, 4, 16, 12, smooth_pairs[1])
    sweep(t4, fd4, x4b, x4a, 5, 15, 10, smooth_pairs[2])

    for r in range(8):
        w4[r] = d4[6 + r] * scaled_residual(t4, fd4, x4a, 6 + r)
    pack(lambda r: w4[r, 6:10, :], 0)
    packed = 0.125 * dot(z5[...], gather)
    for i in range(4):
        g5f[MID, i, pl.ds(sub, 1), :] = packed[i : i + 1]
    fa = []
    for k, dg in enumerate((2, 4, 6)):
        fa.append(
            remote(
                g5f.at[MID, :, pl.ds(sub, 1), :], g5f.at[MID, :, pl.ds(sub, 1), :],
                s_fa.at[k], r_fa.at[k], device(dg, 0),
            )
        )
    started += fa

    p4[0, 6:14, 6:10, :] = f4[6:14, 6:10, :]
    p4[1, 6:14, 6:10, :] = x4a[6:14, 6:10, :]
    for copy in fa:
        copy.wait_recv()
    fb = []
    for k, db in enumerate([s * d for d in range(REACH, 0, -1) for s in (-1, 1)]):
        fb.append(
            remote(
                g5f.at[MID, :, mine, :], g5f.at[MID - db, :, mine, :],
                s_fb.at[k], r_fb.at[k], device(0, db),
            )
        )
    started += fb
    p4_copies = []
    for k, (dg, db) in enumerate(WIDE):
        p4_copies.append(
            halo(inner2(p4, 6, 6), window2(p4), dg, db, 6, 6, 6, 6, (8, 4), s_p4.at[k], r_p4.at[k])
        )
    started += p4_copies

    abc.wait_recv()
    lanes5 = lax.broadcasted_iota(jnp.int32, (8, 128), 1)
    subs5 = lax.broadcasted_iota(jnp.int32, (8, 128), 0)
    low = lanes5 < 64
    front = subs5 < 4
    up_end = (lanes5 == 63) | (lanes5 == 127)
    down_end = (lanes5 == 0) | (lanes5 == 64)

    def next_group(v):
        return jnp.where(front, pltpu.roll(v, 4, 0), pltpu.roll(v, 3, 0))

    def last_group(v):
        return jnp.where(front, pltpu.roll(v, 5, 0), pltpu.roll(v, 4, 0))

    def box_in(k):
        at = b + k - MID
        return jnp.where((at >= 0) & (at < NB), 1.0, 0.0).astype(F32)

    def beta5(k, i):
        return g5ab[1, k, i] * box_in(k)

    def table5(k, carry):
        bc = [beta5(k, i) for i in range(4)]
        half = [pltpu.roll(v, 64, 1) for v in bc]
        after = [pltpu.roll(beta5(k + 1, i), 64, 1) for i in range(4)]
        before = [pltpu.roll(beta5(k - 1, i), 64, 1) for i in range(4)]
        for i in range(4):
            be = bc[i + 1] if i < 3 else jnp.where(subs5 == 7, 0.0, next_group(bc[0]))
            bw = bc[i - 1] if i > 0 else jnp.where(subs5 == 0, 0.0, last_group(bc[3]))
            bn = jnp.where(low, half[i], after[i])
            bs = jnp.where(low, before[i], half[i])
            bu = jnp.where(up_end, 0.0, pltpu.roll(bc[i], 127, 1))
            bd = jnp.where(down_end, 0.0, pltpu.roll(bc[i], 1, 1))
            c = [0.03125 * (bc[i] + v) for v in (be, bw, bn, bs, bu, bd)]
            diag = g5ab[0, k, i] + c[0] + c[1] + c[2] + c[3] + c[4] + c[5]
            inv = box_in(k) / diag
            t5[0, k, i] = c[0] * inv if i < 3 else jnp.where(subs5 == 7, 0.0, c[0] * inv)
            t5[1, k, i] = c[1] * inv if i > 0 else jnp.where(subs5 == 0, 0.0, c[1] * inv)
            t5[2, k, i] = c[2] * inv
            t5[3, k, i] = c[3] * inv
            t5[4, k, i] = jnp.where(up_end, 0.0, c[4] * inv)
            t5[5, k, i] = jnp.where(down_end, 0.0, c[5] * inv)
            inv5[k, i] = inv
        return carry

    lax.fori_loop(1, SPAN - 1, table5, 0)

    for copy in fb:
        copy.wait_recv()
    fc = remote(
        g5f.at[pl.ds(1, SPAN - 2), :, mine, :], g5f.at[pl.ds(1, SPAN - 2), :, mine, :],
        s_fc.at[0], r_fc.at[0], partner,
    )
    started.append(fc)

    bottom_middle, bottom_pairs = coefficients(BOTTOM, BOTTOM_LOW)
    for m, (c1, c2) in enumerate(bottom_pairs):
        ends[m, 0] = F32(c1)
        ends[m, 1] = F32(c2)
    fc.wait_recv()
    for k in range(1, SPAN - 1):
        for i in range(4):
            fd = g5f[k, i] * inv5[k, i]
            fd5[k, i] = fd
            x5b[k, i] = fd * (1.0 / bottom_middle)

    def sweep5(now, old, reach, c1, c2):
        lo, hi = MID - reach, MID + reach + 1
        half = {}

        def turned(k, i):
            if (k, i) not in half:
                half[k, i] = pltpu.roll(now[k, i], 64, 1)
            return half[k, i]

        for k in range(lo, hi):
            x = [now[k, i] for i in range(4)]
            for i in range(4):
                east = x[i + 1] if i < 3 else next_group(x[0])
                west = x[i - 1] if i > 0 else last_group(x[3])
                north = jnp.where(low, turned(k, i), turned(k + 1, i))
                south = jnp.where(low, turned(k - 1, i), turned(k, i))
                total = fd5[k, i] - x[i]
                total = total + t5[0, k, i] * east + t5[1, k, i] * west
                total = total + t5[2, k, i] * north + t5[3, k, i] * south
                total = total + t5[4, k, i] * pltpu.roll(x[i], 127, 1) + t5[5, k, i] * pltpu.roll(x[i], 1, 1)
                old[k, i] = x[i] + c1 * (x[i] - old[k, i]) + c2 * total

    def two(reach, first):
        def body(k, carry):
            m = first + 2 * k
            sweep5(x5b, x5a, reach, ends[m, 0], ends[m, 1])
            sweep5(x5a, x5b, reach, ends[m + 1, 0], ends[m + 1, 1])
            return carry

        return body

    lax.fori_loop(0, 2, two(9, 0), 0)
    lax.fori_loop(0, 2, two(7, 4), 0)
    lax.fori_loop(0, 2, two(5, 8), 0)
    two(3, 12)(0, 0)
    sweep5(x5b, x5a, 2, ends[14, 0], ends[14, 1])

    for a in range(10):
        row = a - 3
        group = lax.rem(g + (row // 4) + NG, NG)
        at = 4 * lax.rem(group, 2) + group // 2
        for k in range(5):
            line = x5a[MID - 2 + k, row % 4, pl.ds(at, 1), :]
            first, last = max(4 * k - 2, 0), min(4 * k + 2, 16)
            q4[a, first:last, :] = jnp.broadcast_to(line, (last - first, 128))
    grown = dot(q4[...].reshape(160, 128), spread).reshape(10, 16, 256)
    rows4 = lax.broadcasted_iota(jnp.int32, (16, 128), 0)
    first_of_box = lax.rem(lax.shift_right_logical(rows4 + 2, 1), 2) == 0
    for copy in p4_copies:
        copy.wait_recv()
    for a in range(10):
        line = jnp.where(first_of_box, grown[a, :, 0:128], grown[a, :, 128:256])
        for r in (2 * a, 2 * a + 1):
            x4b[r] = jnp.where(m4, p4[1, r] + line, 0.0) * row_in(r, 8, 6)
            if 1 <= r < 19:
                fd4[r] = p4[0, r] * inv4[r]
    sweep(t4, fd4, x4b, x4a, 1, 19, 18, (1.0 / smooth_middle,))
    sweep(t4, fd4, x4a, x4b, 2, 18, 16, smooth_pairs[0])
    sweep(t4, fd4, x4b, x4a, 3, 17, 14, smooth_pairs[1])
    sweep(t4, fd4, x4a, x4b, 4, 16, 12, smooth_pairs[2])

    grown = dot(x4b[4:16, 4:12, :].reshape(96, 128), spread).reshape(12, 8, 256)
    for r in range(12):
        for k in range(2):
            line = grown[r, :, 128 * k : 128 * k + 128]
            u4[k, r, pl.ds(0, 8, stride=2), :] = line
            u4[k, r, pl.ds(1, 8, stride=2), :] = line
    for copy in x3_copies:
        copy.wait_recv()
    for r in range(24):
        row = row_in(r, N0, 4)
        for k in range(2):
            lanes = slice(128 * k, 128 * k + 128)
            x3b[r, :, lanes] = jnp.where(m3c[:, lanes], (h3[r, :, lanes] + u4[k, r // 2]) * row, 0.0)
    sweep(t3, fd3, x3b, x3a, 1, 23, 11, (1.0 / smooth_middle,))
    sweep(t3, fd3, x3a, x3b, 2, 22, 10, smooth_pairs[0])
    sweep(t3, fd3, x3b, x3a, 3, 21, 9, smooth_pairs[1])
    sweep(t3, fd3, x3a, x3b, 4, 20, 8, smooth_pairs[2])
    result = pltpu.make_async_copy(x3b.at[pl.ds(4, N0), pl.ds(4, N1), :], out, own_sem.at[0])
    result.start()
    for copy in started:
        copy.wait_send()
    result.wait()


SCRATCH = (
    [pltpu.VMEM(shape, F32) for shape in (
        (24, 16, 256), (24, 16, 256), (26, 24, 256), (6, 24, 16, 256), (24, 16, 256), (24, 16, 256),
        (24, 16, 256), (24, 16, 256), (24, 16, 256),
        (2, 20, 16, 128), (20, 16, 128), (2, 20, 16, 128), (6, 20, 16, 128), (20, 16, 128), (20, 16, 128),
        (20, 16, 128), (20, 16, 128), (20, 16, 128), (8, 16, 128),
        (8, 256), (2, SPAN, 4, 8, 128), (SPAN, 4, 8, 128), (6, SPAN, 4, 8, 128), (SPAN, 4, 8, 128),
        (SPAN, 4, 8, 128), (SPAN, 4, 8, 128), (SPAN, 4, 8, 128), (10, 16, 128), (8, 16, 256),
        (2, 12, 16, 128),
    )]
    + [pltpu.SemaphoreType.DMA((3,)), pltpu.SMEM((16, 2), F32)]
    + [pltpu.SemaphoreType.DMA(shape) for count in (
        (3, 8), (14,), (8,), (8,), (14,), (3,), (2 * MID,), (1,), (3,), (2 * REACH,), (1,)
    ) for shape in (count, count)]
)


def cycle(source, alpha, beta):
    return pl.pallas_call(
        kernel,
        out_shape=jax.ShapeDtypeStruct((N0, N1, N2), F32),
        in_specs=[pl.BlockSpec(memory_space=pl.ANY)] * 3,
        out_specs=pl.BlockSpec(memory_space=pl.ANY),
        scratch_shapes=SCRATCH,
        compiler_params=pltpu.CompilerParams(
            collective_id=0, has_side_effects=True, vmem_limit_bytes=48 << 20
        ),
        name="vcycle",
    )(source, alpha, beta)


def solution(mesh):
    spec = P("grp", "box", None)
    return jax.shard_map(cycle, mesh=mesh, in_specs=(spec,) * 3, out_specs=spec, check_vma=False)
```

```python
import jax
import jax.numpy as jnp
from jax import lax
from jax.experimental import pallas as pl
from jax.experimental.pallas import tpu as pltpu
from jax.sharding import PartitionSpec as P

SMOOTH = 4
BOTTOM = 16
SMOOTH_LOW = 0.25
BOTTOM_LOW = 0.02
UPPER_BOUND = 2.0

MESH = pl.DeviceIdType.MESH
F32 = jnp.float32
NG, NB = 8, 32
N0, N1, N2 = 16, 8, 256
REACH = 9
MID = REACH + 1
SPAN = 2 * MID + 1

FACES = [(dg, db) for db in (-1, 1, 0) for dg in (0, -1, 1) if (dg, db) != (0, 0)]


def coefficients(degree, lower):
    middle = (UPPER_BOUND + lower) / 2.0
    spread = (UPPER_BOUND - lower) / 2.0
    base = middle / spread
    now = 1.0 / base
    pairs = []
    for _ in range(degree - 1):
        after = 1.0 / (2.0 * base - now)
        pairs.append((after * now, 2.0 * after / spread))
        now = after
    return middle, pairs


def part(step, size, width, origin):
    if step == 0:
        return 0, origin, size
    if step == 2:
        return size - (width - size), origin - width, width - size
    if step == -2:
        return 0, origin + 2 * size, width - size
    width = min(width, size)
    if step == 1:
        return size - width, origin - width, width
    return 0, origin + size, width


def kernel(
    source, alpha, beta, out,
    f3, a3, b3, t3, d3, fd3, x3a, x3b, h3,
    ab4, f4, p4, t4, inv4, d4, fd4, x4a, x4b, w4,
    z5, g5ab, g5f, t5, inv5, fd5, x5a, x5b, q4, w3, u4,
    own_sem, ends,
    s_p1, r_p1, s_ab4, r_ab4, s_f4, r_f4, s_x3, r_x3, s_p4, r_p4,
    s_aba, r_aba, s_abb, r_abb, s_abc, r_abc, s_fa, r_fa, s_fb, r_fb, s_fc, r_fc,
):
    g, b = lax.axis_index("grp"), lax.axis_index("box")
    core, chip = lax.rem(g, 2), g // 2
    sub = 4 * core + chip

    def device(dg, db):
        return (lax.rem(g + dg + NG, NG), lax.rem(b + db + NB, NB))

    def remote(src, dst, send, recv, target):
        copy = pltpu.make_async_remote_copy(
            src_ref=src, dst_ref=dst, send_sem=send, recv_sem=recv, device_id=target, device_id_type=MESH
        )
        copy.start()
        return copy

    started = []

    own = [
        pltpu.make_async_copy(beta, b3.at[pl.ds(5, N0), pl.ds(8, N1), :], own_sem.at[0]),
        pltpu.make_async_copy(alpha, a3.at[pl.ds(4, N0), pl.ds(4, N1), :], own_sem.at[1]),
        pltpu.make_async_copy(source, f3.at[pl.ds(4, N0), pl.ds(4, N1), :], own_sem.at[2]),
    ]
    for copy in own:
        copy.start()

    f4[...] = jnp.zeros_like(f4)

    partners = set(FACES) | {(2, 0), (4, 0), (6, 0)}
    partners |= {(0, k) for k in range(-MID, MID + 1) if k}
    partners = sorted(partners, key=lambda p: -abs(p[1]))
    barrier = pltpu.get_barrier_semaphore()
    for dg, db in partners:
        pl.semaphore_signal(barrier, inc=1, device_id=device(dg, db), device_id_type=MESH)

    pl.semaphore_wait(barrier, len(partners))

    def halo(src, dst, dg, db, w0, w1, o0, o1, size, send, recv):
        s0, t0, l0 = part(dg, size[0], w0, o0)
        s1, t1, l1 = part(db, size[1], w1, o1)
        return remote(
            src(s0, l0, s1, l1), dst(t0, l0, t1, l1), send, recv, device(dg, db)
        )

    def window(ref):
        return lambda i, n, j, m: ref.at[pl.ds(i, n), pl.ds(j, m), :]

    def window2(ref):
        return lambda i, n, j, m: ref.at[:, pl.ds(i, n), pl.ds(j, m), :]

    def inner(ref, o0, o1):
        return lambda i, n, j, m: ref.at[pl.ds(o0 + i, n), pl.ds(o1 + j, m), :]

    def inner2(ref, o0, o1):
        return lambda i, n, j, m: ref.at[:, pl.ds(o0 + i, n), pl.ds(o1 + j, m), :]

    p1 = []
    for n, (src, dst, w, o0, o1) in enumerate(
        ((beta, b3, 5, 5, 8), (alpha, a3, 4, 4, 4), (source, f3, 4, 4, 4))
    ):
        for k, (dg, db) in enumerate(FACES):
            p1.append(
                halo(window(src), window(dst), dg, db, w, w, o0, o1, (N0, N1), s_p1.at[n, k], r_p1.at[n, k])
            )
    started += p1

    rows256 = lax.broadcasted_iota(jnp.int32, (256, 128), 0)
    cols128 = lax.broadcasted_iota(jnp.int32, (256, 128), 1)
    gather = jnp.where(lax.shift_right_logical(rows256, 1) == cols128, 1.0, 0.0).astype(F32)
    rows128 = lax.broadcasted_iota(jnp.int32, (128, 256), 0)
    cols256 = lax.broadcasted_iota(jnp.int32, (128, 256), 1)
    spread = jnp.where(lax.shift_right_logical(cols256, 1) == rows128, 1.0, 0.0).astype(F32)

    def dot(x, matrix):
        return jnp.dot(x, matrix, precision=lax.Precision.HIGHEST, preferred_element_type=F32)

    def halve(pairs, o1):
        n = pairs.shape[1]
        w4[:, 0:n, :] = dot(pairs.reshape(8 * n, 256), gather).reshape(8, n, 128)
        return 0.125 * (w4[:, pl.ds(o1, 4, stride=2), :] + w4[:, pl.ds(o1 + 1, 4, stride=2), :])

    def pack(get, row):
        for i in range(4):
            t = get(2 * i) + get(2 * i + 1)
            z5[pl.ds(row + i, 1), 0:128] = t[0:1] + t[1:2]
            z5[pl.ds(row + i, 1), 128:256] = t[2:3] + t[3:4]

    for copy in own[:2]:
        copy.wait()
    ab4[0, 6:14, 6:10, :] = halve(
        jnp.stack([a3[4 + 2 * i, 4:12, :] + a3[5 + 2 * i, 4:12, :] for i in range(8)]), 0
    )
    ab4[1, 6:14, 6:10, :] = halve(
        jnp.stack([b3[5 + 2 * i, 8:16, :] + b3[6 + 2 * i, 8:16, :] for i in range(8)]), 0
    )
    for n in range(2):
        pack(lambda r, n=n: ab4[n, 6 + r, 6:10, :], 4 * n)
    packed = 0.125 * dot(z5[...], gather)
    for n in range(2):
        for i in range(4):
            g5ab[n, MID, i, pl.ds(sub, 1), :] = packed[4 * n + i : 4 * n + i + 1]
    abb = []
    for k, db in enumerate([s * d for d in range(MID, 0, -1) for s in (-1, 1)]):
        abb.append(
            remote(
                g5ab.at[:, MID, :, pl.ds(sub, 1), :],
                g5ab.at[:, MID - db, :, pl.ds(sub, 1), :],
                s_abb.at[k], r_abb.at[k], device(0, db),
            )
        )
    started += abb

    def boxes4(ref, send, recv):
        copies = []
        for k, db in enumerate((-2, 2, -1, 1)):
            copies.append(
                halo(inner2(ref, 6, 6), window2(ref), 0, db, 6, 6, 6, 6, (8, 4), send.at[k], recv.at[k])
            )
        return copies

    def groups4(ref, send, recv):
        copies = []
        for k, dg in enumerate((-1, 1)):
            s0, t0, l0 = part(dg, 8, 6, 6)
            copies.append(
                remote(
                    ref.at[:, pl.ds(6 + s0, l0)], ref.at[:, pl.ds(t0, l0)],
                    send.at[4 + k], recv.at[4 + k], device(dg, 0),
                )
            )
        return copies

    ab4_boxes = boxes4(ab4, s_ab4, r_ab4)
    started += ab4_boxes

    x4a[...] = jnp.zeros_like(x4a)
    x5a[...] = jnp.zeros_like(x5a)
    x5b[...] = jnp.zeros_like(x5b)

    own[2].wait()
    for copy in p1:
        copy.wait_recv()

    def inside(start, shape, axis, count):
        at = lax.broadcasted_iota(jnp.int32, shape, axis) + start
        return (at >= 0) & (at < count)

    lanes3 = lax.broadcasted_iota(jnp.int32, (16, 256), 1)
    m3c = inside(N1 * b - 4, (16, 256), 0, N1 * NB)
    m3n = inside(N1 * b - 3, (16, 256), 0, N1 * NB)
    m3s = inside(N1 * b - 5, (16, 256), 0, N1 * NB)

    def row_in(r, size, origin):
        at = size * g + r - origin
        return jnp.where((at >= 0) & (at < size * NG), 1.0, 0.0).astype(F32)

    def table3(r, carry):
        here = row_in(r, N0, 4)
        bc = jnp.where(m3c, b3[r + 1, pl.ds(4, 16), :], 0.0) * here
        be = jnp.where(m3c, b3[r + 2, pl.ds(4, 16), :], 0.0) * row_in(r + 1, N0, 4)
        bw = jnp.where(m3c, b3[r, pl.ds(4, 16), :], 0.0) * row_in(r - 1, N0, 4)
        bn = jnp.where(m3n, b3[r + 1, pl.ds(5, 16), :], 0.0) * here
        bs = jnp.where(m3s, b3[r + 1, pl.ds(3, 16), :], 0.0) * here
        bu = jnp.where(lanes3 == 255, 0.0, pltpu.roll(bc, 255, 1))
        bd = jnp.where(lanes3 == 0, 0.0, pltpu.roll(bc, 1, 1))
        c = [0.5 * (bc + v) for v in (be, bw, bn, bs, bu, bd)]
        diag = a3[r] + c[0] + c[1] + c[2] + c[3] + c[4] + c[5]
        inv = jnp.where(m3c, 1.0 / diag, 0.0) * here
        for n in range(4):
            t3[n, r] = c[n] * inv
        t3[4, r] = jnp.where(lanes3 == 255, 0.0, c[4] * inv)
        t3[5, r] = jnp.where(lanes3 == 0, 0.0, c[5] * inv)
        d3[r] = diag
        fd = f3[r] * inv
        fd3[r] = fd
        x3b[r] = fd * (1.0 / smooth_middle)
        x3a[r] = jnp.zeros_like(fd)
        return carry

    smooth_middle, smooth_pairs = coefficients(SMOOTH, SMOOTH_LOW)
    lax.fori_loop(0, 24, table3, 0, unroll=4)

    def scaled_residual(t, fd, x, r):
        here = x[r]
        n, m = here.shape
        total = fd[r] - here
        total = total + t[0, r] * x[r + 1] + t[1, r] * x[r - 1]
        total = total + t[2, r] * pltpu.roll(here, n - 1, 0) + t[3, r] * pltpu.roll(here, 1, 0)
        return total + t[4, r] * pltpu.roll(here, m - 1, 1) + t[5, r] * pltpu.roll(here, 1, 1)

    def sweep(t, fd, now, old, lo, hi, chunk, pair):
        def rows(k, carry):
            for i in range(chunk):
                r = lo + k * chunk + i
                total = scaled_residual(t, fd, now, r)
                here = now[r]
                if len(pair) == 1:
                    old[r] = here + pair[0] * total
                else:
                    old[r] = here + pair[0] * (here - old[r]) + pair[1] * total
            return carry

        lax.fori_loop(0, (hi - lo) // chunk, rows, 0)

    sweep(t3, fd3, x3b, x3a, 1, 23, 11, smooth_pairs[0])
    sweep(t3, fd3, x3a, x3b, 2, 22, 10, smooth_pairs[1])
    sweep(t3, fd3, x3b, x3a, 3, 21, 9, smooth_pairs[2])

    def fine_residual(i):
        return d3[i] * scaled_residual(t3, fd3, x3a, i)

    for i in range(8):
        w3[i] = fine_residual(4 + 2 * i) + fine_residual(5 + 2 * i)
    f4[6:14, 6:10, :] = halve(w3[...], 4)
    f4_copies = []
    for k, (dg, db) in enumerate(FACES):
        f4_copies.append(
            halo(inner(f4, 6, 6), window(f4), dg, db, 4, 4, 6, 6, (8, 4), s_f4.at[k], r_f4.at[k])
        )
    started += f4_copies
    for i in range(16):
        h3[4 + i, 4:12, :] = x3a[4 + i, 4:12, :]
    x3_copies = []
    for copy in ab4_boxes:
        copy.wait_recv()
    ab4_groups = groups4(ab4, s_ab4, r_ab4)
    started += ab4_groups
    for k, db in enumerate((-1, 1)):
        x3_copies.append(
            halo(inner(h3, 4, 4), window(h3), 0, db, 4, 4, 4, 4, (N0, N1), s_x3.at[k], r_x3.at[k])
        )
    started += x3_copies

    for copy in abb:
        copy.wait_recv()
    aba = []
    for k, dg in enumerate((2, 4, 6)):
        aba.append(
            remote(
                g5ab.at[:, :, :, pl.ds(sub, 1), :], g5ab.at[:, :, :, pl.ds(sub, 1), :],
                s_aba.at[k], r_aba.at[k], device(dg, 0),
            )
        )
    started += aba

    for copy in ab4_groups:
        copy.wait_recv()
    lanes4 = lax.broadcasted_iota(jnp.int32, (16, 128), 1)
    m4 = inside(4 * b - 6, (16, 128), 0, 4 * NB)

    def masked4(r):
        return jnp.where(m4, ab4[1, r], 0.0) * row_in(r, 8, 6)

    def table4(r, carry):
        bc = masked4(r)
        be, bw = masked4(r + 1), masked4(r - 1)
        bn, bs = pltpu.roll(bc, 15, 0), pltpu.roll(bc, 1, 0)
        bu = jnp.where(lanes4 == 127, 0.0, pltpu.roll(bc, 127, 1))
        bd = jnp.where(lanes4 == 0, 0.0, pltpu.roll(bc, 1, 1))
        c = [0.125 * (bc + v) for v in (be, bw, bn, bs, bu, bd)]
        diag = ab4[0, r] + c[0] + c[1] + c[2] + c[3] + c[4] + c[5]
        inv = jnp.where(m4, 1.0 / diag, 0.0) * row_in(r, 8, 6)
        for n in range(4):
            t4[n, r] = c[n] * inv
        t4[4, r] = jnp.where(lanes4 == 127, 0.0, c[4] * inv)
        t4[5, r] = jnp.where(lanes4 == 0, 0.0, c[5] * inv)
        d4[r] = diag
        inv4[r] = inv
        return carry

    lax.fori_loop(1, 19, table4, 0, unroll=6)

    mine = pl.ds(pl.multiple_of(4 * core, 4), 4)
    partner = (g + 1 - 2 * core, b)

    for copy in f4_copies:
        copy.wait_recv()
    for r in range(2, 18):
        fd = f4[r] * inv4[r]
        fd4[r] = fd
        x4b[r] = fd * (1.0 / smooth_middle)
    sweep(t4, fd4, x4b, x4a, 3, 17, 14, smooth_pairs[0])
    sweep(t4, fd4, x4a, x4b, 4, 16, 12, smooth_pairs[1])
    sweep(t4, fd4, x4b, x4a, 5, 15, 10, smooth_pairs[2])

    for r in range(8):
        w4[r] = d4[6 + r] * scaled_residual(t4, fd4, x4a, 6 + r)
    pack(lambda r: w4[r, 6:10, :], 0)
    packed = 0.125 * dot(z5[...], gather)
    for i in range(4):
        g5f[MID, i, pl.ds(sub, 1), :] = packed[i : i + 1]
    fa = []
    for k, dg in enumerate((2, 4, 6)):
        fa.append(
            remote(
                g5f.at[MID, :, pl.ds(sub, 1), :], g5f.at[MID, :, pl.ds(sub, 1), :],
                s_fa.at[k], r_fa.at[k], device(dg, 0),
            )
        )
    started += fa

    for copy in aba:
        copy.wait_recv()
    abc = remote(
        g5ab.at[:, :, :, mine, :], g5ab.at[:, :, :, mine, :], s_abc.at[0], r_abc.at[0], partner
    )
    started.append(abc)

    for copy in x3_copies:
        copy.wait_recv()
    x3_groups = []
    for k, dg in enumerate((-1, 1)):
        s0, t0, l0 = part(dg, N0, 4, 4)
        x3_groups.append(
            remote(
                h3.at[pl.ds(4 + s0, l0)], h3.at[pl.ds(t0, l0)],
                s_x3.at[2 + k], r_x3.at[2 + k], device(dg, 0),
            )
        )
    started += x3_groups

    p4[0, 6:14, 6:10, :] = f4[6:14, 6:10, :]
    p4[1, 6:14, 6:10, :] = x4a[6:14, 6:10, :]
    for copy in fa:
        copy.wait_recv()
    fb = []
    for k, db in enumerate([s * d for d in range(REACH, 0, -1) for s in (-1, 1)]):
        fb.append(
            remote(
                g5f.at[MID, :, mine, :], g5f.at[MID - db, :, mine, :],
                s_fb.at[k], r_fb.at[k], device(0, db),
            )
        )
    started += fb
    p4_boxes = boxes4(p4, s_p4, r_p4)
    started += p4_boxes

    abc.wait_recv()
    lanes5 = lax.broadcasted_iota(jnp.int32, (8, 128), 1)
    subs5 = lax.broadcasted_iota(jnp.int32, (8, 128), 0)
    low = lanes5 < 64
    front = subs5 < 4
    up_end = (lanes5 == 63) | (lanes5 == 127)
    down_end = (lanes5 == 0) | (lanes5 == 64)

    def next_group(v):
        return jnp.where(front, pltpu.roll(v, 4, 0), pltpu.roll(v, 3, 0))

    def last_group(v):
        return jnp.where(front, pltpu.roll(v, 5, 0), pltpu.roll(v, 4, 0))

    def box_in(k):
        at = b + k - MID
        return jnp.where((at >= 0) & (at < NB), 1.0, 0.0).astype(F32)

    def beta5(k, i):
        return g5ab[1, k, i] * box_in(k)

    def table5(k, carry):
        bc = [beta5(k, i) for i in range(4)]
        half = [pltpu.roll(v, 64, 1) for v in bc]
        after = [pltpu.roll(beta5(k + 1, i), 64, 1) for i in range(4)]
        before = [pltpu.roll(beta5(k - 1, i), 64, 1) for i in range(4)]
        for i in range(4):
            be = bc[i + 1] if i < 3 else jnp.where(subs5 == 7, 0.0, next_group(bc[0]))
            bw = bc[i - 1] if i > 0 else jnp.where(subs5 == 0, 0.0, last_group(bc[3]))
            bn = jnp.where(low, half[i], after[i])
            bs = jnp.where(low, before[i], half[i])
            bu = jnp.where(up_end, 0.0, pltpu.roll(bc[i], 127, 1))
            bd = jnp.where(down_end, 0.0, pltpu.roll(bc[i], 1, 1))
            c = [0.03125 * (bc[i] + v) for v in (be, bw, bn, bs, bu, bd)]
            diag = g5ab[0, k, i] + c[0] + c[1] + c[2] + c[3] + c[4] + c[5]
            inv = box_in(k) / diag
            t5[0, k, i] = c[0] * inv if i < 3 else jnp.where(subs5 == 7, 0.0, c[0] * inv)
            t5[1, k, i] = c[1] * inv if i > 0 else jnp.where(subs5 == 0, 0.0, c[1] * inv)
            t5[2, k, i] = c[2] * inv
            t5[3, k, i] = c[3] * inv
            t5[4, k, i] = jnp.where(up_end, 0.0, c[4] * inv)
            t5[5, k, i] = jnp.where(down_end, 0.0, c[5] * inv)
            inv5[k, i] = inv
        return carry

    lax.fori_loop(1, SPAN - 1, table5, 0)

    for copy in fb:
        copy.wait_recv()
    fc = remote(
        g5f.at[pl.ds(1, SPAN - 2), :, mine, :], g5f.at[pl.ds(1, SPAN - 2), :, mine, :],
        s_fc.at[0], r_fc.at[0], partner,
    )
    started.append(fc)
    for copy in p4_boxes:
        copy.wait_recv()
    p4_groups = groups4(p4, s_p4, r_p4)
    started += p4_groups

    bottom_middle, bottom_pairs = coefficients(BOTTOM, BOTTOM_LOW)
    for m, (c1, c2) in enumerate(bottom_pairs):
        ends[m, 0] = F32(c1)
        ends[m, 1] = F32(c2)
    fc.wait_recv()
    for k in range(1, SPAN - 1):
        for i in range(4):
            fd = g5f[k, i] * inv5[k, i]
            fd5[k, i] = fd
            x5b[k, i] = fd * (1.0 / bottom_middle)

    def sweep5(now, old, reach, c1, c2):
        lo, hi = MID - reach, MID + reach + 1
        half = {}

        def turned(k, i):
            if (k, i) not in half:
                half[k, i] = pltpu.roll(now[k, i], 64, 1)
            return half[k, i]

        for k in range(lo, hi):
            x = [now[k, i] for i in range(4)]
            for i in range(4):
                east = x[i + 1] if i < 3 else next_group(x[0])
                west = x[i - 1] if i > 0 else last_group(x[3])
                north = jnp.where(low, turned(k, i), turned(k + 1, i))
                south = jnp.where(low, turned(k - 1, i), turned(k, i))
                total = fd5[k, i] - x[i]
                total = total + t5[0, k, i] * east + t5[1, k, i] * west
                total = total + t5[2, k, i] * north + t5[3, k, i] * south
                total = total + t5[4, k, i] * pltpu.roll(x[i], 127, 1) + t5[5, k, i] * pltpu.roll(x[i], 1, 1)
                old[k, i] = x[i] + c1 * (x[i] - old[k, i]) + c2 * total

    def two(reach, first):
        def body(k, carry):
            m = first + 2 * k
            sweep5(x5b, x5a, reach, ends[m, 0], ends[m, 1])
            sweep5(x5a, x5b, reach, ends[m + 1, 0], ends[m + 1, 1])
            return carry

        return body

    lax.fori_loop(0, 2, two(9, 0), 0)
    lax.fori_loop(0, 2, two(7, 4), 0)
    lax.fori_loop(0, 2, two(5, 8), 0)
    two(3, 12)(0, 0)
    sweep5(x5b, x5a, 2, ends[14, 0], ends[14, 1])

    for a in range(10):
        row = a - 3
        group = lax.rem(g + (row // 4) + NG, NG)
        at = 4 * lax.rem(group, 2) + group // 2
        for k in range(5):
            line = x5a[MID - 2 + k, row % 4, pl.ds(at, 1), :]
            first, last = max(4 * k - 2, 0), min(4 * k + 2, 16)
            q4[a, first:last, :] = jnp.broadcast_to(line, (last - first, 128))
    grown = dot(q4[...].reshape(160, 128), spread).reshape(10, 16, 256)
    rows4 = lax.broadcasted_iota(jnp.int32, (16, 128), 0)
    first_of_box = lax.rem(lax.shift_right_logical(rows4 + 2, 1), 2) == 0
    for copy in p4_groups:
        copy.wait_recv()
    for a in range(10):
        line = jnp.where(first_of_box, grown[a, :, 0:128], grown[a, :, 128:256])
        for r in (2 * a, 2 * a + 1):
            x4b[r] = jnp.where(m4, p4[1, r] + line, 0.0) * row_in(r, 8, 6)
            if 1 <= r < 19:
                fd4[r] = p4[0, r] * inv4[r]
    sweep(t4, fd4, x4b, x4a, 1, 19, 18, (1.0 / smooth_middle,))
    sweep(t4, fd4, x4a, x4b, 2, 18, 16, smooth_pairs[0])
    sweep(t4, fd4, x4b, x4a, 3, 17, 14, smooth_pairs[1])
    sweep(t4, fd4, x4a, x4b, 4, 16, 12, smooth_pairs[2])

    grown = dot(x4b[4:16, 4:12, :].reshape(96, 128), spread).reshape(12, 8, 256)
    for r in range(12):
        for k in range(2):
            line = grown[r, :, 128 * k : 128 * k + 128]
            u4[k, r, pl.ds(0, 8, stride=2), :] = line
            u4[k, r, pl.ds(1, 8, stride=2), :] = line
    for copy in x3_groups:
        copy.wait_recv()
    for r in range(24):
        row = row_in(r, N0, 4)
        for k in range(2):
            lanes = slice(128 * k, 128 * k + 128)
            x3b[r, :, lanes] = jnp.where(m3c[:, lanes], (h3[r, :, lanes] + u4[k, r // 2]) * row, 0.0)
    sweep(t3, fd3, x3b, x3a, 1, 23, 11, (1.0 / smooth_middle,))
    sweep(t3, fd3, x3a, x3b, 2, 22, 10, smooth_pairs[0])
    sweep(t3, fd3, x3b, x3a, 3, 21, 9, smooth_pairs[1])
    sweep(t3, fd3, x3a, x3b, 4, 20, 8, smooth_pairs[2])
    result = pltpu.make_async_copy(x3b.at[pl.ds(4, N0), pl.ds(4, N1), :], out, own_sem.at[0])
    result.start()
    for copy in started:
        copy.wait_send()
    result.wait()


SCRATCH = (
    [pltpu.VMEM(shape, F32) for shape in (
        (24, 16, 256), (24, 16, 256), (26, 24, 256), (6, 24, 16, 256), (24, 16, 256), (24, 16, 256),
        (24, 16, 256), (24, 16, 256), (24, 16, 256),
        (2, 20, 16, 128), (20, 16, 128), (2, 20, 16, 128), (6, 20, 16, 128), (20, 16, 128), (20, 16, 128),
        (20, 16, 128), (20, 16, 128), (20, 16, 128), (8, 16, 128),
        (8, 256), (2, SPAN, 4, 8, 128), (SPAN, 4, 8, 128), (6, SPAN, 4, 8, 128), (SPAN, 4, 8, 128),
        (SPAN, 4, 8, 128), (SPAN, 4, 8, 128), (SPAN, 4, 8, 128), (10, 16, 128), (8, 16, 256),
        (2, 12, 16, 128),
    )]
    + [pltpu.SemaphoreType.DMA((3,)), pltpu.SMEM((16, 2), F32)]
    + [pltpu.SemaphoreType.DMA(shape) for count in (
        (3, 8), (6,), (8,), (4,), (6,), (3,), (2 * MID,), (1,), (3,), (2 * REACH,), (1,)
    ) for shape in (count, count)]
)


def cycle(source, alpha, beta):
    return pl.pallas_call(
        kernel,
        out_shape=jax.ShapeDtypeStruct((N0, N1, N2), F32),
        in_specs=[pl.BlockSpec(memory_space=pl.ANY)] * 3,
        out_specs=pl.BlockSpec(memory_space=pl.ANY),
        scratch_shapes=SCRATCH,
        compiler_params=pltpu.CompilerParams(
            collective_id=0, has_side_effects=True, vmem_limit_bytes=63 << 20
        ),
        name="vcycle",
    )(source, alpha, beta)


def solution(mesh):
    spec = P("grp", "box", None)
    return jax.shard_map(cycle, mesh=mesh, in_specs=(spec,) * 3, out_specs=spec, check_vma=False)
```

```python
import jax
import jax.numpy as jnp
from jax import lax
from jax.experimental import pallas as pl
from jax.experimental.pallas import tpu as pltpu
from jax.sharding import PartitionSpec as P

SMOOTH = 4
BOTTOM = 16
SMOOTH_LOW = 0.25
BOTTOM_LOW = 0.02
UPPER_BOUND = 2.0

MESH = pl.DeviceIdType.MESH
F32 = jnp.float32
NG, NB = 8, 32
N0, N1, N2 = 16, 8, 256
REACH = 9
MID = REACH + 1
SPAN = 2 * MID + 1

FACES = [(dg, db) for db in (-1, 1, 0) for dg in (0, -1, 1) if (dg, db) != (0, 0)]


def coefficients(degree, lower):
    middle = (UPPER_BOUND + lower) / 2.0
    spread = (UPPER_BOUND - lower) / 2.0
    base = middle / spread
    now = 1.0 / base
    pairs = []
    for _ in range(degree - 1):
        after = 1.0 / (2.0 * base - now)
        pairs.append((after * now, 2.0 * after / spread))
        now = after
    return middle, pairs


def part(step, size, width, origin):
    if step == 0:
        return 0, origin, size
    if step == 2:
        return size - (width - size), origin - width, width - size
    if step == -2:
        return 0, origin + 2 * size, width - size
    width = min(width, size)
    if step == 1:
        return size - width, origin - width, width
    return 0, origin + size, width


def kernel(
    source, alpha, beta, out,
    f3, a3, b3, t3, d3, fd3, x3a, x3b, h3,
    ab4, f4, p4, t4, inv4, d4, fd4, x4a, x4b, w4,
    z5, g5ab, g5f, t5, inv5, fd5, x5a, x5b, q4, w3, u4,
    own_sem, hello, ends,
    s_p1, r_p1, s_ab4, r_ab4, s_f4, r_f4, s_x3, r_x3, s_p4, r_p4,
    s_aba, r_aba, s_abb, r_abb, s_abc, r_abc, s_fa, r_fa, s_fb, r_fb, s_fc, r_fc,
):
    g, b = lax.axis_index("grp"), lax.axis_index("box")
    core, chip = lax.rem(g, 2), g // 2
    sub = 4 * core + chip

    def device(dg, db):
        return (lax.rem(g + dg + NG, NG), lax.rem(b + db + NB, NB))

    def remote(src, dst, send, recv, target):
        copy = pltpu.make_async_remote_copy(
            src_ref=src, dst_ref=dst, send_sem=send, recv_sem=recv, device_id=target, device_id_type=MESH
        )
        copy.start()
        return copy

    started = []

    own = [
        pltpu.make_async_copy(beta, b3.at[pl.ds(5, N0), pl.ds(8, N1), :], own_sem.at[0]),
        pltpu.make_async_copy(alpha, a3.at[pl.ds(4, N0), pl.ds(4, N1), :], own_sem.at[1]),
        pltpu.make_async_copy(source, f3.at[pl.ds(4, N0), pl.ds(4, N1), :], own_sem.at[2]),
    ]
    for copy in own:
        copy.start()

    f4[...] = jnp.zeros_like(f4)

    partners = FACES + [(0, -8), (0, 8)]
    barrier = pltpu.get_barrier_semaphore()
    for dg, db in partners:
        pl.semaphore_signal(barrier, inc=1, device_id=device(dg, db), device_id_type=MESH)

    pl.semaphore_wait(barrier, len(partners))

    def halo(src, dst, dg, db, w0, w1, o0, o1, size, send, recv):
        s0, t0, l0 = part(dg, size[0], w0, o0)
        s1, t1, l1 = part(db, size[1], w1, o1)
        return remote(
            src(s0, l0, s1, l1), dst(t0, l0, t1, l1), send, recv, device(dg, db)
        )

    def window(ref):
        return lambda i, n, j, m: ref.at[pl.ds(i, n), pl.ds(j, m), :]

    def window2(ref):
        return lambda i, n, j, m: ref.at[:, pl.ds(i, n), pl.ds(j, m), :]

    def inner(ref, o0, o1):
        return lambda i, n, j, m: ref.at[pl.ds(o0 + i, n), pl.ds(o1 + j, m), :]

    def inner2(ref, o0, o1):
        return lambda i, n, j, m: ref.at[:, pl.ds(o0 + i, n), pl.ds(o1 + j, m), :]

    p1 = []
    for n, (src, dst, w, o0, o1) in enumerate(
        ((beta, b3, 5, 5, 8), (alpha, a3, 4, 4, 4), (source, f3, 4, 4, 4))
    ):
        for k, (dg, db) in enumerate(FACES):
            p1.append(
                halo(window(src), window(dst), dg, db, w, w, o0, o1, (N0, N1), s_p1.at[n, k], r_p1.at[n, k])
            )
    started += p1

    def greet(n, peers):
        for dg, db in peers:
            pl.semaphore_signal(hello.at[n], inc=1, device_id=device(dg, db), device_id_type=MESH)

    greet(0, ((0, -1), (0, 1), (-1, 0), (1, 0)))

    rows256 = lax.broadcasted_iota(jnp.int32, (256, 128), 0)
    cols128 = lax.broadcasted_iota(jnp.int32, (256, 128), 1)
    gather = jnp.where(lax.shift_right_logical(rows256, 1) == cols128, 1.0, 0.0).astype(F32)
    rows128 = lax.broadcasted_iota(jnp.int32, (128, 256), 0)
    cols256 = lax.broadcasted_iota(jnp.int32, (128, 256), 1)
    spread = jnp.where(lax.shift_right_logical(cols256, 1) == rows128, 1.0, 0.0).astype(F32)

    def dot(x, matrix):
        return jnp.dot(x, matrix, precision=lax.Precision.HIGHEST, preferred_element_type=F32)

    def halve(pairs, o1):
        n = pairs.shape[1]
        w4[:, 0:n, :] = dot(pairs.reshape(8 * n, 256), gather).reshape(8, n, 128)
        return 0.125 * (w4[:, pl.ds(o1, 4, stride=2), :] + w4[:, pl.ds(o1 + 1, 4, stride=2), :])

    def pack(get, row):
        for i in range(4):
            t = get(2 * i) + get(2 * i + 1)
            z5[pl.ds(row + i, 1), 0:128] = t[0:1] + t[1:2]
            z5[pl.ds(row + i, 1), 128:256] = t[2:3] + t[3:4]

    for copy in own[:2]:
        copy.wait()
    ab4[0, 6:14, 6:10, :] = halve(
        jnp.stack([a3[4 + 2 * i, 4:12, :] + a3[5 + 2 * i, 4:12, :] for i in range(8)]), 0
    )
    ab4[1, 6:14, 6:10, :] = halve(
        jnp.stack([b3[5 + 2 * i, 8:16, :] + b3[6 + 2 * i, 8:16, :] for i in range(8)]), 0
    )
    pl.semaphore_wait(hello.at[0], 4)
    greet(1, ((0, -2), (0, 2), (-2, 0), (2, 0)))
    for n in range(2):
        pack(lambda r, n=n: ab4[n, 6 + r, 6:10, :], 4 * n)
    packed = 0.125 * dot(z5[...], gather)
    for n in range(2):
        for i in range(4):
            g5ab[n, MID, i, pl.ds(sub, 1), :] = packed[4 * n + i : 4 * n + i + 1]
    pl.semaphore_wait(hello.at[1], 4)
    abb = []
    for k, db in enumerate([s * d for d in range(MID, 0, -1) for s in (-1, 1)]):
        abb.append(
            remote(
                g5ab.at[:, MID, :, pl.ds(sub, 1), :],
                g5ab.at[:, MID - db, :, pl.ds(sub, 1), :],
                s_abb.at[k], r_abb.at[k], device(0, db),
            )
        )
    started += abb

    def boxes4(ref, send, recv):
        copies = []
        for k, db in enumerate((-2, 2, -1, 1)):
            copies.append(
                halo(inner2(ref, 6, 6), window2(ref), 0, db, 6, 6, 6, 6, (8, 4), send.at[k], recv.at[k])
            )
        return copies

    def groups4(ref, send, recv):
        copies = []
        for k, dg in enumerate((-1, 1)):
            s0, t0, l0 = part(dg, 8, 6, 6)
            copies.append(
                remote(
                    ref.at[:, pl.ds(6 + s0, l0)], ref.at[:, pl.ds(t0, l0)],
                    send.at[4 + k], recv.at[4 + k], device(dg, 0),
                )
            )
        return copies

    ab4_boxes = boxes4(ab4, s_ab4, r_ab4)
    started += ab4_boxes

    x4a[...] = jnp.zeros_like(x4a)
    x5a[...] = jnp.zeros_like(x5a)
    x5b[...] = jnp.zeros_like(x5b)

    for copy in p1[:16]:
        copy.wait_recv()

    def inside(start, shape, axis, count):
        at = lax.broadcasted_iota(jnp.int32, shape, axis) + start
        return (at >= 0) & (at < count)

    lanes3 = lax.broadcasted_iota(jnp.int32, (16, 256), 1)
    m3c = inside(N1 * b - 4, (16, 256), 0, N1 * NB)
    m3n = inside(N1 * b - 3, (16, 256), 0, N1 * NB)
    m3s = inside(N1 * b - 5, (16, 256), 0, N1 * NB)

    def row_in(r, size, origin):
        at = size * g + r - origin
        return jnp.where((at >= 0) & (at < size * NG), 1.0, 0.0).astype(F32)

    def table3(r, carry):
        here = row_in(r, N0, 4)
        bc = jnp.where(m3c, b3[r + 1, pl.ds(4, 16), :], 0.0) * here
        be = jnp.where(m3c, b3[r + 2, pl.ds(4, 16), :], 0.0) * row_in(r + 1, N0, 4)
        bw = jnp.where(m3c, b3[r, pl.ds(4, 16), :], 0.0) * row_in(r - 1, N0, 4)
        bn = jnp.where(m3n, b3[r + 1, pl.ds(5, 16), :], 0.0) * here
        bs = jnp.where(m3s, b3[r + 1, pl.ds(3, 16), :], 0.0) * here
        bu = jnp.where(lanes3 == 255, 0.0, pltpu.roll(bc, 255, 1))
        bd = jnp.where(lanes3 == 0, 0.0, pltpu.roll(bc, 1, 1))
        c = [0.5 * (bc + v) for v in (be, bw, bn, bs, bu, bd)]
        diag = a3[r] + c[0] + c[1] + c[2] + c[3] + c[4] + c[5]
        inv = jnp.where(m3c, 1.0 / diag, 0.0) * here
        for n in range(4):
            t3[n, r] = c[n] * inv
        t3[4, r] = jnp.where(lanes3 == 255, 0.0, c[4] * inv)
        t3[5, r] = jnp.where(lanes3 == 0, 0.0, c[5] * inv)
        d3[r] = diag
        fd3[r] = inv
        return carry

    def start3(r, carry):
        fd = f3[r] * fd3[r]
        fd3[r] = fd
        x3b[r] = fd * (1.0 / smooth_middle)
        x3a[r] = jnp.zeros_like(fd)
        return carry

    smooth_middle, smooth_pairs = coefficients(SMOOTH, SMOOTH_LOW)
    lax.fori_loop(0, 24, table3, 0, unroll=4)
    own[2].wait()
    for copy in p1[16:]:
        copy.wait_recv()
    lax.fori_loop(0, 24, start3, 0, unroll=8)

    def scaled_residual(t, fd, x, r):
        here = x[r]
        n, m = here.shape
        total = fd[r] - here
        total = total + t[0, r] * x[r + 1] + t[1, r] * x[r - 1]
        total = total + t[2, r] * pltpu.roll(here, n - 1, 0) + t[3, r] * pltpu.roll(here, 1, 0)
        return total + t[4, r] * pltpu.roll(here, m - 1, 1) + t[5, r] * pltpu.roll(here, 1, 1)

    def sweep(t, fd, now, old, lo, hi, chunk, pair):
        def rows(k, carry):
            for i in range(chunk):
                r = lo + k * chunk + i
                total = scaled_residual(t, fd, now, r)
                here = now[r]
                if len(pair) == 1:
                    old[r] = here + pair[0] * total
                else:
                    old[r] = here + pair[0] * (here - old[r]) + pair[1] * total
            return carry

        lax.fori_loop(0, (hi - lo) // chunk, rows, 0)

    sweep(t3, fd3, x3b, x3a, 1, 23, 11, smooth_pairs[0])
    sweep(t3, fd3, x3a, x3b, 2, 22, 10, smooth_pairs[1])
    sweep(t3, fd3, x3b, x3a, 3, 21, 9, smooth_pairs[2])

    def fine_residual(i):
        return d3[i] * scaled_residual(t3, fd3, x3a, i)

    for i in range(8):
        w3[i] = fine_residual(4 + 2 * i) + fine_residual(5 + 2 * i)
    f4[6:14, 6:10, :] = halve(w3[...], 4)
    f4_copies = []
    for k, (dg, db) in enumerate(FACES):
        f4_copies.append(
            halo(inner(f4, 6, 6), window(f4), dg, db, 4, 4, 6, 6, (8, 4), s_f4.at[k], r_f4.at[k])
        )
    started += f4_copies
    for i in range(16):
        h3[4 + i, 4:12, :] = x3a[4 + i, 4:12, :]
    x3_copies = []
    for copy in ab4_boxes:
        copy.wait_recv()
    ab4_groups = groups4(ab4, s_ab4, r_ab4)
    started += ab4_groups
    for k, db in enumerate((-1, 1)):
        x3_copies.append(
            halo(inner(h3, 4, 4), window(h3), 0, db, 4, 4, 4, 4, (N0, N1), s_x3.at[k], r_x3.at[k])
        )
    started += x3_copies

    for copy in abb:
        copy.wait_recv()
    aba = []
    for k, dg in enumerate((2, 4, 6)):
        aba.append(
            remote(
                g5ab.at[:, :, :, pl.ds(sub, 1), :], g5ab.at[:, :, :, pl.ds(sub, 1), :],
                s_aba.at[k], r_aba.at[k], device(dg, 0),
            )
        )
    started += aba

    for copy in ab4_groups:
        copy.wait_recv()
    lanes4 = lax.broadcasted_iota(jnp.int32, (16, 128), 1)
    m4 = inside(4 * b - 6, (16, 128), 0, 4 * NB)

    def masked4(r):
        return jnp.where(m4, ab4[1, r], 0.0) * row_in(r, 8, 6)

    def table4(r, carry):
        bc = masked4(r)
        be, bw = masked4(r + 1), masked4(r - 1)
        bn, bs = pltpu.roll(bc, 15, 0), pltpu.roll(bc, 1, 0)
        bu = jnp.where(lanes4 == 127, 0.0, pltpu.roll(bc, 127, 1))
        bd = jnp.where(lanes4 == 0, 0.0, pltpu.roll(bc, 1, 1))
        c = [0.125 * (bc + v) for v in (be, bw, bn, bs, bu, bd)]
        diag = ab4[0, r] + c[0] + c[1] + c[2] + c[3] + c[4] + c[5]
        inv = jnp.where(m4, 1.0 / diag, 0.0) * row_in(r, 8, 6)
        for n in range(4):
            t4[n, r] = c[n] * inv
        t4[4, r] = jnp.where(lanes4 == 127, 0.0, c[4] * inv)
        t4[5, r] = jnp.where(lanes4 == 0, 0.0, c[5] * inv)
        d4[r] = diag
        inv4[r] = inv
        return carry

    lax.fori_loop(1, 19, table4, 0, unroll=6)

    mine = pl.ds(pl.multiple_of(4 * core, 4), 4)
    partner = (g + 1 - 2 * core, b)

    for copy in f4_copies:
        copy.wait_recv()
    for r in range(2, 18):
        fd = f4[r] * inv4[r]
        fd4[r] = fd
        x4b[r] = fd * (1.0 / smooth_middle)
    sweep(t4, fd4, x4b, x4a, 3, 17, 14, smooth_pairs[0])
    sweep(t4, fd4, x4a, x4b, 4, 16, 12, smooth_pairs[1])
    sweep(t4, fd4, x4b, x4a, 5, 15, 10, smooth_pairs[2])

    for r in range(8):
        w4[r] = d4[6 + r] * scaled_residual(t4, fd4, x4a, 6 + r)
    pack(lambda r: w4[r, 6:10, :], 0)
    packed = 0.125 * dot(z5[...], gather)
    for i in range(4):
        g5f[MID, i, pl.ds(sub, 1), :] = packed[i : i + 1]
    fa = []
    for k, dg in enumerate((2, 4, 6)):
        fa.append(
            remote(
                g5f.at[MID, :, pl.ds(sub, 1), :], g5f.at[MID, :, pl.ds(sub, 1), :],
                s_fa.at[k], r_fa.at[k], device(dg, 0),
            )
        )
    started += fa

    for copy in aba:
        copy.wait_recv()
    abc = remote(
        g5ab.at[:, :, :, mine, :], g5ab.at[:, :, :, mine, :], s_abc.at[0], r_abc.at[0], partner
    )
    started.append(abc)

    for copy in x3_copies:
        copy.wait_recv()
    x3_groups = []
    for k, dg in enumerate((-1, 1)):
        s0, t0, l0 = part(dg, N0, 4, 4)
        x3_groups.append(
            remote(
                h3.at[pl.ds(4 + s0, l0)], h3.at[pl.ds(t0, l0)],
                s_x3.at[2 + k], r_x3.at[2 + k], device(dg, 0),
            )
        )
    started += x3_groups

    p4[0, 6:14, 6:10, :] = f4[6:14, 6:10, :]
    p4[1, 6:14, 6:10, :] = x4a[6:14, 6:10, :]
    for copy in fa:
        copy.wait_recv()
    fb = []
    fb_from = [s * d for d in range(REACH, 0, -1) for s in (-1, 1)]
    for k, db in enumerate(fb_from):
        fb.append(
            remote(
                g5f.at[MID, :, mine, :], g5f.at[MID - db, :, mine, :],
                s_fb.at[k], r_fb.at[k], device(0, db),
            )
        )
    started += fb
    p4_boxes = boxes4(p4, s_p4, r_p4)
    started += p4_boxes

    abc.wait_recv()
    lanes5 = lax.broadcasted_iota(jnp.int32, (8, 128), 1)
    subs5 = lax.broadcasted_iota(jnp.int32, (8, 128), 0)
    low = lanes5 < 64
    front = subs5 < 4
    up_end = (lanes5 == 63) | (lanes5 == 127)
    down_end = (lanes5 == 0) | (lanes5 == 64)

    def next_group(v):
        return jnp.where(front, pltpu.roll(v, 4, 0), pltpu.roll(v, 3, 0))

    def last_group(v):
        return jnp.where(front, pltpu.roll(v, 5, 0), pltpu.roll(v, 4, 0))

    def box_in(k):
        at = b + k - MID
        return jnp.where((at >= 0) & (at < NB), 1.0, 0.0).astype(F32)

    def beta5(k, i):
        return g5ab[1, k, i] * box_in(k)

    def table5(k, carry):
        bc = [beta5(k, i) for i in range(4)]
        half = [pltpu.roll(v, 64, 1) for v in bc]
        after = [pltpu.roll(beta5(k + 1, i), 64, 1) for i in range(4)]
        before = [pltpu.roll(beta5(k - 1, i), 64, 1) for i in range(4)]
        for i in range(4):
            be = bc[i + 1] if i < 3 else jnp.where(subs5 == 7, 0.0, next_group(bc[0]))
            bw = bc[i - 1] if i > 0 else jnp.where(subs5 == 0, 0.0, last_group(bc[3]))
            bn = jnp.where(low, half[i], after[i])
            bs = jnp.where(low, before[i], half[i])
            bu = jnp.where(up_end, 0.0, pltpu.roll(bc[i], 127, 1))
            bd = jnp.where(down_end, 0.0, pltpu.roll(bc[i], 1, 1))
            c = [0.03125 * (bc[i] + v) for v in (be, bw, bn, bs, bu, bd)]
            diag = g5ab[0, k, i] + c[0] + c[1] + c[2] + c[3] + c[4] + c[5]
            inv = box_in(k) / diag
            t5[0, k, i] = c[0] * inv if i < 3 else jnp.where(subs5 == 7, 0.0, c[0] * inv)
            t5[1, k, i] = c[1] * inv if i > 0 else jnp.where(subs5 == 0, 0.0, c[1] * inv)
            t5[2, k, i] = c[2] * inv
            t5[3, k, i] = c[3] * inv
            t5[4, k, i] = jnp.where(up_end, 0.0, c[4] * inv)
            t5[5, k, i] = jnp.where(down_end, 0.0, c[5] * inv)
            inv5[k, i] = inv
        return carry

    lax.fori_loop(1, SPAN - 1, table5, 0)
    for copy in started:
        copy.wait_send()
    started = []

    fc = []
    for k, (first, last) in enumerate(((MID - 3, MID + 3), (1, MID - 4), (MID + 4, SPAN - 2))):
        for copy, db in zip(fb, fb_from):
            if first <= MID - db <= last:
                copy.wait_recv()
        span = pl.ds(first, last - first + 1)
        fc.append(
            remote(g5f.at[span, :, mine, :], g5f.at[span, :, mine, :], s_fc.at[k], r_fc.at[k], partner)
        )
    started += fc
    for copy in p4_boxes:
        copy.wait_recv()
    p4_groups = groups4(p4, s_p4, r_p4)
    started += p4_groups

    bottom_middle, bottom_pairs = coefficients(BOTTOM, BOTTOM_LOW)
    for m, (c1, c2) in enumerate(bottom_pairs):
        ends[m, 0] = F32(c1)
        ends[m, 1] = F32(c2)
    for copy in fc:
        copy.wait_recv()
    for k in range(1, SPAN - 1):
        for i in range(4):
            fd = g5f[k, i] * inv5[k, i]
            fd5[k, i] = fd
            x5b[k, i] = fd * (1.0 / bottom_middle)

    def sweep5(now, old, reach, c1, c2):
        lo, hi = MID - reach, MID + reach + 1
        half = {}

        def turned(k, i):
            if (k, i) not in half:
                half[k, i] = pltpu.roll(now[k, i], 64, 1)
            return half[k, i]

        for k in range(lo, hi):
            x = [now[k, i] for i in range(4)]
            for i in range(4):
                east = x[i + 1] if i < 3 else next_group(x[0])
                west = x[i - 1] if i > 0 else last_group(x[3])
                north = jnp.where(low, turned(k, i), turned(k + 1, i))
                south = jnp.where(low, turned(k - 1, i), turned(k, i))
                total = fd5[k, i] - x[i]
                total = total + t5[0, k, i] * east + t5[1, k, i] * west
                total = total + t5[2, k, i] * north + t5[3, k, i] * south
                total = total + t5[4, k, i] * pltpu.roll(x[i], 127, 1) + t5[5, k, i] * pltpu.roll(x[i], 1, 1)
                old[k, i] = x[i] + c1 * (x[i] - old[k, i]) + c2 * total

    def two(reach, first):
        def body(k, carry):
            m = first + 2 * k
            sweep5(x5b, x5a, reach, ends[m, 0], ends[m, 1])
            sweep5(x5a, x5b, reach - 1, ends[m + 1, 0], ends[m + 1, 1])
            return carry

        return body

    lax.fori_loop(0, 2, two(9, 0), 0)
    lax.fori_loop(0, 2, two(7, 4), 0)
    lax.fori_loop(0, 2, two(5, 8), 0)
    two(3, 12)(0, 0)
    sweep5(x5b, x5a, 2, ends[14, 0], ends[14, 1])

    for a in range(10):
        row = a - 3
        group = lax.rem(g + (row // 4) + NG, NG)
        at = 4 * lax.rem(group, 2) + group // 2
        for k in range(5):
            line = x5a[MID - 2 + k, row % 4, pl.ds(at, 1), :]
            first, last = max(4 * k - 2, 0), min(4 * k + 2, 16)
            q4[a, first:last, :] = jnp.broadcast_to(line, (last - first, 128))
    grown = dot(q4[...].reshape(160, 128), spread).reshape(10, 16, 256)
    rows4 = lax.broadcasted_iota(jnp.int32, (16, 128), 0)
    first_of_box = lax.rem(lax.shift_right_logical(rows4 + 2, 1), 2) == 0
    for copy in p4_groups:
        copy.wait_recv()
    for a in range(10):
        line = jnp.where(first_of_box, grown[a, :, 0:128], grown[a, :, 128:256])
        for r in (2 * a, 2 * a + 1):
            x4b[r] = jnp.where(m4, p4[1, r] + line, 0.0) * row_in(r, 8, 6)
            if 1 <= r < 19:
                fd4[r] = p4[0, r] * inv4[r]
    sweep(t4, fd4, x4b, x4a, 1, 19, 18, (1.0 / smooth_middle,))
    sweep(t4, fd4, x4a, x4b, 2, 18, 16, smooth_pairs[0])
    sweep(t4, fd4, x4b, x4a, 3, 17, 14, smooth_pairs[1])
    sweep(t4, fd4, x4a, x4b, 4, 16, 12, smooth_pairs[2])

    grown = dot(x4b[4:16, 4:12, :].reshape(96, 128), spread).reshape(12, 8, 256)
    for r in range(12):
        for k in range(2):
            line = grown[r, :, 128 * k : 128 * k + 128]
            u4[k, r, pl.ds(0, 8, stride=2), :] = line
            u4[k, r, pl.ds(1, 8, stride=2), :] = line
    for copy in x3_groups:
        copy.wait_recv()
    for r in range(24):
        row = row_in(r, N0, 4)
        for k in range(2):
            lanes = slice(128 * k, 128 * k + 128)
            x3b[r, :, lanes] = jnp.where(m3c[:, lanes], (h3[r, :, lanes] + u4[k, r // 2]) * row, 0.0)
    sweep(t3, fd3, x3b, x3a, 1, 23, 11, (1.0 / smooth_middle,))
    sweep(t3, fd3, x3a, x3b, 2, 22, 10, smooth_pairs[0])
    sweep(t3, fd3, x3b, x3a, 3, 21, 9, smooth_pairs[1])
    sweep(t3, fd3, x3a, x3b, 4, 20, 8, smooth_pairs[2])
    result = pltpu.make_async_copy(x3b.at[pl.ds(4, N0), pl.ds(4, N1), :], out, own_sem.at[0])
    result.start()
    for copy in started:
        copy.wait_send()
    result.wait()


SCRATCH = (
    [pltpu.VMEM(shape, F32) for shape in (
        (24, 16, 256), (24, 16, 256), (26, 24, 256), (6, 24, 16, 256), (24, 16, 256), (24, 16, 256),
        (24, 16, 256), (24, 16, 256), (24, 16, 256),
        (2, 20, 16, 128), (20, 16, 128), (2, 20, 16, 128), (6, 20, 16, 128), (20, 16, 128), (20, 16, 128),
        (20, 16, 128), (20, 16, 128), (20, 16, 128), (8, 16, 128),
        (8, 256), (2, SPAN, 4, 8, 128), (SPAN, 4, 8, 128), (6, SPAN, 4, 8, 128), (SPAN, 4, 8, 128),
        (SPAN, 4, 8, 128), (SPAN, 4, 8, 128), (SPAN, 4, 8, 128), (10, 16, 128), (8, 16, 256),
        (2, 12, 16, 128),
    )]
    + [pltpu.SemaphoreType.DMA((3,)), pltpu.SemaphoreType.REGULAR((2,)), pltpu.SMEM((16, 2), F32)]
    + [pltpu.SemaphoreType.DMA(shape) for count in (
        (3, 8), (6,), (8,), (4,), (6,), (3,), (2 * MID,), (1,), (3,), (2 * REACH,), (3,)
    ) for shape in (count, count)]
)


def cycle(source, alpha, beta):
    return pl.pallas_call(
        kernel,
        out_shape=jax.ShapeDtypeStruct((N0, N1, N2), F32),
        in_specs=[pl.BlockSpec(memory_space=pl.ANY)] * 3,
        out_specs=pl.BlockSpec(memory_space=pl.ANY),
        scratch_shapes=SCRATCH,
        compiler_params=pltpu.CompilerParams(
            collective_id=0, has_side_effects=True, vmem_limit_bytes=63 << 20
        ),
        name="vcycle",
    )(source, alpha, beta)


def solution(mesh):
    spec = P("grp", "box", None)
    return jax.shard_map(cycle, mesh=mesh, in_specs=(spec,) * 3, out_specs=spec, check_vma=False)
```

```python
import jax
import jax.numpy as jnp
from jax import lax
from jax.experimental import pallas as pl
from jax.experimental.pallas import tpu as pltpu
from jax.sharding import PartitionSpec as P

SMOOTH = 4
BOTTOM = 16
SMOOTH_LOW = 0.25
BOTTOM_LOW = 0.02
UPPER_BOUND = 2.0

MESH = pl.DeviceIdType.MESH
F32 = jnp.float32
NG, NB = 8, 32
N0, N1, N2 = 16, 8, 256
REACH = 9
MID = REACH + 1
SPAN = 2 * MID + 1

FACES = [(dg, db) for db in (-1, 1, 0) for dg in (0, -1, 1) if (dg, db) != (0, 0)]


def coefficients(degree, lower):
    middle = (UPPER_BOUND + lower) / 2.0
    spread = (UPPER_BOUND - lower) / 2.0
    base = middle / spread
    now = 1.0 / base
    pairs = []
    for _ in range(degree - 1):
        after = 1.0 / (2.0 * base - now)
        pairs.append((after * now, 2.0 * after / spread))
        now = after
    return middle, pairs


def part(step, size, width, origin):
    if step == 0:
        return 0, origin, size
    if step == 2:
        return size - (width - size), origin - width, width - size
    if step == -2:
        return 0, origin + 2 * size, width - size
    width = min(width, size)
    if step == 1:
        return size - width, origin - width, width
    return 0, origin + size, width


def kernel(
    source, alpha, beta, out,
    bo, af, to, fdo, xo, xr, lb, lz, f3, a3, b3, t3, d3, fd3, x3a, x3b, h3,
    ab4, f4, p4, t4, inv4, d4, fd4, x4a, x4b, w4,
    z5, g5ab, g5f, t5, inv5, fd5, x5a, x5b, q4, w3, u4,
    own_sem, hello, ends,
    s_p1, r_p1, s_x12, r_x12, s_late, r_late, s_ab4, r_ab4, s_f4, r_f4, s_x3, r_x3, s_p4, r_p4,
    s_aba, r_aba, s_abb, r_abb, s_abc, r_abc, s_fa, r_fa, s_fb, r_fb, s_fc, r_fc,
):
    g, b = lax.axis_index("grp"), lax.axis_index("box")
    core, chip = lax.rem(g, 2), g // 2
    sub = 4 * core + chip

    def device(dg, db):
        return (lax.rem(g + dg + NG, NG), lax.rem(b + db + NB, NB))

    def remote(src, dst, send, recv, target):
        copy = pltpu.make_async_remote_copy(
            src_ref=src, dst_ref=dst, send_sem=send, recv_sem=recv, device_id=target, device_id_type=MESH
        )
        copy.start()
        return copy

    started = []

    own = [
        pltpu.make_async_copy(beta, bo.at[pl.ds(5, N0)], own_sem.at[0]),
        pltpu.make_async_copy(alpha, af.at[0, pl.ds(4, N0)], own_sem.at[1]),
        pltpu.make_async_copy(source, af.at[1, pl.ds(4, N0)], own_sem.at[2]),
    ]
    for copy in own:
        copy.start()

    f4[...] = jnp.zeros_like(f4)

    partners = FACES + [(0, -8), (0, 8)]
    barrier = pltpu.get_barrier_semaphore()
    for dg, db in partners:
        pl.semaphore_signal(barrier, inc=1, device_id=device(dg, db), device_id_type=MESH)

    pl.semaphore_wait(barrier, len(partners))

    def halo(src, dst, dg, db, w0, w1, o0, o1, size, send, recv):
        s0, t0, l0 = part(dg, size[0], w0, o0)
        s1, t1, l1 = part(db, size[1], w1, o1)
        return remote(
            src(s0, l0, s1, l1), dst(t0, l0, t1, l1), send, recv, device(dg, db)
        )

    def window(ref):
        return lambda i, n, j, m: ref.at[pl.ds(i, n), pl.ds(j, m), :]

    def window2(ref):
        return lambda i, n, j, m: ref.at[:, pl.ds(i, n), pl.ds(j, m), :]

    def inner(ref, o0, o1):
        return lambda i, n, j, m: ref.at[pl.ds(o0 + i, n), pl.ds(o1 + j, m), :]

    def inner2(ref, o0, o1):
        return lambda i, n, j, m: ref.at[:, pl.ds(o0 + i, n), pl.ds(o1 + j, m), :]

    along = []
    for n, (src, dst, w, o0) in enumerate(
        ((beta, bo, 5, 5), (alpha, af.at[0], 4, 4), (source, af.at[1], 4, 4))
    ):
        for k, dg in enumerate((-1, 1)):
            s0, t0, l0 = part(dg, N0, w, o0)
            along.append(
                remote(src.at[pl.ds(s0, l0)], dst.at[pl.ds(t0, l0)], s_p1.at[n, k], r_p1.at[n, k], device(dg, 0))
            )
    started += along
    p1 = []
    for n, (src, dst, w0, w1, o0, o1) in enumerate(
        ((beta, b3, 5, 3, 5, 8), (alpha, a3, 4, 2, 4, 4), (source, f3, 4, 2, 4, 4))
    ):
        for k, (dg, db) in enumerate(FACES[:6]):
            p1.append(
                halo(
                    window(src), window(dst), dg, db, w0, w1, o0, o1, (N0, N1),
                    s_p1.at[n, 2 + k], r_p1.at[n, 2 + k],
                )
            )
    started += p1

    def greet(n, peers):
        for dg, db in peers:
            pl.semaphore_signal(hello.at[n], inc=1, device_id=device(dg, db), device_id_type=MESH)

    greet(0, ((0, -1), (0, 1), (-1, 0), (1, 0)))

    rows256 = lax.broadcasted_iota(jnp.int32, (256, 128), 0)
    cols128 = lax.broadcasted_iota(jnp.int32, (256, 128), 1)
    gather = jnp.where(lax.shift_right_logical(rows256, 1) == cols128, 1.0, 0.0).astype(F32)
    rows128 = lax.broadcasted_iota(jnp.int32, (128, 256), 0)
    cols256 = lax.broadcasted_iota(jnp.int32, (128, 256), 1)
    spread = jnp.where(lax.shift_right_logical(cols256, 1) == rows128, 1.0, 0.0).astype(F32)

    def dot(x, matrix):
        return jnp.dot(x, matrix, precision=lax.Precision.HIGHEST, preferred_element_type=F32)

    def halve(pairs, o1):
        n = pairs.shape[1]
        w4[:, 0:n, :] = dot(pairs.reshape(8 * n, 256), gather).reshape(8, n, 128)
        return 0.125 * (w4[:, pl.ds(o1, 4, stride=2), :] + w4[:, pl.ds(o1 + 1, 4, stride=2), :])

    def pack(get, row):
        for i in range(4):
            t = get(2 * i) + get(2 * i + 1)
            z5[pl.ds(row + i, 1), 0:128] = t[0:1] + t[1:2]
            z5[pl.ds(row + i, 1), 128:256] = t[2:3] + t[3:4]

    for copy in own[:2]:
        copy.wait()
    ab4[0, 6:14, 6:10, :] = halve(
        jnp.stack([af[0, 4 + 2 * i] + af[0, 5 + 2 * i] for i in range(8)]), 0
    )
    ab4[1, 6:14, 6:10, :] = halve(
        jnp.stack([bo[5 + 2 * i] + bo[6 + 2 * i] for i in range(8)]), 0
    )
    pl.semaphore_wait(hello.at[0], 4)
    greet(1, ((0, -2), (0, 2), (-2, 0), (2, 0)))
    def inside(start, shape, axis, count):
        at = lax.broadcasted_iota(jnp.int32, shape, axis) + start
        return (at >= 0) & (at < count)

    def row_in(r, size, origin):
        at = size * g + r - origin
        return jnp.where((at >= 0) & (at < size * NG), 1.0, 0.0).astype(F32)

    lanes3 = lax.broadcasted_iota(jnp.int32, (16, 256), 1)
    smooth_middle, smooth_pairs = coefficients(SMOOTH, SMOOTH_LOW)

    def scaled_residual(t, fd, x, r):
        here = x[r]
        n, m = here.shape
        total = fd[r] - here
        total = total + t[0, r] * x[r + 1] + t[1, r] * x[r - 1]
        total = total + t[2, r] * pltpu.roll(here, n - 1, 0) + t[3, r] * pltpu.roll(here, 1, 0)
        return total + t[4, r] * pltpu.roll(here, m - 1, 1) + t[5, r] * pltpu.roll(here, 1, 1)

    def first(r, carry):
        here = row_in(r, N0, 4)
        bc = bo[r + 1] * here
        be = bo[r + 2] * row_in(r + 1, N0, 4)
        bw = bo[r] * row_in(r - 1, N0, 4)
        bn, bs = pltpu.roll(bc, 7, 0), pltpu.roll(bc, 1, 0)
        bu = jnp.where(lanes3[0:8] == 255, 0.0, pltpu.roll(bc, 255, 1))
        bd = jnp.where(lanes3[0:8] == 0, 0.0, pltpu.roll(bc, 1, 1))
        c = [0.5 * (bc + v) for v in (be, bw, bn, bs, bu, bd)]
        inv = here / (af[0, r] + c[0] + c[1] + c[2] + c[3] + c[4] + c[5])
        for n in range(4):
            to[n, r] = c[n] * inv
        to[4, r] = jnp.where(lanes3[0:8] == 255, 0.0, c[4] * inv)
        to[5, r] = jnp.where(lanes3[0:8] == 0, 0.0, c[5] * inv)
        fd = af[1, r] * inv
        fdo[r] = fd
        xo[0, r] = fd * (1.0 / smooth_middle)
        return carry

    def second(r, carry):
        here = xo[0, r]
        total = scaled_residual(to, fdo, xo.at[0], r)
        xo[1, r] = here + smooth_pairs[0][0] * here + smooth_pairs[0][1] * total
        return carry

    own[2].wait()
    for copy in along:
        copy.wait_recv()
    lax.fori_loop(0, 24, first, 0, unroll=6)
    lax.fori_loop(1, 23, second, 0, unroll=11)
    for r in (0, 23):
        xo[1, r] = jnp.zeros_like(xo[1, r])
    x12 = []
    for k, (db, src_at, dst_at) in enumerate(((1, 5, 1), (-1, 2, 6))):
        x12.append(
            remote(
                xo.at[:, :, pl.ds(src_at, 1), :], xr.at[:, :, pl.ds(dst_at, 1), :],
                s_x12.at[k], r_x12.at[k], device(0, db),
            )
        )
    started += x12

    for n in range(2):
        pack(lambda r, n=n: ab4[n, 6 + r, 6:10, :], 4 * n)
    packed = 0.125 * dot(z5[...], gather)
    for n in range(2):
        for i in range(4):
            g5ab[n, MID, i, pl.ds(sub, 1), :] = packed[4 * n + i : 4 * n + i + 1]
    pl.semaphore_wait(hello.at[1], 4)
    abb = []
    for k, db in enumerate([s * d for d in range(MID, 0, -1) for s in (-1, 1)]):
        abb.append(
            remote(
                g5ab.at[:, MID, :, pl.ds(sub, 1), :],
                g5ab.at[:, MID - db, :, pl.ds(sub, 1), :],
                s_abb.at[k], r_abb.at[k], device(0, db),
            )
        )
    started += abb

    def boxes4(ref, send, recv):
        copies = []
        for k, db in enumerate((-2, 2, -1, 1)):
            copies.append(
                halo(inner2(ref, 6, 6), window2(ref), 0, db, 6, 6, 6, 6, (8, 4), send.at[k], recv.at[k])
            )
        return copies

    def groups4(ref, send, recv):
        copies = []
        for k, dg in enumerate((-1, 1)):
            s0, t0, l0 = part(dg, 8, 6, 6)
            copies.append(
                remote(
                    ref.at[:, pl.ds(6 + s0, l0)], ref.at[:, pl.ds(t0, l0)],
                    send.at[4 + k], recv.at[4 + k], device(dg, 0),
                )
            )
        return copies

    ab4_boxes = boxes4(ab4, s_ab4, r_ab4)
    started += ab4_boxes

    x4a[...] = jnp.zeros_like(x4a)
    x5a[...] = jnp.zeros_like(x5a)
    x5b[...] = jnp.zeros_like(x5b)

    def place(r, carry):
        b3[r, 8:16, :] = bo[r]
        return carry

    def place2(r, carry):
        a3[r, 4:12, :] = af[0, r]
        f3[r, 4:12, :] = af[1, r]
        return carry

    lax.fori_loop(0, 26, place, 0, unroll=13)
    lax.fori_loop(0, 24, place2, 0, unroll=8)
    for copy in p1[:12]:
        copy.wait_recv()

    m3c = inside(N1 * b - 4, (16, 256), 0, N1 * NB)
    m3n = inside(N1 * b - 3, (16, 256), 0, N1 * NB)
    m3s = inside(N1 * b - 5, (16, 256), 0, N1 * NB)

    def table3(r, carry):
        here = row_in(r, N0, 4)
        bc = jnp.where(m3c, b3[r + 1, pl.ds(4, 16), :], 0.0) * here
        be = jnp.where(m3c, b3[r + 2, pl.ds(4, 16), :], 0.0) * row_in(r + 1, N0, 4)
        bw = jnp.where(m3c, b3[r, pl.ds(4, 16), :], 0.0) * row_in(r - 1, N0, 4)
        bn = jnp.where(m3n, b3[r + 1, pl.ds(5, 16), :], 0.0) * here
        bs = jnp.where(m3s, b3[r + 1, pl.ds(3, 16), :], 0.0) * here
        bu = jnp.where(lanes3 == 255, 0.0, pltpu.roll(bc, 255, 1))
        bd = jnp.where(lanes3 == 0, 0.0, pltpu.roll(bc, 1, 1))
        c = [0.5 * (bc + v) for v in (be, bw, bn, bs, bu, bd)]
        diag = a3[r] + c[0] + c[1] + c[2] + c[3] + c[4] + c[5]
        inv = jnp.where(m3c, 1.0 / diag, 0.0) * here
        for n in range(4):
            t3[n, r] = c[n] * inv
        t3[4, r] = jnp.where(lanes3 == 255, 0.0, c[4] * inv)
        t3[5, r] = jnp.where(lanes3 == 0, 0.0, c[5] * inv)
        d3[r] = diag
        fd3[r] = inv
        return carry

    def start3(r, carry):
        fd = f3[r] * fd3[r]
        fd3[r] = fd
        x3b[r] = fd * (1.0 / smooth_middle)
        x3a[r] = jnp.zeros_like(fd)
        return carry

    lax.fori_loop(0, 24, table3, 0, unroll=4)
    for copy in p1[12:]:
        copy.wait_recv()
    lax.fori_loop(0, 24, start3, 0, unroll=8)
    below = jnp.where(b > 0, 1.0, 0.0).astype(F32)
    above = jnp.where(b < NB - 1, 1.0, 0.0).astype(F32)

    def given(ref, n):
        def rows(r, carry):
            ref[r, 1:2, :] = xr[n, r, 1:2, :] * below
            ref[r, 14:15, :] = xr[n, r, 6:7, :] * above
            return carry

        lax.fori_loop(0, 24, rows, 0, unroll=8)

    for copy in x12:
        copy.wait_recv()
    given(x3b, 0)

    def sweep(t, fd, now, old, lo, hi, chunk, pair):
        def rows(k, carry):
            for i in range(chunk):
                r = lo + k * chunk + i
                total = scaled_residual(t, fd, now, r)
                here = now[r]
                if len(pair) == 1:
                    old[r] = here + pair[0] * total
                else:
                    old[r] = here + pair[0] * (here - old[r]) + pair[1] * total
            return carry

        lax.fori_loop(0, (hi - lo) // chunk, rows, 0)

    sweep(t3, fd3, x3b, x3a, 1, 23, 11, smooth_pairs[0])
    given(x3a, 1)
    sweep(t3, fd3, x3a, x3b, 2, 22, 10, smooth_pairs[1])
    sweep(t3, fd3, x3b, x3a, 3, 21, 9, smooth_pairs[2])

    def fine_residual(i):
        return d3[i] * scaled_residual(t3, fd3, x3a, i)

    for i in range(8):
        w3[i] = fine_residual(4 + 2 * i) + fine_residual(5 + 2 * i)
    f4[6:14, 6:10, :] = halve(w3[...], 4)
    f4_copies = []
    for k, (dg, db) in enumerate(FACES):
        f4_copies.append(
            halo(inner(f4, 6, 6), window(f4), dg, db, 4, 4, 6, 6, (8, 4), s_f4.at[k], r_f4.at[k])
        )
    started += f4_copies
    for i in range(16):
        h3[4 + i, 4:12, :] = x3a[4 + i, 4:12, :]
    x3_copies = []
    for copy in ab4_boxes:
        copy.wait_recv()
    ab4_groups = groups4(ab4, s_ab4, r_ab4)
    started += ab4_groups
    for k, db in enumerate((-1, 1)):
        x3_copies.append(
            halo(inner(h3, 4, 4), window(h3), 0, db, 4, 4, 4, 4, (N0, N1), s_x3.at[k], r_x3.at[k])
        )
    started += x3_copies
    late = []
    for k, (db, b_at, b_to, a_at, a_to) in enumerate(((1, 4, 4, 5, 1), (-1, 3, 3, 2, 6))):
        late.append(
            remote(
                bo.at[:, pl.ds(b_at, 1), :], lb.at[:, pl.ds(b_to, 1), :],
                s_late.at[0, k], r_late.at[0, k], device(0, db),
            )
        )
        late.append(
            remote(
                af.at[:, :, pl.ds(a_at, 1), :], lz.at[:, :, pl.ds(a_to, 1), :],
                s_late.at[1, k], r_late.at[1, k], device(0, db),
            )
        )
    started += late

    for copy in abb:
        copy.wait_recv()
    aba = []
    for k, dg in enumerate((2, 4, 6)):
        aba.append(
            remote(
                g5ab.at[:, :, :, pl.ds(sub, 1), :], g5ab.at[:, :, :, pl.ds(sub, 1), :],
                s_aba.at[k], r_aba.at[k], device(dg, 0),
            )
        )
    started += aba

    for copy in ab4_groups:
        copy.wait_recv()
    lanes4 = lax.broadcasted_iota(jnp.int32, (16, 128), 1)
    m4 = inside(4 * b - 6, (16, 128), 0, 4 * NB)

    def masked4(r):
        return jnp.where(m4, ab4[1, r], 0.0) * row_in(r, 8, 6)

    def table4(r, carry):
        bc = masked4(r)
        be, bw = masked4(r + 1), masked4(r - 1)
        bn, bs = pltpu.roll(bc, 15, 0), pltpu.roll(bc, 1, 0)
        bu = jnp.where(lanes4 == 127, 0.0, pltpu.roll(bc, 127, 1))
        bd = jnp.where(lanes4 == 0, 0.0, pltpu.roll(bc, 1, 1))
        c = [0.125 * (bc + v) for v in (be, bw, bn, bs, bu, bd)]
        diag = ab4[0, r] + c[0] + c[1] + c[2] + c[3] + c[4] + c[5]
        inv = jnp.where(m4, 1.0 / diag, 0.0) * row_in(r, 8, 6)
        for n in range(4):
            t4[n, r] = c[n] * inv
        t4[4, r] = jnp.where(lanes4 == 127, 0.0, c[4] * inv)
        t4[5, r] = jnp.where(lanes4 == 0, 0.0, c[5] * inv)
        d4[r] = diag
        inv4[r] = inv
        return carry

    lax.fori_loop(1, 19, table4, 0, unroll=6)

    mine = pl.ds(pl.multiple_of(4 * core, 4), 4)
    partner = (g + 1 - 2 * core, b)

    for copy in f4_copies:
        copy.wait_recv()
    for r in range(2, 18):
        fd = f4[r] * inv4[r]
        fd4[r] = fd
        x4b[r] = fd * (1.0 / smooth_middle)
    sweep(t4, fd4, x4b, x4a, 3, 17, 14, smooth_pairs[0])
    sweep(t4, fd4, x4a, x4b, 4, 16, 12, smooth_pairs[1])
    sweep(t4, fd4, x4b, x4a, 5, 15, 10, smooth_pairs[2])

    for r in range(8):
        w4[r] = d4[6 + r] * scaled_residual(t4, fd4, x4a, 6 + r)
    pack(lambda r: w4[r, 6:10, :], 0)
    packed = 0.125 * dot(z5[...], gather)
    for i in range(4):
        g5f[MID, i, pl.ds(sub, 1), :] = packed[i : i + 1]
    fa = []
    for k, dg in enumerate((2, 4, 6)):
        fa.append(
            remote(
                g5f.at[MID, :, pl.ds(sub, 1), :], g5f.at[MID, :, pl.ds(sub, 1), :],
                s_fa.at[k], r_fa.at[k], device(dg, 0),
            )
        )
    started += fa

    for copy in aba:
        copy.wait_recv()
    abc = remote(
        g5ab.at[:, :, :, mine, :], g5ab.at[:, :, :, mine, :], s_abc.at[0], r_abc.at[0], partner
    )
    started.append(abc)

    for copy in x3_copies:
        copy.wait_recv()
    x3_groups = []
    for k, dg in enumerate((-1, 1)):
        s0, t0, l0 = part(dg, N0, 4, 4)
        x3_groups.append(
            remote(
                h3.at[pl.ds(4 + s0, l0)], h3.at[pl.ds(t0, l0)],
                s_x3.at[2 + k], r_x3.at[2 + k], device(dg, 0),
            )
        )
    started += x3_groups

    p4[0, 6:14, 6:10, :] = f4[6:14, 6:10, :]
    p4[1, 6:14, 6:10, :] = x4a[6:14, 6:10, :]
    for copy in fa:
        copy.wait_recv()
    fb = []
    fb_from = [s * d for d in range(REACH, 0, -1) for s in (-1, 1)]
    for k, db in enumerate(fb_from):
        fb.append(
            remote(
                g5f.at[MID, :, mine, :], g5f.at[MID - db, :, mine, :],
                s_fb.at[k], r_fb.at[k], device(0, db),
            )
        )
    started += fb
    p4_boxes = boxes4(p4, s_p4, r_p4)
    started += p4_boxes

    abc.wait_recv()
    lanes5 = lax.broadcasted_iota(jnp.int32, (8, 128), 1)
    subs5 = lax.broadcasted_iota(jnp.int32, (8, 128), 0)
    low = lanes5 < 64
    front = subs5 < 4
    up_end = (lanes5 == 63) | (lanes5 == 127)
    down_end = (lanes5 == 0) | (lanes5 == 64)

    def next_group(v):
        return jnp.where(front, pltpu.roll(v, 4, 0), pltpu.roll(v, 3, 0))

    def last_group(v):
        return jnp.where(front, pltpu.roll(v, 5, 0), pltpu.roll(v, 4, 0))

    def box_in(k):
        at = b + k - MID
        return jnp.where((at >= 0) & (at < NB), 1.0, 0.0).astype(F32)

    def beta5(k, i):
        return g5ab[1, k, i] * box_in(k)

    def table5(k, carry):
        bc = [beta5(k, i) for i in range(4)]
        half = [pltpu.roll(v, 64, 1) for v in bc]
        after = [pltpu.roll(beta5(k + 1, i), 64, 1) for i in range(4)]
        before = [pltpu.roll(beta5(k - 1, i), 64, 1) for i in range(4)]
        for i in range(4):
            be = bc[i + 1] if i < 3 else jnp.where(subs5 == 7, 0.0, next_group(bc[0]))
            bw = bc[i - 1] if i > 0 else jnp.where(subs5 == 0, 0.0, last_group(bc[3]))
            bn = jnp.where(low, half[i], after[i])
            bs = jnp.where(low, before[i], half[i])
            bu = jnp.where(up_end, 0.0, pltpu.roll(bc[i], 127, 1))
            bd = jnp.where(down_end, 0.0, pltpu.roll(bc[i], 1, 1))
            c = [0.03125 * (bc[i] + v) for v in (be, bw, bn, bs, bu, bd)]
            diag = g5ab[0, k, i] + c[0] + c[1] + c[2] + c[3] + c[4] + c[5]
            inv = box_in(k) / diag
            t5[0, k, i] = c[0] * inv if i < 3 else jnp.where(subs5 == 7, 0.0, c[0] * inv)
            t5[1, k, i] = c[1] * inv if i > 0 else jnp.where(subs5 == 0, 0.0, c[1] * inv)
            t5[2, k, i] = c[2] * inv
            t5[3, k, i] = c[3] * inv
            t5[4, k, i] = jnp.where(up_end, 0.0, c[4] * inv)
            t5[5, k, i] = jnp.where(down_end, 0.0, c[5] * inv)
            inv5[k, i] = inv
        return carry

    lax.fori_loop(1, SPAN - 1, table5, 0)

    for copy in late:
        copy.wait_recv()

    def widen(r, carry):
        b3[r, 4:5, :] = lb[r, 4:5, :]
        b3[r, 19:20, :] = lb[r, 3:4, :]
        return carry

    def widen2(r, carry):
        a3[r, 1:2, :] = lz[0, r, 1:2, :]
        a3[r, 14:15, :] = lz[0, r, 6:7, :]
        f3[r, 1:2, :] = lz[1, r, 1:2, :]
        f3[r, 14:15, :] = lz[1, r, 6:7, :]
        return carry

    def restart3(r, carry):
        fd3[r] = f3[r] * fd3[r]
        return carry

    lax.fori_loop(0, 26, widen, 0, unroll=13)
    lax.fori_loop(0, 24, widen2, 0, unroll=8)
    lax.fori_loop(0, 24, table3, 0, unroll=4)
    lax.fori_loop(0, 24, restart3, 0, unroll=8)
    for copy in started:
        copy.wait_send()
    started = []

    fc = []
    for k, (first, last) in enumerate(((MID - 3, MID + 3), (1, MID - 4), (MID + 4, SPAN - 2))):
        for copy, db in zip(fb, fb_from):
            if first <= MID - db <= last:
                copy.wait_recv()
        span = pl.ds(first, last - first + 1)
        fc.append(
            remote(g5f.at[span, :, mine, :], g5f.at[span, :, mine, :], s_fc.at[k], r_fc.at[k], partner)
        )
    started += fc
    for copy in p4_boxes:
        copy.wait_recv()
    p4_groups = groups4(p4, s_p4, r_p4)
    started += p4_groups

    bottom_middle, bottom_pairs = coefficients(BOTTOM, BOTTOM_LOW)
    for m, (c1, c2) in enumerate(bottom_pairs):
        ends[m, 0] = F32(c1)
        ends[m, 1] = F32(c2)
    for copy in fc:
        copy.wait_recv()
    for k in range(1, SPAN - 1):
        for i in range(4):
            fd = g5f[k, i] * inv5[k, i]
            fd5[k, i] = fd
            x5b[k, i] = fd * (1.0 / bottom_middle)

    def sweep5(now, old, reach, c1, c2):
        lo, hi = MID - reach, MID + reach + 1
        half = {}

        def turned(k, i):
            if (k, i) not in half:
                half[k, i] = pltpu.roll(now[k, i], 64, 1)
            return half[k, i]

        for k in range(lo, hi):
            x = [now[k, i] for i in range(4)]
            for i in range(4):
                east = x[i + 1] if i < 3 else next_group(x[0])
                west = x[i - 1] if i > 0 else last_group(x[3])
                north = jnp.where(low, turned(k, i), turned(k + 1, i))
                south = jnp.where(low, turned(k - 1, i), turned(k, i))
                total = fd5[k, i] - x[i]
                total = total + t5[0, k, i] * east + t5[1, k, i] * west
                total = total + t5[2, k, i] * north + t5[3, k, i] * south
                total = total + t5[4, k, i] * pltpu.roll(x[i], 127, 1) + t5[5, k, i] * pltpu.roll(x[i], 1, 1)
                old[k, i] = x[i] + c1 * (x[i] - old[k, i]) + c2 * total

    def two(reach, first):
        def body(k, carry):
            m = first + 2 * k
            sweep5(x5b, x5a, reach, ends[m, 0], ends[m, 1])
            sweep5(x5a, x5b, reach - 1, ends[m + 1, 0], ends[m + 1, 1])
            return carry

        return body

    lax.fori_loop(0, 2, two(9, 0), 0)
    lax.fori_loop(0, 2, two(7, 4), 0)
    lax.fori_loop(0, 2, two(5, 8), 0)
    two(3, 12)(0, 0)
    sweep5(x5b, x5a, 2, ends[14, 0], ends[14, 1])

    for a in range(10):
        row = a - 3
        group = lax.rem(g + (row // 4) + NG, NG)
        at = 4 * lax.rem(group, 2) + group // 2
        for k in range(5):
            line = x5a[MID - 2 + k, row % 4, pl.ds(at, 1), :]
            first, last = max(4 * k - 2, 0), min(4 * k + 2, 16)
            q4[a, first:last, :] = jnp.broadcast_to(line, (last - first, 128))
    grown = dot(q4[...].reshape(160, 128), spread).reshape(10, 16, 256)
    rows4 = lax.broadcasted_iota(jnp.int32, (16, 128), 0)
    first_of_box = lax.rem(lax.shift_right_logical(rows4 + 2, 1), 2) == 0
    for copy in p4_groups:
        copy.wait_recv()
    for a in range(10):
        line = jnp.where(first_of_box, grown[a, :, 0:128], grown[a, :, 128:256])
        for r in (2 * a, 2 * a + 1):
            x4b[r] = jnp.where(m4, p4[1, r] + line, 0.0) * row_in(r, 8, 6)
            if 1 <= r < 19:
                fd4[r] = p4[0, r] * inv4[r]
    sweep(t4, fd4, x4b, x4a, 1, 19, 18, (1.0 / smooth_middle,))
    sweep(t4, fd4, x4a, x4b, 2, 18, 16, smooth_pairs[0])
    sweep(t4, fd4, x4b, x4a, 3, 17, 14, smooth_pairs[1])
    sweep(t4, fd4, x4a, x4b, 4, 16, 12, smooth_pairs[2])

    grown = dot(x4b[4:16, 4:12, :].reshape(96, 128), spread).reshape(12, 8, 256)
    for r in range(12):
        for k in range(2):
            line = grown[r, :, 128 * k : 128 * k + 128]
            u4[k, r, pl.ds(0, 8, stride=2), :] = line
            u4[k, r, pl.ds(1, 8, stride=2), :] = line
    for copy in x3_groups:
        copy.wait_recv()
    for r in range(24):
        row = row_in(r, N0, 4)
        for k in range(2):
            lanes = slice(128 * k, 128 * k + 128)
            x3b[r, :, lanes] = jnp.where(m3c[:, lanes], (h3[r, :, lanes] + u4[k, r // 2]) * row, 0.0)
    sweep(t3, fd3, x3b, x3a, 1, 23, 11, (1.0 / smooth_middle,))
    sweep(t3, fd3, x3a, x3b, 2, 22, 10, smooth_pairs[0])
    sweep(t3, fd3, x3b, x3a, 3, 21, 9, smooth_pairs[1])
    sweep(t3, fd3, x3a, x3b, 4, 20, 8, smooth_pairs[2])
    result = pltpu.make_async_copy(x3b.at[pl.ds(4, N0), pl.ds(4, N1), :], out, own_sem.at[0])
    result.start()
    for copy in started:
        copy.wait_send()
    result.wait()


SCRATCH = (
    [pltpu.VMEM(shape, F32) for shape in (
        (26, 8, 256), (2, 24, 8, 256), (6, 24, 8, 256), (24, 8, 256), (2, 24, 8, 256), (2, 24, 8, 256),
        (26, 8, 256), (2, 24, 8, 256),
        (24, 16, 256), (24, 16, 256), (26, 24, 256), (6, 24, 16, 256), (24, 16, 256), (24, 16, 256),
        (24, 16, 256), (24, 16, 256), (24, 16, 256),
        (2, 20, 16, 128), (20, 16, 128), (2, 20, 16, 128), (6, 20, 16, 128), (20, 16, 128), (20, 16, 128),
        (20, 16, 128), (20, 16, 128), (20, 16, 128), (8, 16, 128),
        (8, 256), (2, SPAN, 4, 8, 128), (SPAN, 4, 8, 128), (6, SPAN, 4, 8, 128), (SPAN, 4, 8, 128),
        (SPAN, 4, 8, 128), (SPAN, 4, 8, 128), (SPAN, 4, 8, 128), (10, 16, 128), (8, 16, 256),
        (2, 12, 16, 128),
    )]
    + [pltpu.SemaphoreType.DMA((3,)), pltpu.SemaphoreType.REGULAR((2,)), pltpu.SMEM((16, 2), F32)]
    + [pltpu.SemaphoreType.DMA(shape) for count in (
        (3, 8), (2,), (2, 2), (6,), (8,), (4,), (6,), (3,), (2 * MID,), (1,), (3,), (2 * REACH,), (3,)
    ) for shape in (count, count)]
)


def cycle(source, alpha, beta):
    return pl.pallas_call(
        kernel,
        out_shape=jax.ShapeDtypeStruct((N0, N1, N2), F32),
        in_specs=[pl.BlockSpec(memory_space=pl.ANY)] * 3,
        out_specs=pl.BlockSpec(memory_space=pl.ANY),
        scratch_shapes=SCRATCH,
        compiler_params=pltpu.CompilerParams(
            collective_id=0, has_side_effects=True, vmem_limit_bytes=63 << 20
        ),
        name="vcycle",
    )(source, alpha, beta)


def solution(mesh):
    spec = P("grp", "box", None)
    return jax.shard_map(cycle, mesh=mesh, in_specs=(spec,) * 3, out_specs=spec, check_vma=False)
```

```python
import jax
import jax.numpy as jnp
from jax import lax
from jax.experimental import pallas as pl
from jax.experimental.pallas import tpu as pltpu
from jax.sharding import PartitionSpec as P

SMOOTH = 4
BOTTOM = 16
SMOOTH_LOW = 0.25
BOTTOM_LOW = 0.02
UPPER_BOUND = 2.0

MESH = pl.DeviceIdType.MESH
F32 = jnp.float32
NG, NB = 8, 32
N0, N1, N2 = 16, 8, 256
REACH = 9
MID = REACH + 1
SPAN = 2 * MID + 1

FACES = [(dg, db) for db in (-1, 1, 0) for dg in (0, -1, 1) if (dg, db) != (0, 0)]


def coefficients(degree, lower):
    middle = (UPPER_BOUND + lower) / 2.0
    spread = (UPPER_BOUND - lower) / 2.0
    base = middle / spread
    now = 1.0 / base
    pairs = []
    for _ in range(degree - 1):
        after = 1.0 / (2.0 * base - now)
        pairs.append((after * now, 2.0 * after / spread))
        now = after
    return middle, pairs


def part(step, size, width, origin):
    if step == 0:
        return 0, origin, size
    if step == 2:
        return size - (width - size), origin - width, width - size
    if step == -2:
        return 0, origin + 2 * size, width - size
    width = min(width, size)
    if step == 1:
        return size - width, origin - width, width
    return 0, origin + size, width


def kernel(
    source, alpha, beta, out,
    bo, af, to, fdo, xo, xr, lb, lz, f3, a3, b3, t3, d3, fd3, x3a, x3b, h3,
    ab4, f4, p4, t4, inv4, d4, fd4, x4a, x4b, w4,
    z5, g5ab, g5f, t5, inv5, fd5, x5a, x5b, q4, w3, u4,
    own_sem, hello, ends,
    s_p1, r_p1, s_x12, r_x12, s_late, r_late, s_ab4, r_ab4, s_f4, r_f4, s_x3, r_x3, s_p4, r_p4,
    s_aba, r_aba, s_abb, r_abb, s_abc, r_abc, s_fa, r_fa, s_fb, r_fb, s_fc, r_fc,
):
    g, b = lax.axis_index("grp"), lax.axis_index("box")
    core, chip = lax.rem(g, 2), g // 2
    sub = 4 * core + chip

    def device(dg, db):
        return (lax.rem(g + dg + NG, NG), lax.rem(b + db + NB, NB))

    def remote(src, dst, send, recv, target):
        copy = pltpu.make_async_remote_copy(
            src_ref=src, dst_ref=dst, send_sem=send, recv_sem=recv, device_id=target, device_id_type=MESH
        )
        copy.start()
        return copy

    started = []

    own = [
        pltpu.make_async_copy(beta, bo.at[pl.ds(5, N0)], own_sem.at[0]),
        pltpu.make_async_copy(alpha, af.at[0, pl.ds(4, N0)], own_sem.at[1]),
        pltpu.make_async_copy(source, af.at[1, pl.ds(4, N0)], own_sem.at[2]),
    ]
    for copy in own:
        copy.start()

    partners = FACES + [(0, -8), (0, 8)]
    barrier = pltpu.get_barrier_semaphore()
    for dg, db in partners:
        pl.semaphore_signal(barrier, inc=1, device_id=device(dg, db), device_id_type=MESH)

    f4[...] = jnp.zeros_like(f4)
    pl.semaphore_wait(barrier, len(partners))

    def halo(src, dst, dg, db, w0, w1, o0, o1, size, send, recv):
        s0, t0, l0 = part(dg, size[0], w0, o0)
        s1, t1, l1 = part(db, size[1], w1, o1)
        return remote(
            src(s0, l0, s1, l1), dst(t0, l0, t1, l1), send, recv, device(dg, db)
        )

    def window(ref):
        return lambda i, n, j, m: ref.at[pl.ds(i, n), pl.ds(j, m), :]

    def window2(ref):
        return lambda i, n, j, m: ref.at[:, pl.ds(i, n), pl.ds(j, m), :]

    def inner(ref, o0, o1):
        return lambda i, n, j, m: ref.at[pl.ds(o0 + i, n), pl.ds(o1 + j, m), :]

    def inner2(ref, o0, o1):
        return lambda i, n, j, m: ref.at[:, pl.ds(o0 + i, n), pl.ds(o1 + j, m), :]

    along = []
    for n, (src, dst, w, o0) in enumerate(
        ((beta, bo, 5, 5), (alpha, af.at[0], 4, 4), (source, af.at[1], 4, 4))
    ):
        for k, dg in enumerate((-1, 1)):
            s0, t0, l0 = part(dg, N0, w, o0)
            along.append(
                remote(src.at[pl.ds(s0, l0)], dst.at[pl.ds(t0, l0)], s_p1.at[n, k], r_p1.at[n, k], device(dg, 0))
            )
    started += along
    p1 = []
    for n, (src, dst, w0, w1, o0, o1) in enumerate(
        ((beta, b3, 5, 3, 5, 8), (alpha, a3, 4, 2, 4, 4), (source, f3, 4, 2, 4, 4))
    ):
        for k, (dg, db) in enumerate(FACES[:6]):
            p1.append(
                halo(
                    window(src), window(dst), dg, db, w0, w1, o0, o1, (N0, N1),
                    s_p1.at[n, 2 + k], r_p1.at[n, 2 + k],
                )
            )
    started += p1

    def greet(n, peers):
        for dg, db in peers:
            pl.semaphore_signal(hello.at[n], inc=1, device_id=device(dg, db), device_id_type=MESH)

    greet(0, ((0, -1), (0, 1), (-1, 0), (1, 0)))

    rows256 = lax.broadcasted_iota(jnp.int32, (256, 128), 0)
    cols128 = lax.broadcasted_iota(jnp.int32, (256, 128), 1)
    gather = jnp.where(lax.shift_right_logical(rows256, 1) == cols128, 1.0, 0.0).astype(F32)
    rows128 = lax.broadcasted_iota(jnp.int32, (128, 256), 0)
    cols256 = lax.broadcasted_iota(jnp.int32, (128, 256), 1)
    spread = jnp.where(lax.shift_right_logical(cols256, 1) == rows128, 1.0, 0.0).astype(F32)

    def dot(x, matrix):
        return jnp.dot(x, matrix, precision=lax.Precision.HIGHEST, preferred_element_type=F32)

    def halve(pairs, o1):
        n = pairs.shape[1]
        w4[:, 0:n, :] = dot(pairs.reshape(8 * n, 256), gather).reshape(8, n, 128)
        return 0.125 * (w4[:, pl.ds(o1, 4, stride=2), :] + w4[:, pl.ds(o1 + 1, 4, stride=2), :])

    def pack(get, row):
        for i in range(4):
            t = get(2 * i) + get(2 * i + 1)
            z5[pl.ds(row + i, 1), 0:128] = t[0:1] + t[1:2]
            z5[pl.ds(row + i, 1), 128:256] = t[2:3] + t[3:4]

    for copy in own[:2]:
        copy.wait()
    ab4[0, 6:14, 6:10, :] = halve(
        jnp.stack([af[0, 4 + 2 * i] + af[0, 5 + 2 * i] for i in range(8)]), 0
    )
    ab4[1, 6:14, 6:10, :] = halve(
        jnp.stack([bo[5 + 2 * i] + bo[6 + 2 * i] for i in range(8)]), 0
    )
    pl.semaphore_wait(hello.at[0], 4)
    greet(1, ((0, -2), (0, 2), (-2, 0), (2, 0)))
    def inside(start, shape, axis, count):
        at = lax.broadcasted_iota(jnp.int32, shape, axis) + start
        return (at >= 0) & (at < count)

    def row_in(r, size, origin):
        at = size * g + r - origin
        return jnp.where((at >= 0) & (at < size * NG), 1.0, 0.0).astype(F32)

    lanes3 = lax.broadcasted_iota(jnp.int32, (16, 256), 1)
    smooth_middle, smooth_pairs = coefficients(SMOOTH, SMOOTH_LOW)

    def scaled_residual(t, fd, x, r):
        here = x[r]
        n, m = here.shape
        total = fd[r] - here
        total = total + t[0, r] * x[r + 1] + t[1, r] * x[r - 1]
        total = total + t[2, r] * pltpu.roll(here, n - 1, 0) + t[3, r] * pltpu.roll(here, 1, 0)
        return total + t[4, r] * pltpu.roll(here, m - 1, 1) + t[5, r] * pltpu.roll(here, 1, 1)

    def first(r, carry):
        here = row_in(r, N0, 4)
        bc = bo[r + 1] * here
        be = bo[r + 2] * row_in(r + 1, N0, 4)
        bw = bo[r] * row_in(r - 1, N0, 4)
        bn, bs = pltpu.roll(bc, 7, 0), pltpu.roll(bc, 1, 0)
        bu = jnp.where(lanes3[0:8] == 255, 0.0, pltpu.roll(bc, 255, 1))
        bd = jnp.where(lanes3[0:8] == 0, 0.0, pltpu.roll(bc, 1, 1))
        c = [0.5 * (bc + v) for v in (be, bw, bn, bs, bu, bd)]
        inv = here / (af[0, r] + c[0] + c[1] + c[2] + c[3] + c[4] + c[5])
        for n in range(4):
            to[n, r] = c[n] * inv
        to[4, r] = jnp.where(lanes3[0:8] == 255, 0.0, c[4] * inv)
        to[5, r] = jnp.where(lanes3[0:8] == 0, 0.0, c[5] * inv)
        fd = af[1, r] * inv
        fdo[r] = fd
        xo[0, r] = fd * (1.0 / smooth_middle)
        return carry

    def second(r, carry):
        here = xo[0, r]
        total = scaled_residual(to, fdo, xo.at[0], r)
        xo[1, r] = here + smooth_pairs[0][0] * here + smooth_pairs[0][1] * total
        return carry

    own[2].wait()
    for copy in along:
        copy.wait_recv()
    lax.fori_loop(0, 24, first, 0, unroll=6)
    lax.fori_loop(1, 23, second, 0, unroll=11)
    for r in (0, 23):
        xo[1, r] = jnp.zeros_like(xo[1, r])
    x12 = []
    for k, (db, src_at, dst_at) in enumerate(((1, 5, 1), (-1, 2, 6))):
        x12.append(
            remote(
                xo.at[:, :, pl.ds(src_at, 1), :], xr.at[:, :, pl.ds(dst_at, 1), :],
                s_x12.at[k], r_x12.at[k], device(0, db),
            )
        )
    started += x12

    for n in range(2):
        pack(lambda r, n=n: ab4[n, 6 + r, 6:10, :], 4 * n)
    packed = 0.125 * dot(z5[...], gather)
    for n in range(2):
        for i in range(4):
            g5ab[n, MID, i, pl.ds(sub, 1), :] = packed[4 * n + i : 4 * n + i + 1]
    pl.semaphore_wait(hello.at[1], 4)
    abb = []
    for k, db in enumerate([s * d for d in range(MID, 0, -1) for s in (-1, 1)]):
        abb.append(
            remote(
                g5ab.at[:, MID, :, pl.ds(sub, 1), :],
                g5ab.at[:, MID - db, :, pl.ds(sub, 1), :],
                s_abb.at[k], r_abb.at[k], device(0, db),
            )
        )
    started += abb

    def boxes4(ref, send, recv):
        copies = []
        for k, db in enumerate((-2, 2, -1, 1)):
            copies.append(
                halo(inner2(ref, 6, 6), window2(ref), 0, db, 6, 6, 6, 6, (8, 4), send.at[k], recv.at[k])
            )
        return copies

    def groups4(ref, send, recv):
        copies = []
        for k, dg in enumerate((-1, 1)):
            s0, t0, l0 = part(dg, 8, 6, 6)
            copies.append(
                remote(
                    ref.at[:, pl.ds(6 + s0, l0)], ref.at[:, pl.ds(t0, l0)],
                    send.at[4 + k], recv.at[4 + k], device(dg, 0),
                )
            )
        return copies

    ab4_boxes = boxes4(ab4, s_ab4, r_ab4)
    started += ab4_boxes

    x4a[...] = jnp.zeros_like(x4a)
    x5a[...] = jnp.zeros_like(x5a)
    x5b[...] = jnp.zeros_like(x5b)

    def place(r, carry):
        b3[r, 8:16, :] = bo[r]
        return carry

    def place2(r, carry):
        a3[r, 4:12, :] = af[0, r]
        f3[r, 4:12, :] = af[1, r]
        return carry

    lax.fori_loop(0, 26, place, 0, unroll=13)
    lax.fori_loop(0, 24, place2, 0, unroll=8)
    for copy in p1[:12]:
        copy.wait_recv()

    m3c = inside(N1 * b - 4, (16, 256), 0, N1 * NB)
    m3n = inside(N1 * b - 3, (16, 256), 0, N1 * NB)
    m3s = inside(N1 * b - 5, (16, 256), 0, N1 * NB)

    def table3(r, carry):
        here = row_in(r, N0, 4)
        bc = jnp.where(m3c, b3[r + 1, pl.ds(4, 16), :], 0.0) * here
        be = jnp.where(m3c, b3[r + 2, pl.ds(4, 16), :], 0.0) * row_in(r + 1, N0, 4)
        bw = jnp.where(m3c, b3[r, pl.ds(4, 16), :], 0.0) * row_in(r - 1, N0, 4)
        bn = jnp.where(m3n, b3[r + 1, pl.ds(5, 16), :], 0.0) * here
        bs = jnp.where(m3s, b3[r + 1, pl.ds(3, 16), :], 0.0) * here
        bu = jnp.where(lanes3 == 255, 0.0, pltpu.roll(bc, 255, 1))
        bd = jnp.where(lanes3 == 0, 0.0, pltpu.roll(bc, 1, 1))
        c = [0.5 * (bc + v) for v in (be, bw, bn, bs, bu, bd)]
        diag = a3[r] + c[0] + c[1] + c[2] + c[3] + c[4] + c[5]
        inv = jnp.where(m3c, 1.0 / diag, 0.0) * here
        for n in range(4):
            t3[n, r] = c[n] * inv
        t3[4, r] = jnp.where(lanes3 == 255, 0.0, c[4] * inv)
        t3[5, r] = jnp.where(lanes3 == 0, 0.0, c[5] * inv)
        d3[r] = diag
        fd3[r] = inv
        return carry

    def start3(r, carry):
        fd = f3[r] * fd3[r]
        fd3[r] = fd
        x3b[r] = fd * (1.0 / smooth_middle)
        x3a[r] = jnp.zeros_like(fd)
        return carry

    lax.fori_loop(0, 24, table3, 0, unroll=4)
    for copy in p1[12:]:
        copy.wait_recv()
    lax.fori_loop(0, 24, start3, 0, unroll=8)
    below = jnp.where(b > 0, 1.0, 0.0).astype(F32)
    above = jnp.where(b < NB - 1, 1.0, 0.0).astype(F32)

    def given(ref, n):
        def rows(r, carry):
            ref[r, 1:2, :] = xr[n, r, 1:2, :] * below
            ref[r, 14:15, :] = xr[n, r, 6:7, :] * above
            return carry

        lax.fori_loop(0, 24, rows, 0, unroll=8)

    for copy in x12:
        copy.wait_recv()
    given(x3b, 0)

    def sweep(t, fd, now, old, lo, hi, chunk, pair):
        def rows(k, carry):
            for i in range(chunk):
                r = lo + k * chunk + i
                total = scaled_residual(t, fd, now, r)
                here = now[r]
                if len(pair) == 1:
                    old[r] = here + pair[0] * total
                else:
                    old[r] = here + pair[0] * (here - old[r]) + pair[1] * total
            return carry

        lax.fori_loop(0, (hi - lo) // chunk, rows, 0)

    sweep(t3, fd3, x3b, x3a, 1, 23, 11, smooth_pairs[0])
    given(x3a, 1)
    sweep(t3, fd3, x3a, x3b, 2, 22, 10, smooth_pairs[1])
    sweep(t3, fd3, x3b, x3a, 3, 21, 9, smooth_pairs[2])

    def fine_residual(i):
        return d3[i] * scaled_residual(t3, fd3, x3a, i)

    for i in range(8):
        w3[i] = fine_residual(4 + 2 * i) + fine_residual(5 + 2 * i)
    f4[6:14, 6:10, :] = halve(w3[...], 4)
    f4_copies = []
    for k, (dg, db) in enumerate(FACES):
        f4_copies.append(
            halo(inner(f4, 6, 6), window(f4), dg, db, 4, 4, 6, 6, (8, 4), s_f4.at[k], r_f4.at[k])
        )
    started += f4_copies
    for i in range(16):
        h3[4 + i, 4:12, :] = x3a[4 + i, 4:12, :]
    x3_copies = []
    for copy in ab4_boxes:
        copy.wait_recv()
    ab4_groups = groups4(ab4, s_ab4, r_ab4)
    started += ab4_groups
    for k, db in enumerate((-1, 1)):
        x3_copies.append(
            halo(inner(h3, 4, 4), window(h3), 0, db, 4, 4, 4, 4, (N0, N1), s_x3.at[k], r_x3.at[k])
        )
    started += x3_copies
    late = []
    for k, (db, b_at, b_to, a_at, a_to) in enumerate(((1, 4, 4, 5, 1), (-1, 3, 3, 2, 6))):
        late.append(
            remote(
                bo.at[:, pl.ds(b_at, 1), :], lb.at[:, pl.ds(b_to, 1), :],
                s_late.at[0, k], r_late.at[0, k], device(0, db),
            )
        )
        late.append(
            remote(
                af.at[:, :, pl.ds(a_at, 1), :], lz.at[:, :, pl.ds(a_to, 1), :],
                s_late.at[1, k], r_late.at[1, k], device(0, db),
            )
        )
    started += late

    for copy in abb:
        copy.wait_recv()
    aba = []
    for k, dg in enumerate((2, 4, 6)):
        aba.append(
            remote(
                g5ab.at[:, :, :, pl.ds(sub, 1), :], g5ab.at[:, :, :, pl.ds(sub, 1), :],
                s_aba.at[k], r_aba.at[k], device(dg, 0),
            )
        )
    started += aba

    for copy in ab4_groups:
        copy.wait_recv()
    lanes4 = lax.broadcasted_iota(jnp.int32, (16, 128), 1)
    m4 = inside(4 * b - 6, (16, 128), 0, 4 * NB)

    def masked4(r):
        return jnp.where(m4, ab4[1, r], 0.0) * row_in(r, 8, 6)

    def table4(r, carry):
        bc = masked4(r)
        be, bw = masked4(r + 1), masked4(r - 1)
        bn, bs = pltpu.roll(bc, 15, 0), pltpu.roll(bc, 1, 0)
        bu = jnp.where(lanes4 == 127, 0.0, pltpu.roll(bc, 127, 1))
        bd = jnp.where(lanes4 == 0, 0.0, pltpu.roll(bc, 1, 1))
        c = [0.125 * (bc + v) for v in (be, bw, bn, bs, bu, bd)]
        diag = ab4[0, r] + c[0] + c[1] + c[2] + c[3] + c[4] + c[5]
        inv = jnp.where(m4, 1.0 / diag, 0.0) * row_in(r, 8, 6)
        for n in range(4):
            t4[n, r] = c[n] * inv
        t4[4, r] = jnp.where(lanes4 == 127, 0.0, c[4] * inv)
        t4[5, r] = jnp.where(lanes4 == 0, 0.0, c[5] * inv)
        d4[r] = diag
        inv4[r] = inv
        return carry

    lax.fori_loop(1, 19, table4, 0, unroll=6)

    mine = pl.ds(pl.multiple_of(4 * core, 4), 4)
    partner = (g + 1 - 2 * core, b)

    for copy in f4_copies:
        copy.wait_recv()
    for r in range(2, 18):
        fd = f4[r] * inv4[r]
        fd4[r] = fd
        x4b[r] = fd * (1.0 / smooth_middle)
    sweep(t4, fd4, x4b, x4a, 3, 17, 14, smooth_pairs[0])
    sweep(t4, fd4, x4a, x4b, 4, 16, 12, smooth_pairs[1])
    sweep(t4, fd4, x4b, x4a, 5, 15, 10, smooth_pairs[2])

    for r in range(8):
        w4[r] = d4[6 + r] * scaled_residual(t4, fd4, x4a, 6 + r)
    pack(lambda r: w4[r, 6:10, :], 0)
    packed = 0.125 * dot(z5[...], gather)
    for i in range(4):
        g5f[MID, i, pl.ds(sub, 1), :] = packed[i : i + 1]
    fa = []
    for k, dg in enumerate((2, 4, 6)):
        fa.append(
            remote(
                g5f.at[MID, :, pl.ds(sub, 1), :], g5f.at[MID, :, pl.ds(sub, 1), :],
                s_fa.at[k], r_fa.at[k], device(dg, 0),
            )
        )
    started += fa

    for copy in aba:
        copy.wait_recv()
    abc = remote(
        g5ab.at[:, :, :, mine, :], g5ab.at[:, :, :, mine, :], s_abc.at[0], r_abc.at[0], partner
    )
    started.append(abc)

    for copy in x3_copies:
        copy.wait_recv()
    x3_groups = []
    for k, dg in enumerate((-1, 1)):
        s0, t0, l0 = part(dg, N0, 4, 4)
        x3_groups.append(
            remote(
                h3.at[pl.ds(4 + s0, l0)], h3.at[pl.ds(t0, l0)],
                s_x3.at[2 + k], r_x3.at[2 + k], device(dg, 0),
            )
        )
    started += x3_groups

    p4[0, 6:14, 6:10, :] = f4[6:14, 6:10, :]
    p4[1, 6:14, 6:10, :] = x4a[6:14, 6:10, :]
    for copy in fa:
        copy.wait_recv()
    fb = []
    fb_from = [s * d for d in range(REACH, 0, -1) for s in (-1, 1)]
    for k, db in enumerate(fb_from):
        fb.append(
            remote(
                g5f.at[MID, :, mine, :], g5f.at[MID - db, :, mine, :],
                s_fb.at[k], r_fb.at[k], device(0, db),
            )
        )
    started += fb
    p4_boxes = boxes4(p4, s_p4, r_p4)
    started += p4_boxes

    abc.wait_recv()
    lanes5 = lax.broadcasted_iota(jnp.int32, (8, 128), 1)
    subs5 = lax.broadcasted_iota(jnp.int32, (8, 128), 0)
    low = lanes5 < 64
    front = subs5 < 4
    up_end = (lanes5 == 63) | (lanes5 == 127)
    down_end = (lanes5 == 0) | (lanes5 == 64)

    def next_group(v):
        return jnp.where(front, pltpu.roll(v, 4, 0), pltpu.roll(v, 3, 0))

    def last_group(v):
        return jnp.where(front, pltpu.roll(v, 5, 0), pltpu.roll(v, 4, 0))

    def box_in(k):
        at = b + k - MID
        return jnp.where((at >= 0) & (at < NB), 1.0, 0.0).astype(F32)

    def beta5(k, i):
        return g5ab[1, k, i] * box_in(k)

    def table5(k, carry):
        bc = [beta5(k, i) for i in range(4)]
        half = [pltpu.roll(v, 64, 1) for v in bc]
        after = [pltpu.roll(beta5(k + 1, i), 64, 1) for i in range(4)]
        before = [pltpu.roll(beta5(k - 1, i), 64, 1) for i in range(4)]
        for i in range(4):
            be = bc[i + 1] if i < 3 else jnp.where(subs5 == 7, 0.0, next_group(bc[0]))
            bw = bc[i - 1] if i > 0 else jnp.where(subs5 == 0, 0.0, last_group(bc[3]))
            bn = jnp.where(low, half[i], after[i])
            bs = jnp.where(low, before[i], half[i])
            bu = jnp.where(up_end, 0.0, pltpu.roll(bc[i], 127, 1))
            bd = jnp.where(down_end, 0.0, pltpu.roll(bc[i], 1, 1))
            c = [0.03125 * (bc[i] + v) for v in (be, bw, bn, bs, bu, bd)]
            diag = g5ab[0, k, i] + c[0] + c[1] + c[2] + c[3] + c[4] + c[5]
            inv = box_in(k) / diag
            t5[0, k, i] = c[0] * inv if i < 3 else jnp.where(subs5 == 7, 0.0, c[0] * inv)
            t5[1, k, i] = c[1] * inv if i > 0 else jnp.where(subs5 == 0, 0.0, c[1] * inv)
            t5[2, k, i] = c[2] * inv
            t5[3, k, i] = c[3] * inv
            t5[4, k, i] = jnp.where(up_end, 0.0, c[4] * inv)
            t5[5, k, i] = jnp.where(down_end, 0.0, c[5] * inv)
            inv5[k, i] = inv
        return carry

    lax.fori_loop(1, SPAN - 1, table5, 0)

    for copy in late:
        copy.wait_recv()

    def widen(r, carry):
        b3[r, 4:5, :] = lb[r, 4:5, :]
        b3[r, 19:20, :] = lb[r, 3:4, :]
        return carry

    def widen2(r, carry):
        a3[r, 1:2, :] = lz[0, r, 1:2, :]
        a3[r, 14:15, :] = lz[0, r, 6:7, :]
        f3[r, 1:2, :] = lz[1, r, 1:2, :]
        f3[r, 14:15, :] = lz[1, r, 6:7, :]
        return carry

    def restart3(r, carry):
        fd3[r] = f3[r] * fd3[r]
        return carry

    lax.fori_loop(0, 26, widen, 0, unroll=13)
    lax.fori_loop(0, 24, widen2, 0, unroll=8)
    lax.fori_loop(0, 24, table3, 0, unroll=4)
    lax.fori_loop(0, 24, restart3, 0, unroll=8)
    for copy in started:
        copy.wait_send()
    started = []

    fc = []
    for k, (first, last) in enumerate(((MID - 3, MID + 3), (1, MID - 4), (MID + 4, SPAN - 2))):
        for copy, db in zip(fb, fb_from):
            if first <= MID - db <= last:
                copy.wait_recv()
        span = pl.ds(first, last - first + 1)
        fc.append(
            remote(g5f.at[span, :, mine, :], g5f.at[span, :, mine, :], s_fc.at[k], r_fc.at[k], partner)
        )
    started += fc
    for copy in p4_boxes:
        copy.wait_recv()
    p4_groups = groups4(p4, s_p4, r_p4)
    started += p4_groups

    bottom_middle, bottom_pairs = coefficients(BOTTOM, BOTTOM_LOW)
    for m, (c1, c2) in enumerate(bottom_pairs):
        ends[m, 0] = F32(c1)
        ends[m, 1] = F32(c2)
    for copy in fc:
        copy.wait_recv()
    for k in range(1, SPAN - 1):
        for i in range(4):
            fd = g5f[k, i] * inv5[k, i]
            fd5[k, i] = fd
            x5b[k, i] = fd * (1.0 / bottom_middle)

    def sweep5(now, old, reach, c1, c2):
        lo, hi = MID - reach, MID + reach + 1
        half = {}

        def turned(k, i):
            if (k, i) not in half:
                half[k, i] = pltpu.roll(now[k, i], 64, 1)
            return half[k, i]

        for k in range(lo, hi):
            x = [now[k, i] for i in range(4)]
            for i in range(4):
                east = x[i + 1] if i < 3 else next_group(x[0])
                west = x[i - 1] if i > 0 else last_group(x[3])
                north = jnp.where(low, turned(k, i), turned(k + 1, i))
                south = jnp.where(low, turned(k - 1, i), turned(k, i))
                total = fd5[k, i] - x[i]
                total = total + t5[0, k, i] * east + t5[1, k, i] * west
                total = total + t5[2, k, i] * north + t5[3, k, i] * south
                total = total + t5[4, k, i] * pltpu.roll(x[i], 127, 1) + t5[5, k, i] * pltpu.roll(x[i], 1, 1)
                old[k, i] = x[i] + c1 * (x[i] - old[k, i]) + c2 * total

    def two(reach, first):
        def body(k, carry):
            m = first + 2 * k
            sweep5(x5b, x5a, reach, ends[m, 0], ends[m, 1])
            sweep5(x5a, x5b, reach - 1, ends[m + 1, 0], ends[m + 1, 1])
            return carry

        return body

    lax.fori_loop(0, 2, two(9, 0), 0)
    lax.fori_loop(0, 2, two(7, 4), 0)
    lax.fori_loop(0, 2, two(5, 8), 0)
    two(3, 12)(0, 0)
    sweep5(x5b, x5a, 2, ends[14, 0], ends[14, 1])

    for a in range(10):
        row = a - 3
        group = lax.rem(g + (row // 4) + NG, NG)
        at = 4 * lax.rem(group, 2) + group // 2
        for k in range(5):
            line = x5a[MID - 2 + k, row % 4, pl.ds(at, 1), :]
            first, last = max(4 * k - 2, 0), min(4 * k + 2, 16)
            q4[a, first:last, :] = jnp.broadcast_to(line, (last - first, 128))
    grown = dot(q4[...].reshape(160, 128), spread).reshape(10, 16, 256)
    rows4 = lax.broadcasted_iota(jnp.int32, (16, 128), 0)
    first_of_box = lax.rem(lax.shift_right_logical(rows4 + 2, 1), 2) == 0
    for copy in p4_groups:
        copy.wait_recv()
    for a in range(10):
        line = jnp.where(first_of_box, grown[a, :, 0:128], grown[a, :, 128:256])
        for r in (2 * a, 2 * a + 1):
            x4b[r] = jnp.where(m4, p4[1, r] + line, 0.0) * row_in(r, 8, 6)
            if 1 <= r < 19:
                fd4[r] = p4[0, r] * inv4[r]
    sweep(t4, fd4, x4b, x4a, 1, 19, 18, (1.0 / smooth_middle,))
    sweep(t4, fd4, x4a, x4b, 2, 18, 16, smooth_pairs[0])
    sweep(t4, fd4, x4b, x4a, 3, 17, 14, smooth_pairs[1])
    sweep(t4, fd4, x4a, x4b, 4, 16, 12, smooth_pairs[2])

    grown = dot(x4b[4:16, 4:12, :].reshape(96, 128), spread).reshape(12, 8, 256)
    for r in range(12):
        for k in range(2):
            line = grown[r, :, 128 * k : 128 * k + 128]
            u4[k, r, pl.ds(0, 8, stride=2), :] = line
            u4[k, r, pl.ds(1, 8, stride=2), :] = line
    for copy in x3_groups:
        copy.wait_recv()
    for r in range(24):
        row = row_in(r, N0, 4)
        for k in range(2):
            lanes = slice(128 * k, 128 * k + 128)
            x3b[r, :, lanes] = jnp.where(m3c[:, lanes], (h3[r, :, lanes] + u4[k, r // 2]) * row, 0.0)
    sweep(t3, fd3, x3b, x3a, 1, 23, 11, (1.0 / smooth_middle,))
    sweep(t3, fd3, x3a, x3b, 2, 22, 10, smooth_pairs[0])
    sweep(t3, fd3, x3b, x3a, 3, 21, 9, smooth_pairs[1])
    for copy in started:
        copy.wait_send()

    def last(k, carry):
        for i in range(8):
            r = 4 + 8 * k + i
            total = scaled_residual(t3, fd3, x3a, r)
            here = x3a[r]
            line = here + smooth_pairs[2][0] * (here - x3b[r]) + smooth_pairs[2][1] * total
            out[r - 4] = line[4:12]
        return carry

    lax.fori_loop(0, 2, last, 0)


SCRATCH = (
    [pltpu.VMEM(shape, F32) for shape in (
        (26, 8, 256), (2, 24, 8, 256), (6, 24, 8, 256), (24, 8, 256), (2, 24, 8, 256), (2, 24, 8, 256),
        (26, 8, 256), (2, 24, 8, 256),
        (24, 16, 256), (24, 16, 256), (26, 24, 256), (6, 24, 16, 256), (24, 16, 256), (24, 16, 256),
        (24, 16, 256), (24, 16, 256), (24, 16, 256),
        (2, 20, 16, 128), (20, 16, 128), (2, 20, 16, 128), (6, 20, 16, 128), (20, 16, 128), (20, 16, 128),
        (20, 16, 128), (20, 16, 128), (20, 16, 128), (8, 16, 128),
        (8, 256), (2, SPAN, 4, 8, 128), (SPAN, 4, 8, 128), (6, SPAN, 4, 8, 128), (SPAN, 4, 8, 128),
        (SPAN, 4, 8, 128), (SPAN, 4, 8, 128), (SPAN, 4, 8, 128), (10, 16, 128), (8, 16, 256),
        (2, 12, 16, 128),
    )]
    + [pltpu.SemaphoreType.DMA((3,)), pltpu.SemaphoreType.REGULAR((2,)), pltpu.SMEM((16, 2), F32)]
    + [pltpu.SemaphoreType.DMA(shape) for count in (
        (3, 8), (2,), (2, 2), (6,), (8,), (4,), (6,), (3,), (2 * MID,), (1,), (3,), (2 * REACH,), (3,)
    ) for shape in (count, count)]
)


def cycle(source, alpha, beta):
    return pl.pallas_call(
        kernel,
        out_shape=pltpu.VMEM((N0, N1, N2), F32),
        in_specs=[pl.BlockSpec(memory_space=pl.ANY)] * 3,
        out_specs=pl.BlockSpec(memory_space=pltpu.VMEM),
        scratch_shapes=SCRATCH,
        compiler_params=pltpu.CompilerParams(
            collective_id=0, has_side_effects=True, vmem_limit_bytes=63 << 20
        ),
        name="vcycle",
    )(source, alpha, beta)


def solution(mesh):
    spec = P("grp", "box", None)
    return jax.shard_map(cycle, mesh=mesh, in_specs=(spec,) * 3, out_specs=spec, check_vma=False)
```

```python
import jax
import jax.numpy as jnp
from jax import lax
from jax.experimental import pallas as pl
from jax.experimental.pallas import tpu as pltpu
from jax.sharding import PartitionSpec as P

SMOOTH = 4
BOTTOM = 16
SMOOTH_LOW = 0.25
BOTTOM_LOW = 0.02
UPPER_BOUND = 2.0

MESH = pl.DeviceIdType.MESH
F32 = jnp.float32
NG, NB = 8, 32
N0, N1, N2 = 16, 8, 256
REACH = 9
MID = REACH + 1
SPAN = 2 * MID + 1

FACES = [(dg, db) for db in (-1, 1, 0) for dg in (0, -1, 1) if (dg, db) != (0, 0)]


def coefficients(degree, lower):
    middle = (UPPER_BOUND + lower) / 2.0
    spread = (UPPER_BOUND - lower) / 2.0
    base = middle / spread
    now = 1.0 / base
    pairs = []
    for _ in range(degree - 1):
        after = 1.0 / (2.0 * base - now)
        pairs.append((after * now, 2.0 * after / spread))
        now = after
    return middle, pairs


def part(step, size, width, origin):
    if step == 0:
        return 0, origin, size
    if step == 2:
        return size - (width - size), origin - width, width - size
    if step == -2:
        return 0, origin + 2 * size, width - size
    width = min(width, size)
    if step == 1:
        return size - width, origin - width, width
    return 0, origin + size, width


def kernel(
    source, alpha, beta, out,
    bo, af, to, fdo, xo, xr, lb, lz, f3, a3, b3, t3, d3, fd3, x3a, x3b, h3,
    ab4, f4, p4, t4, inv4, d4, fd4, x4a, x4b, w4,
    z5, g5ab, g5f, t5, inv5, fd5, x5a, x5b, q4, w3, u4,
    own_sem, hello, ends,
    s_p1, r_p1, s_x12, r_x12, s_late, r_late, s_ab4, r_ab4, s_f4, r_f4, s_x3, r_x3, s_p4, r_p4,
    s_aba, r_aba, s_abb, r_abb, s_abc, r_abc, s_fa, r_fa, s_fb, r_fb, s_fc, r_fc,
):
    g, b = lax.axis_index("grp"), lax.axis_index("box")
    core, chip = lax.rem(g, 2), g // 2
    sub = 4 * core + chip

    def device(dg, db):
        return (lax.rem(g + dg + NG, NG), lax.rem(b + db + NB, NB))

    def remote(src, dst, send, recv, target):
        copy = pltpu.make_async_remote_copy(
            src_ref=src, dst_ref=dst, send_sem=send, recv_sem=recv, device_id=target, device_id_type=MESH
        )
        copy.start()
        return copy

    started = []

    own = [
        pltpu.make_async_copy(beta, bo.at[pl.ds(5, N0)], own_sem.at[0]),
        pltpu.make_async_copy(alpha, af.at[0, pl.ds(4, N0)], own_sem.at[1]),
        pltpu.make_async_copy(source, af.at[1, pl.ds(4, N0)], own_sem.at[2]),
    ]
    for copy in own:
        copy.start()

    partners = FACES + [(0, -8), (0, 8)]
    barrier = pltpu.get_barrier_semaphore()
    for dg, db in partners:
        pl.semaphore_signal(barrier, inc=1, device_id=device(dg, db), device_id_type=MESH)

    f4[...] = jnp.zeros_like(f4)
    pl.semaphore_wait(barrier, len(partners))

    def halo(src, dst, dg, db, w0, w1, o0, o1, size, send, recv):
        s0, t0, l0 = part(dg, size[0], w0, o0)
        s1, t1, l1 = part(db, size[1], w1, o1)
        return remote(
            src(s0, l0, s1, l1), dst(t0, l0, t1, l1), send, recv, device(dg, db)
        )

    def window(ref):
        return lambda i, n, j, m: ref.at[pl.ds(i, n), pl.ds(j, m), :]

    def window2(ref):
        return lambda i, n, j, m: ref.at[:, pl.ds(i, n), pl.ds(j, m), :]

    def inner(ref, o0, o1):
        return lambda i, n, j, m: ref.at[pl.ds(o0 + i, n), pl.ds(o1 + j, m), :]

    def inner2(ref, o0, o1):
        return lambda i, n, j, m: ref.at[:, pl.ds(o0 + i, n), pl.ds(o1 + j, m), :]

    along = []
    for n, (src, dst, w, o0) in enumerate(
        ((beta, bo, 5, 5), (alpha, af.at[0], 4, 4), (source, af.at[1], 4, 4))
    ):
        for k, dg in enumerate((-1, 1)):
            s0, t0, l0 = part(dg, N0, w, o0)
            along.append(
                remote(src.at[pl.ds(s0, l0)], dst.at[pl.ds(t0, l0)], s_p1.at[n, k], r_p1.at[n, k], device(dg, 0))
            )
    started += along
    p1 = []
    for n, (src, dst, w0, w1, o0, o1) in enumerate(
        ((beta, b3, 5, 3, 5, 8), (alpha, a3, 4, 2, 4, 4), (source, f3, 4, 2, 4, 4))
    ):
        for k, (dg, db) in enumerate(FACES[:6]):
            p1.append(
                halo(
                    window(src), window(dst), dg, db, w0, w1, o0, o1, (N0, N1),
                    s_p1.at[n, 2 + k], r_p1.at[n, 2 + k],
                )
            )
    started += p1

    def greet(n, peers):
        for dg, db in peers:
            pl.semaphore_signal(hello.at[n], inc=1, device_id=device(dg, db), device_id_type=MESH)

    greet(0, ((0, -1), (0, 1), (-1, 0), (1, 0)))

    rows256 = lax.broadcasted_iota(jnp.int32, (256, 128), 0)
    cols128 = lax.broadcasted_iota(jnp.int32, (256, 128), 1)
    gather = jnp.where(lax.shift_right_logical(rows256, 1) == cols128, 1.0, 0.0).astype(F32)
    rows128 = lax.broadcasted_iota(jnp.int32, (128, 256), 0)
    cols256 = lax.broadcasted_iota(jnp.int32, (128, 256), 1)
    spread = jnp.where(lax.shift_right_logical(cols256, 1) == rows128, 1.0, 0.0).astype(F32)

    def dot(x, matrix):
        return jnp.dot(x, matrix, precision=lax.Precision.HIGHEST, preferred_element_type=F32)

    def halve(pairs, o1):
        n = pairs.shape[1]
        w4[:, 0:n, :] = dot(pairs.reshape(8 * n, 256), gather).reshape(8, n, 128)
        return 0.125 * (w4[:, pl.ds(o1, 4, stride=2), :] + w4[:, pl.ds(o1 + 1, 4, stride=2), :])

    def pack(get, row):
        for i in range(4):
            t = get(2 * i) + get(2 * i + 1)
            z5[pl.ds(row + i, 1), 0:128] = t[0:1] + t[1:2]
            z5[pl.ds(row + i, 1), 128:256] = t[2:3] + t[3:4]

    for copy in own[:2]:
        copy.wait()
    ab4[0, 6:14, 6:10, :] = halve(
        jnp.stack([af[0, 4 + 2 * i] + af[0, 5 + 2 * i] for i in range(8)]), 0
    )
    ab4[1, 6:14, 6:10, :] = halve(
        jnp.stack([bo[5 + 2 * i] + bo[6 + 2 * i] for i in range(8)]), 0
    )
    pl.semaphore_wait(hello.at[0], 4)
    greet(1, ((0, -2), (0, 2), (-2, 0), (2, 0)))
    def inside(start, shape, axis, count):
        at = lax.broadcasted_iota(jnp.int32, shape, axis) + start
        return (at >= 0) & (at < count)

    def row_in(r, size, origin):
        at = size * g + r - origin
        return jnp.where((at >= 0) & (at < size * NG), 1.0, 0.0).astype(F32)

    lanes3 = lax.broadcasted_iota(jnp.int32, (16, 256), 1)
    smooth_middle, smooth_pairs = coefficients(SMOOTH, SMOOTH_LOW)

    def scaled_residual(t, fd, x, r):
        here = x[r]
        n, m = here.shape
        total = fd[r] - here
        total = total + t[0, r] * x[r + 1] + t[1, r] * x[r - 1]
        total = total + t[2, r] * pltpu.roll(here, n - 1, 0) + t[3, r] * pltpu.roll(here, 1, 0)
        return total + t[4, r] * pltpu.roll(here, m - 1, 1) + t[5, r] * pltpu.roll(here, 1, 1)

    def first(r, carry):
        here = row_in(r, N0, 4)
        bc = bo[r + 1] * here
        be = bo[r + 2] * row_in(r + 1, N0, 4)
        bw = bo[r] * row_in(r - 1, N0, 4)
        bn, bs = pltpu.roll(bc, 7, 0), pltpu.roll(bc, 1, 0)
        bu = jnp.where(lanes3[0:8] == 255, 0.0, pltpu.roll(bc, 255, 1))
        bd = jnp.where(lanes3[0:8] == 0, 0.0, pltpu.roll(bc, 1, 1))
        c = [0.5 * (bc + v) for v in (be, bw, bn, bs, bu, bd)]
        inv = here / (af[0, r] + c[0] + c[1] + c[2] + c[3] + c[4] + c[5])
        for n in range(4):
            to[n, r] = c[n] * inv
        to[4, r] = jnp.where(lanes3[0:8] == 255, 0.0, c[4] * inv)
        to[5, r] = jnp.where(lanes3[0:8] == 0, 0.0, c[5] * inv)
        fd = af[1, r] * inv
        fdo[r] = fd
        xo[0, r] = fd * (1.0 / smooth_middle)
        return carry

    def second(r, carry):
        here = xo[0, r]
        total = scaled_residual(to, fdo, xo.at[0], r)
        xo[1, r] = here + smooth_pairs[0][0] * here + smooth_pairs[0][1] * total
        return carry

    own[2].wait()
    for copy in along:
        copy.wait_recv()
    lax.fori_loop(0, 24, first, 0, unroll=6)
    lax.fori_loop(1, 23, second, 0, unroll=11)
    for r in (0, 23):
        xo[1, r] = jnp.zeros_like(xo[1, r])
    x12 = []
    for k, (db, src_at, dst_at) in enumerate(((1, 5, 1), (-1, 2, 6))):
        x12.append(
            remote(
                xo.at[:, :, pl.ds(src_at, 1), :], xr.at[:, :, pl.ds(dst_at, 1), :],
                s_x12.at[k], r_x12.at[k], device(0, db),
            )
        )
    started += x12

    def boxes4(ref, send, recv):
        copies = []
        for k, db in enumerate((-2, 2, -1, 1)):
            copies.append(
                halo(inner2(ref, 6, 6), window2(ref), 0, db, 6, 6, 6, 6, (8, 4), send.at[k], recv.at[k])
            )
        return copies

    def groups4(ref, send, recv):
        copies = []
        for k, dg in enumerate((-1, 1)):
            s0, t0, l0 = part(dg, 8, 6, 6)
            copies.append(
                remote(
                    ref.at[:, pl.ds(6 + s0, l0)], ref.at[:, pl.ds(t0, l0)],
                    send.at[4 + k], recv.at[4 + k], device(dg, 0),
                )
            )
        return copies

    ab4_boxes = boxes4(ab4, s_ab4, r_ab4)
    started += ab4_boxes
    for n in range(2):
        pack(lambda r, n=n: ab4[n, 6 + r, 6:10, :], 4 * n)
    packed = 0.125 * dot(z5[...], gather)
    for n in range(2):
        for i in range(4):
            g5ab[n, MID, i, pl.ds(sub, 1), :] = packed[4 * n + i : 4 * n + i + 1]
    pl.semaphore_wait(hello.at[1], 4)
    abb = []
    for k, db in enumerate([s * d for d in range(MID, 0, -1) for s in (-1, 1)]):
        abb.append(
            remote(
                g5ab.at[:, MID, :, pl.ds(sub, 1), :],
                g5ab.at[:, MID - db, :, pl.ds(sub, 1), :],
                s_abb.at[k], r_abb.at[k], device(0, db),
            )
        )
    started += abb


    x4a[...] = jnp.zeros_like(x4a)
    x5a[...] = jnp.zeros_like(x5a)
    x5b[...] = jnp.zeros_like(x5b)

    def place(r, carry):
        b3[r, 8:16, :] = bo[r]
        return carry

    def place2(r, carry):
        a3[r, 4:12, :] = af[0, r]
        f3[r, 4:12, :] = af[1, r]
        return carry

    lax.fori_loop(0, 26, place, 0, unroll=13)
    lax.fori_loop(0, 24, place2, 0, unroll=8)
    for copy in p1[:12]:
        copy.wait_recv()

    m3c = inside(N1 * b - 4, (16, 256), 0, N1 * NB)
    m3n = inside(N1 * b - 3, (16, 256), 0, N1 * NB)
    m3s = inside(N1 * b - 5, (16, 256), 0, N1 * NB)

    def table3(r, carry):
        here = row_in(r, N0, 4)
        bc = jnp.where(m3c, b3[r + 1, pl.ds(4, 16), :], 0.0) * here
        be = jnp.where(m3c, b3[r + 2, pl.ds(4, 16), :], 0.0) * row_in(r + 1, N0, 4)
        bw = jnp.where(m3c, b3[r, pl.ds(4, 16), :], 0.0) * row_in(r - 1, N0, 4)
        bn = jnp.where(m3n, b3[r + 1, pl.ds(5, 16), :], 0.0) * here
        bs = jnp.where(m3s, b3[r + 1, pl.ds(3, 16), :], 0.0) * here
        bu = jnp.where(lanes3 == 255, 0.0, pltpu.roll(bc, 255, 1))
        bd = jnp.where(lanes3 == 0, 0.0, pltpu.roll(bc, 1, 1))
        c = [0.5 * (bc + v) for v in (be, bw, bn, bs, bu, bd)]
        diag = a3[r] + c[0] + c[1] + c[2] + c[3] + c[4] + c[5]
        inv = jnp.where(m3c, 1.0 / diag, 0.0) * here
        for n in range(4):
            t3[n, r] = c[n] * inv
        t3[4, r] = jnp.where(lanes3 == 255, 0.0, c[4] * inv)
        t3[5, r] = jnp.where(lanes3 == 0, 0.0, c[5] * inv)
        d3[r] = diag
        fd3[r] = inv
        return carry

    def start3(r, carry):
        fd = f3[r] * fd3[r]
        fd3[r] = fd
        x3b[r] = fd * (1.0 / smooth_middle)
        x3a[r] = jnp.zeros_like(fd)
        return carry

    lax.fori_loop(0, 24, table3, 0, unroll=4)
    for copy in p1[12:]:
        copy.wait_recv()
    lax.fori_loop(0, 24, start3, 0, unroll=8)
    below = jnp.where(b > 0, 1.0, 0.0).astype(F32)
    above = jnp.where(b < NB - 1, 1.0, 0.0).astype(F32)

    def given(ref, n):
        def rows(r, carry):
            ref[r, 1:2, :] = xr[n, r, 1:2, :] * below
            ref[r, 14:15, :] = xr[n, r, 6:7, :] * above
            return carry

        lax.fori_loop(0, 24, rows, 0, unroll=8)

    for copy in x12:
        copy.wait_recv()
    given(x3b, 0)

    def sweep(t, fd, now, old, lo, hi, chunk, pair):
        def rows(k, carry):
            for i in range(chunk):
                r = lo + k * chunk + i
                total = scaled_residual(t, fd, now, r)
                here = now[r]
                if len(pair) == 1:
                    old[r] = here + pair[0] * total
                else:
                    old[r] = here + pair[0] * (here - old[r]) + pair[1] * total
            return carry

        lax.fori_loop(0, (hi - lo) // chunk, rows, 0)

    sweep(t3, fd3, x3b, x3a, 1, 23, 11, smooth_pairs[0])
    given(x3a, 1)
    sweep(t3, fd3, x3a, x3b, 2, 22, 10, smooth_pairs[1])
    sweep(t3, fd3, x3b, x3a, 3, 21, 9, smooth_pairs[2])

    def fine_residual(i):
        return d3[i] * scaled_residual(t3, fd3, x3a, i)

    for i in range(8):
        w3[i] = fine_residual(4 + 2 * i) + fine_residual(5 + 2 * i)
    f4[6:14, 6:10, :] = halve(w3[...], 4)
    f4_copies = []
    for k, (dg, db) in enumerate(FACES):
        f4_copies.append(
            halo(inner(f4, 6, 6), window(f4), dg, db, 4, 4, 6, 6, (8, 4), s_f4.at[k], r_f4.at[k])
        )
    started += f4_copies
    for i in range(16):
        h3[4 + i, 4:12, :] = x3a[4 + i, 4:12, :]
    x3_copies = []
    for copy in ab4_boxes:
        copy.wait_recv()
    ab4_groups = groups4(ab4, s_ab4, r_ab4)
    started += ab4_groups
    for k, db in enumerate((-1, 1)):
        x3_copies.append(
            halo(inner(h3, 4, 4), window(h3), 0, db, 4, 4, 4, 4, (N0, N1), s_x3.at[k], r_x3.at[k])
        )
    started += x3_copies
    late = []
    for k, (db, b_at, b_to, a_at, a_to) in enumerate(((1, 4, 4, 5, 1), (-1, 3, 3, 2, 6))):
        late.append(
            remote(
                bo.at[:, pl.ds(b_at, 1), :], lb.at[:, pl.ds(b_to, 1), :],
                s_late.at[0, k], r_late.at[0, k], device(0, db),
            )
        )
        late.append(
            remote(
                af.at[:, :, pl.ds(a_at, 1), :], lz.at[:, :, pl.ds(a_to, 1), :],
                s_late.at[1, k], r_late.at[1, k], device(0, db),
            )
        )
    started += late

    for copy in abb:
        copy.wait_recv()
    aba = []
    for k, dg in enumerate((2, -2)):
        aba.append(
            remote(
                g5ab.at[:, :, :, pl.ds(sub, 1), :], g5ab.at[:, :, :, pl.ds(sub, 1), :],
                s_aba.at[k], r_aba.at[k], device(dg, 0),
            )
        )
    started += aba

    for copy in ab4_groups:
        copy.wait_recv()
    lanes4 = lax.broadcasted_iota(jnp.int32, (16, 128), 1)
    m4 = inside(4 * b - 6, (16, 128), 0, 4 * NB)

    def masked4(r):
        return jnp.where(m4, ab4[1, r], 0.0) * row_in(r, 8, 6)

    def table4(r, carry):
        bc = masked4(r)
        be, bw = masked4(r + 1), masked4(r - 1)
        bn, bs = pltpu.roll(bc, 15, 0), pltpu.roll(bc, 1, 0)
        bu = jnp.where(lanes4 == 127, 0.0, pltpu.roll(bc, 127, 1))
        bd = jnp.where(lanes4 == 0, 0.0, pltpu.roll(bc, 1, 1))
        c = [0.125 * (bc + v) for v in (be, bw, bn, bs, bu, bd)]
        diag = ab4[0, r] + c[0] + c[1] + c[2] + c[3] + c[4] + c[5]
        inv = jnp.where(m4, 1.0 / diag, 0.0) * row_in(r, 8, 6)
        for n in range(4):
            t4[n, r] = c[n] * inv
        t4[4, r] = jnp.where(lanes4 == 127, 0.0, c[4] * inv)
        t4[5, r] = jnp.where(lanes4 == 0, 0.0, c[5] * inv)
        d4[r] = diag
        inv4[r] = inv
        return carry

    lax.fori_loop(1, 19, table4, 0, unroll=6)

    mine = pl.ds(pl.multiple_of(4 * core, 4), 4)
    partner = (g + 1 - 2 * core, b)

    for copy in f4_copies:
        copy.wait_recv()
    for r in range(2, 18):
        fd = f4[r] * inv4[r]
        fd4[r] = fd
        x4b[r] = fd * (1.0 / smooth_middle)
    sweep(t4, fd4, x4b, x4a, 3, 17, 14, smooth_pairs[0])
    sweep(t4, fd4, x4a, x4b, 4, 16, 12, smooth_pairs[1])
    sweep(t4, fd4, x4b, x4a, 5, 15, 10, smooth_pairs[2])

    for r in range(8):
        w4[r] = d4[6 + r] * scaled_residual(t4, fd4, x4a, 6 + r)
    pack(lambda r: w4[r, 6:10, :], 0)
    packed = 0.125 * dot(z5[...], gather)
    for i in range(4):
        g5f[MID, i, pl.ds(sub, 1), :] = packed[i : i + 1]
    fa = []
    for k, dg in enumerate((2, 4, 6)):
        fa.append(
            remote(
                g5f.at[MID, :, pl.ds(sub, 1), :], g5f.at[MID, :, pl.ds(sub, 1), :],
                s_fa.at[k], r_fa.at[k], device(dg, 0),
            )
        )
    started += fa

    forward = []
    for k, (dg, first, size) in enumerate(((2, 0, MID + 1), (-2, MID + 1, MID))):
        aba[k].wait_recv()
        other = 4 * core + lax.rem(chip + (3, 1)[k], 4)
        block = g5ab.at[:, pl.ds(first, size), :, pl.ds(other, 1), :]
        forward.append(remote(block, block, s_aba.at[2 + k], r_aba.at[2 + k], device(dg, 0)))
    started += forward

    for copy in x3_copies:
        copy.wait_recv()
    x3_groups = []
    for k, dg in enumerate((-1, 1)):
        s0, t0, l0 = part(dg, N0, 4, 4)
        x3_groups.append(
            remote(
                h3.at[pl.ds(4 + s0, l0)], h3.at[pl.ds(t0, l0)],
                s_x3.at[2 + k], r_x3.at[2 + k], device(dg, 0),
            )
        )
    started += x3_groups

    p4[0, 6:14, 6:10, :] = f4[6:14, 6:10, :]
    p4[1, 6:14, 6:10, :] = x4a[6:14, 6:10, :]
    for copy in fa:
        copy.wait_recv()
    fb = []
    fb_from = [s * d for d in range(REACH, 0, -1) for s in (-1, 1)]
    for k, db in enumerate(fb_from):
        fb.append(
            remote(
                g5f.at[MID, :, mine, :], g5f.at[MID - db, :, mine, :],
                s_fb.at[k], r_fb.at[k], device(0, db),
            )
        )
    started += fb
    p4_boxes = boxes4(p4, s_p4, r_p4)
    started += p4_boxes

    for copy in forward:
        copy.wait_recv()
    abc = remote(
        g5ab.at[:, :, :, mine, :], g5ab.at[:, :, :, mine, :], s_abc.at[0], r_abc.at[0], partner
    )
    started.append(abc)

    abc.wait_recv()
    lanes5 = lax.broadcasted_iota(jnp.int32, (8, 128), 1)
    subs5 = lax.broadcasted_iota(jnp.int32, (8, 128), 0)
    low = lanes5 < 64
    front = subs5 < 4
    up_end = (lanes5 == 63) | (lanes5 == 127)
    down_end = (lanes5 == 0) | (lanes5 == 64)

    def next_group(v):
        return jnp.where(front, pltpu.roll(v, 4, 0), pltpu.roll(v, 3, 0))

    def last_group(v):
        return jnp.where(front, pltpu.roll(v, 5, 0), pltpu.roll(v, 4, 0))

    def box_in(k):
        at = b + k - MID
        return jnp.where((at >= 0) & (at < NB), 1.0, 0.0).astype(F32)

    def beta5(k, i):
        return g5ab[1, k, i] * box_in(k)

    def table5(k, carry):
        bc = [beta5(k, i) for i in range(4)]
        half = [pltpu.roll(v, 64, 1) for v in bc]
        after = [pltpu.roll(beta5(k + 1, i), 64, 1) for i in range(4)]
        before = [pltpu.roll(beta5(k - 1, i), 64, 1) for i in range(4)]
        for i in range(4):
            be = bc[i + 1] if i < 3 else jnp.where(subs5 == 7, 0.0, next_group(bc[0]))
            bw = bc[i - 1] if i > 0 else jnp.where(subs5 == 0, 0.0, last_group(bc[3]))
            bn = jnp.where(low, half[i], after[i])
            bs = jnp.where(low, before[i], half[i])
            bu = jnp.where(up_end, 0.0, pltpu.roll(bc[i], 127, 1))
            bd = jnp.where(down_end, 0.0, pltpu.roll(bc[i], 1, 1))
            c = [0.03125 * (bc[i] + v) for v in (be, bw, bn, bs, bu, bd)]
            diag = g5ab[0, k, i] + c[0] + c[1] + c[2] + c[3] + c[4] + c[5]
            inv = box_in(k) / diag
            t5[0, k, i] = c[0] * inv if i < 3 else jnp.where(subs5 == 7, 0.0, c[0] * inv)
            t5[1, k, i] = c[1] * inv if i > 0 else jnp.where(subs5 == 0, 0.0, c[1] * inv)
            t5[2, k, i] = c[2] * inv
            t5[3, k, i] = c[3] * inv
            t5[4, k, i] = jnp.where(up_end, 0.0, c[4] * inv)
            t5[5, k, i] = jnp.where(down_end, 0.0, c[5] * inv)
            inv5[k, i] = inv
        return carry

    lax.fori_loop(1, SPAN - 1, table5, 0)

    for copy in late:
        copy.wait_recv()

    def widen(r, carry):
        b3[r, 4:5, :] = lb[r, 4:5, :]
        b3[r, 19:20, :] = lb[r, 3:4, :]
        return carry

    def widen2(r, carry):
        a3[r, 1:2, :] = lz[0, r, 1:2, :]
        a3[r, 14:15, :] = lz[0, r, 6:7, :]
        f3[r, 1:2, :] = lz[1, r, 1:2, :]
        f3[r, 14:15, :] = lz[1, r, 6:7, :]
        return carry

    def restart3(r, carry):
        fd3[r] = f3[r] * fd3[r]
        return carry

    lax.fori_loop(0, 26, widen, 0, unroll=13)
    lax.fori_loop(0, 24, widen2, 0, unroll=8)
    lax.fori_loop(0, 24, table3, 0, unroll=4)
    lax.fori_loop(0, 24, restart3, 0, unroll=8)
    for copy in started:
        copy.wait_send()
    started = []

    fc = []
    for k, (first, last) in enumerate(((MID - 3, MID + 3), (1, MID - 4), (MID + 4, SPAN - 2))):
        for copy, db in zip(fb, fb_from):
            if first <= MID - db <= last:
                copy.wait_recv()
        span = pl.ds(first, last - first + 1)
        fc.append(
            remote(g5f.at[span, :, mine, :], g5f.at[span, :, mine, :], s_fc.at[k], r_fc.at[k], partner)
        )
    started += fc
    for copy in p4_boxes:
        copy.wait_recv()
    p4_groups = groups4(p4, s_p4, r_p4)
    started += p4_groups

    bottom_middle, bottom_pairs = coefficients(BOTTOM, BOTTOM_LOW)
    for m, (c1, c2) in enumerate(bottom_pairs):
        ends[m, 0] = F32(c1)
        ends[m, 1] = F32(c2)
    for copy in fc:
        copy.wait_recv()
    for k in range(1, SPAN - 1):
        for i in range(4):
            fd = g5f[k, i] * inv5[k, i]
            fd5[k, i] = fd
            x5b[k, i] = fd * (1.0 / bottom_middle)

    def sweep5(now, old, reach, c1, c2):
        lo, hi = MID - reach, MID + reach + 1
        half = {}

        def turned(k, i):
            if (k, i) not in half:
                half[k, i] = pltpu.roll(now[k, i], 64, 1)
            return half[k, i]

        for k in range(lo, hi):
            x = [now[k, i] for i in range(4)]
            for i in range(4):
                east = x[i + 1] if i < 3 else next_group(x[0])
                west = x[i - 1] if i > 0 else last_group(x[3])
                north = jnp.where(low, turned(k, i), turned(k + 1, i))
                south = jnp.where(low, turned(k - 1, i), turned(k, i))
                total = fd5[k, i] - x[i]
                total = total + t5[0, k, i] * east + t5[1, k, i] * west
                total = total + t5[2, k, i] * north + t5[3, k, i] * south
                total = total + t5[4, k, i] * pltpu.roll(x[i], 127, 1) + t5[5, k, i] * pltpu.roll(x[i], 1, 1)
                old[k, i] = x[i] + c1 * (x[i] - old[k, i]) + c2 * total

    def two(reach, first):
        def body(k, carry):
            m = first + 2 * k
            sweep5(x5b, x5a, reach, ends[m, 0], ends[m, 1])
            sweep5(x5a, x5b, reach - 1, ends[m + 1, 0], ends[m + 1, 1])
            return carry

        return body

    lax.fori_loop(0, 2, two(9, 0), 0)
    lax.fori_loop(0, 2, two(7, 4), 0)
    lax.fori_loop(0, 2, two(5, 8), 0)
    two(3, 12)(0, 0)
    sweep5(x5b, x5a, 2, ends[14, 0], ends[14, 1])

    for a in range(10):
        row = a - 3
        group = lax.rem(g + (row // 4) + NG, NG)
        at = 4 * lax.rem(group, 2) + group // 2
        for k in range(5):
            line = x5a[MID - 2 + k, row % 4, pl.ds(at, 1), :]
            first, last = max(4 * k - 2, 0), min(4 * k + 2, 16)
            q4[a, first:last, :] = jnp.broadcast_to(line, (last - first, 128))
    grown = dot(q4[...].reshape(160, 128), spread).reshape(10, 16, 256)
    rows4 = lax.broadcasted_iota(jnp.int32, (16, 128), 0)
    first_of_box = lax.rem(lax.shift_right_logical(rows4 + 2, 1), 2) == 0
    for copy in p4_groups:
        copy.wait_recv()
    for a in range(10):
        line = jnp.where(first_of_box, grown[a, :, 0:128], grown[a, :, 128:256])
        for r in (2 * a, 2 * a + 1):
            x4b[r] = jnp.where(m4, p4[1, r] + line, 0.0) * row_in(r, 8, 6)
            if 1 <= r < 19:
                fd4[r] = p4[0, r] * inv4[r]
    sweep(t4, fd4, x4b, x4a, 1, 19, 18, (1.0 / smooth_middle,))
    sweep(t4, fd4, x4a, x4b, 2, 18, 16, smooth_pairs[0])
    sweep(t4, fd4, x4b, x4a, 3, 17, 14, smooth_pairs[1])
    sweep(t4, fd4, x4a, x4b, 4, 16, 12, smooth_pairs[2])

    grown = dot(x4b[4:16, 4:12, :].reshape(96, 128), spread).reshape(12, 8, 256)
    for r in range(12):
        for k in range(2):
            line = grown[r, :, 128 * k : 128 * k + 128]
            u4[k, r, pl.ds(0, 8, stride=2), :] = line
            u4[k, r, pl.ds(1, 8, stride=2), :] = line
    for copy in x3_groups:
        copy.wait_recv()
    for r in range(24):
        row = row_in(r, N0, 4)
        for k in range(2):
            lanes = slice(128 * k, 128 * k + 128)
            x3b[r, :, lanes] = jnp.where(m3c[:, lanes], (h3[r, :, lanes] + u4[k, r // 2]) * row, 0.0)
    sweep(t3, fd3, x3b, x3a, 1, 23, 11, (1.0 / smooth_middle,))
    sweep(t3, fd3, x3a, x3b, 2, 22, 10, smooth_pairs[0])
    sweep(t3, fd3, x3b, x3a, 3, 21, 9, smooth_pairs[1])
    for copy in started:
        copy.wait_send()

    def last(k, carry):
        for i in range(8):
            r = 4 + 8 * k + i
            total = scaled_residual(t3, fd3, x3a, r)
            here = x3a[r]
            line = here + smooth_pairs[2][0] * (here - x3b[r]) + smooth_pairs[2][1] * total
            out[r - 4] = line[4:12]
        return carry

    lax.fori_loop(0, 2, last, 0)


SCRATCH = (
    [pltpu.VMEM(shape, F32) for shape in (
        (26, 8, 256), (2, 24, 8, 256), (6, 24, 8, 256), (24, 8, 256), (2, 24, 8, 256), (2, 24, 8, 256),
        (26, 8, 256), (2, 24, 8, 256),
        (24, 16, 256), (24, 16, 256), (26, 24, 256), (6, 24, 16, 256), (24, 16, 256), (24, 16, 256),
        (24, 16, 256), (24, 16, 256), (24, 16, 256),
        (2, 20, 16, 128), (20, 16, 128), (2, 20, 16, 128), (6, 20, 16, 128), (20, 16, 128), (20, 16, 128),
        (20, 16, 128), (20, 16, 128), (20, 16, 128), (8, 16, 128),
        (8, 256), (2, SPAN, 4, 8, 128), (SPAN, 4, 8, 128), (6, SPAN, 4, 8, 128), (SPAN, 4, 8, 128),
        (SPAN, 4, 8, 128), (SPAN, 4, 8, 128), (SPAN, 4, 8, 128), (10, 16, 128), (8, 16, 256),
        (2, 12, 16, 128),
    )]
    + [pltpu.SemaphoreType.DMA((3,)), pltpu.SemaphoreType.REGULAR((2,)), pltpu.SMEM((16, 2), F32)]
    + [pltpu.SemaphoreType.DMA(shape) for count in (
        (3, 8), (2,), (2, 2), (6,), (8,), (4,), (6,), (4,), (2 * MID,), (1,), (3,), (2 * REACH,), (3,)
    ) for shape in (count, count)]
)


def cycle(source, alpha, beta):
    return pl.pallas_call(
        kernel,
        out_shape=pltpu.VMEM((N0, N1, N2), F32),
        in_specs=[pl.BlockSpec(memory_space=pl.ANY)] * 3,
        out_specs=pl.BlockSpec(memory_space=pltpu.VMEM),
        scratch_shapes=SCRATCH,
        compiler_params=pltpu.CompilerParams(
            collective_id=0, has_side_effects=True, vmem_limit_bytes=63 << 20
        ),
        name="vcycle",
    )(source, alpha, beta)


def solution(mesh):
    spec = P("grp", "box", None)
    return jax.shard_map(cycle, mesh=mesh, in_specs=(spec,) * 3, out_specs=spec, check_vma=False)
```

```python
import jax
import jax.numpy as jnp
from jax import lax
from jax.experimental import pallas as pl
from jax.experimental.pallas import tpu as pltpu
from jax.sharding import PartitionSpec as P

SMOOTH = 4
BOTTOM = 16
SMOOTH_LOW = 0.25
BOTTOM_LOW = 0.02
UPPER_BOUND = 2.0

MESH = pl.DeviceIdType.MESH
F32 = jnp.float32
NG, NB = 8, 32
N0, N1, N2 = 16, 8, 256
REACH = 9
MID = REACH + 1
SPAN = 2 * MID + 1

FACES = [(dg, db) for db in (-1, 1, 0) for dg in (0, -1, 1) if (dg, db) != (0, 0)]


def coefficients(degree, lower):
    middle = (UPPER_BOUND + lower) / 2.0
    spread = (UPPER_BOUND - lower) / 2.0
    base = middle / spread
    now = 1.0 / base
    pairs = []
    for _ in range(degree - 1):
        after = 1.0 / (2.0 * base - now)
        pairs.append((after * now, 2.0 * after / spread))
        now = after
    return middle, pairs


def part(step, size, width, origin):
    if step == 0:
        return 0, origin, size
    if step == 2:
        return size - (width - size), origin - width, width - size
    if step == -2:
        return 0, origin + 2 * size, width - size
    width = min(width, size)
    if step == 1:
        return size - width, origin - width, width
    return 0, origin + size, width


def kernel(
    source, alpha, beta, out,
    bo, af, to, fdo, xo, xr, lb, lz, f3, a3, b3, t3, d3, fd3, x3a, x3b, h3,
    ab4, f4, p4, t4, inv4, d4, fd4, x4a, x4b, w4,
    z5, g5ab, g5f, m5, c5, t5, inv5, fd5, x5a, x5b, q4, w3, u4,
    own_sem, hello, ends,
    s_p1, r_p1, s_x12, r_x12, s_late, r_late, s_ab4, r_ab4, s_f4, r_f4, s_x3, r_x3, s_p4, r_p4,
    s_aba, r_aba, s_abb, r_abb, s_abc, r_abc, s_fa, r_fa, s_fb, r_fb, s_fc, r_fc,
):
    g, b = lax.axis_index("grp"), lax.axis_index("box")
    core, chip = lax.rem(g, 2), g // 2
    sub = 4 * core + chip

    def device(dg, db):
        return (lax.rem(g + dg + NG, NG), lax.rem(b + db + NB, NB))

    def remote(src, dst, send, recv, target):
        copy = pltpu.make_async_remote_copy(
            src_ref=src, dst_ref=dst, send_sem=send, recv_sem=recv, device_id=target, device_id_type=MESH
        )
        copy.start()
        return copy

    started = []

    own = [
        pltpu.make_async_copy(beta, bo.at[pl.ds(5, N0)], own_sem.at[0]),
        pltpu.make_async_copy(alpha, af.at[0, pl.ds(4, N0)], own_sem.at[1]),
        pltpu.make_async_copy(source, af.at[1, pl.ds(4, N0)], own_sem.at[2]),
    ]
    for copy in own:
        copy.start()

    partners = FACES + [(0, -8), (0, 8)]
    barrier = pltpu.get_barrier_semaphore()
    for dg, db in partners:
        pl.semaphore_signal(barrier, inc=1, device_id=device(dg, db), device_id_type=MESH)

    f4[...] = jnp.zeros_like(f4)
    pl.semaphore_wait(barrier, len(partners))

    def halo(src, dst, dg, db, w0, w1, o0, o1, size, send, recv):
        s0, t0, l0 = part(dg, size[0], w0, o0)
        s1, t1, l1 = part(db, size[1], w1, o1)
        return remote(
            src(s0, l0, s1, l1), dst(t0, l0, t1, l1), send, recv, device(dg, db)
        )

    def window(ref):
        return lambda i, n, j, m: ref.at[pl.ds(i, n), pl.ds(j, m), :]

    def window2(ref):
        return lambda i, n, j, m: ref.at[:, pl.ds(i, n), pl.ds(j, m), :]

    def inner(ref, o0, o1):
        return lambda i, n, j, m: ref.at[pl.ds(o0 + i, n), pl.ds(o1 + j, m), :]

    def inner2(ref, o0, o1):
        return lambda i, n, j, m: ref.at[:, pl.ds(o0 + i, n), pl.ds(o1 + j, m), :]

    along = []
    for n, (src, dst, w, o0) in enumerate(
        ((beta, bo, 5, 5), (alpha, af.at[0], 4, 4), (source, af.at[1], 4, 4))
    ):
        for k, dg in enumerate((-1, 1)):
            s0, t0, l0 = part(dg, N0, w, o0)
            along.append(
                remote(src.at[pl.ds(s0, l0)], dst.at[pl.ds(t0, l0)], s_p1.at[n, k], r_p1.at[n, k], device(dg, 0))
            )
    started += along
    p1 = []
    for n, (src, dst, w0, w1, o0, o1) in enumerate(
        ((beta, b3, 5, 3, 5, 8), (alpha, a3, 4, 2, 4, 4), (source, f3, 4, 2, 4, 4))
    ):
        for k, (dg, db) in enumerate(FACES[:6]):
            p1.append(
                halo(
                    window(src), window(dst), dg, db, w0, w1, o0, o1, (N0, N1),
                    s_p1.at[n, 2 + k], r_p1.at[n, 2 + k],
                )
            )
    started += p1

    def greet(n, peers):
        for dg, db in peers:
            pl.semaphore_signal(hello.at[n], inc=1, device_id=device(dg, db), device_id_type=MESH)

    greet(0, ((0, -1), (0, 1), (-1, 0), (1, 0)))

    rows256 = lax.broadcasted_iota(jnp.int32, (256, 128), 0)
    cols128 = lax.broadcasted_iota(jnp.int32, (256, 128), 1)
    gather = jnp.where(lax.shift_right_logical(rows256, 1) == cols128, 1.0, 0.0).astype(F32)
    rows128 = lax.broadcasted_iota(jnp.int32, (128, 256), 0)
    cols256 = lax.broadcasted_iota(jnp.int32, (128, 256), 1)
    spread = jnp.where(lax.shift_right_logical(cols256, 1) == rows128, 1.0, 0.0).astype(F32)

    def dot(x, matrix):
        return jnp.dot(x, matrix, precision=lax.Precision.HIGHEST, preferred_element_type=F32)

    def halve(pairs, o1):
        n = pairs.shape[1]
        w4[:, 0:n, :] = dot(pairs.reshape(8 * n, 256), gather).reshape(8, n, 128)
        return 0.125 * (w4[:, pl.ds(o1, 4, stride=2), :] + w4[:, pl.ds(o1 + 1, 4, stride=2), :])

    def pack(get, row):
        for i in range(4):
            t = get(2 * i) + get(2 * i + 1)
            z5[pl.ds(row + i, 1), 0:128] = t[0:1] + t[1:2]
            z5[pl.ds(row + i, 1), 128:256] = t[2:3] + t[3:4]

    for copy in own[:2]:
        copy.wait()
    ab4[0, 6:14, 6:10, :] = halve(
        jnp.stack([af[0, 4 + 2 * i] + af[0, 5 + 2 * i] for i in range(8)]), 0
    )
    ab4[1, 6:14, 6:10, :] = halve(
        jnp.stack([bo[5 + 2 * i] + bo[6 + 2 * i] for i in range(8)]), 0
    )
    pl.semaphore_wait(hello.at[0], 4)
    greet(1, ((0, -2), (0, 2), (-2, 0), (2, 0)))
    def inside(start, shape, axis, count):
        at = lax.broadcasted_iota(jnp.int32, shape, axis) + start
        return (at >= 0) & (at < count)

    def row_in(r, size, origin):
        at = size * g + r - origin
        return jnp.where((at >= 0) & (at < size * NG), 1.0, 0.0).astype(F32)

    lanes3 = lax.broadcasted_iota(jnp.int32, (16, 256), 1)
    smooth_middle, smooth_pairs = coefficients(SMOOTH, SMOOTH_LOW)

    def scaled_residual(t, fd, x, r):
        here = x[r]
        n, m = here.shape
        total = fd[r] - here
        total = total + t[0, r] * x[r + 1] + t[1, r] * x[r - 1]
        total = total + t[2, r] * pltpu.roll(here, n - 1, 0) + t[3, r] * pltpu.roll(here, 1, 0)
        return total + t[4, r] * pltpu.roll(here, m - 1, 1) + t[5, r] * pltpu.roll(here, 1, 1)

    def first(r, carry):
        here = row_in(r, N0, 4)
        bc = bo[r + 1] * here
        be = bo[r + 2] * row_in(r + 1, N0, 4)
        bw = bo[r] * row_in(r - 1, N0, 4)
        bn, bs = pltpu.roll(bc, 7, 0), pltpu.roll(bc, 1, 0)
        bu = jnp.where(lanes3[0:8] == 255, 0.0, pltpu.roll(bc, 255, 1))
        bd = jnp.where(lanes3[0:8] == 0, 0.0, pltpu.roll(bc, 1, 1))
        c = [0.5 * (bc + v) for v in (be, bw, bn, bs, bu, bd)]
        inv = here / (af[0, r] + c[0] + c[1] + c[2] + c[3] + c[4] + c[5])
        for n in range(4):
            to[n, r] = c[n] * inv
        to[4, r] = jnp.where(lanes3[0:8] == 255, 0.0, c[4] * inv)
        to[5, r] = jnp.where(lanes3[0:8] == 0, 0.0, c[5] * inv)
        fd = af[1, r] * inv
        fdo[r] = fd
        xo[0, r] = fd * (1.0 / smooth_middle)
        return carry

    def second(r, carry):
        here = xo[0, r]
        total = scaled_residual(to, fdo, xo.at[0], r)
        xo[1, r] = here + smooth_pairs[0][0] * here + smooth_pairs[0][1] * total
        return carry

    own[2].wait()
    for copy in along:
        copy.wait_recv()
    lax.fori_loop(0, 24, first, 0, unroll=6)
    lax.fori_loop(1, 23, second, 0, unroll=11)
    for r in (0, 23):
        xo[1, r] = jnp.zeros_like(xo[1, r])
    x12 = []
    for k, (db, src_at, dst_at) in enumerate(((1, 5, 1), (-1, 2, 6))):
        x12.append(
            remote(
                xo.at[:, :, pl.ds(src_at, 1), :], xr.at[:, :, pl.ds(dst_at, 1), :],
                s_x12.at[k], r_x12.at[k], device(0, db),
            )
        )
    started += x12

    def boxes4(ref, send, recv):
        copies = []
        for k, db in enumerate((-2, 2, -1, 1)):
            copies.append(
                halo(inner2(ref, 6, 6), window2(ref), 0, db, 6, 6, 6, 6, (8, 4), send.at[k], recv.at[k])
            )
        return copies

    def groups4(ref, send, recv):
        copies = []
        for k, dg in enumerate((-1, 1)):
            s0, t0, l0 = part(dg, 8, 6, 6)
            copies.append(
                remote(
                    ref.at[:, pl.ds(6 + s0, l0)], ref.at[:, pl.ds(t0, l0)],
                    send.at[4 + k], recv.at[4 + k], device(dg, 0),
                )
            )
        return copies

    ab4_boxes = boxes4(ab4, s_ab4, r_ab4)
    started += ab4_boxes
    for n in range(2):
        pack(lambda r, n=n: ab4[n, 6 + r, 6:10, :], 4 * n)
    packed = 0.125 * dot(z5[...], gather)
    for n in range(2):
        for i in range(4):
            g5ab[n, MID, i, pl.ds(sub, 1), :] = packed[4 * n + i : 4 * n + i + 1]
    pl.semaphore_wait(hello.at[1], 4)
    abb = []
    for k, db in enumerate([s * d for d in range(MID, 0, -1) for s in (-1, 1)]):
        abb.append(
            remote(
                g5ab.at[:, MID, :, pl.ds(sub, 1), :],
                g5ab.at[:, MID - db, :, pl.ds(sub, 1), :],
                s_abb.at[k], r_abb.at[k], device(0, db),
            )
        )
    started += abb


    x4a[...] = jnp.zeros_like(x4a)
    x5a[...] = jnp.zeros_like(x5a)
    x5b[...] = jnp.zeros_like(x5b)

    def place(r, carry):
        b3[r, 8:16, :] = bo[r]
        return carry

    def place2(r, carry):
        a3[r, 4:12, :] = af[0, r]
        f3[r, 4:12, :] = af[1, r]
        return carry

    lax.fori_loop(0, 26, place, 0, unroll=13)
    lax.fori_loop(0, 24, place2, 0, unroll=8)
    for copy in p1[:12]:
        copy.wait_recv()

    m3c = inside(N1 * b - 4, (16, 256), 0, N1 * NB)
    m3n = inside(N1 * b - 3, (16, 256), 0, N1 * NB)
    m3s = inside(N1 * b - 5, (16, 256), 0, N1 * NB)

    def table3(r, carry):
        here = row_in(r, N0, 4)
        bc = jnp.where(m3c, b3[r + 1, pl.ds(4, 16), :], 0.0) * here
        be = jnp.where(m3c, b3[r + 2, pl.ds(4, 16), :], 0.0) * row_in(r + 1, N0, 4)
        bw = jnp.where(m3c, b3[r, pl.ds(4, 16), :], 0.0) * row_in(r - 1, N0, 4)
        bn = jnp.where(m3n, b3[r + 1, pl.ds(5, 16), :], 0.0) * here
        bs = jnp.where(m3s, b3[r + 1, pl.ds(3, 16), :], 0.0) * here
        bu = jnp.where(lanes3 == 255, 0.0, pltpu.roll(bc, 255, 1))
        bd = jnp.where(lanes3 == 0, 0.0, pltpu.roll(bc, 1, 1))
        c = [0.5 * (bc + v) for v in (be, bw, bn, bs, bu, bd)]
        diag = a3[r] + c[0] + c[1] + c[2] + c[3] + c[4] + c[5]
        inv = jnp.where(m3c, 1.0 / diag, 0.0) * here
        for n in range(4):
            t3[n, r] = c[n] * inv
        t3[4, r] = jnp.where(lanes3 == 255, 0.0, c[4] * inv)
        t3[5, r] = jnp.where(lanes3 == 0, 0.0, c[5] * inv)
        d3[r] = diag
        fd3[r] = inv
        return carry

    def start3(r, carry):
        fd = f3[r] * fd3[r]
        fd3[r] = fd
        x3b[r] = fd * (1.0 / smooth_middle)
        x3a[r] = jnp.zeros_like(fd)
        return carry

    lax.fori_loop(0, 24, table3, 0, unroll=4)
    for copy in p1[12:]:
        copy.wait_recv()
    lax.fori_loop(0, 24, start3, 0, unroll=8)
    below = jnp.where(b > 0, 1.0, 0.0).astype(F32)
    above = jnp.where(b < NB - 1, 1.0, 0.0).astype(F32)

    def given(ref, n):
        def rows(r, carry):
            ref[r, 1:2, :] = xr[n, r, 1:2, :] * below
            ref[r, 14:15, :] = xr[n, r, 6:7, :] * above
            return carry

        lax.fori_loop(0, 24, rows, 0, unroll=8)

    for copy in x12:
        copy.wait_recv()
    given(x3b, 0)

    def sweep(t, fd, now, old, lo, hi, chunk, pair):
        def rows(k, carry):
            for i in range(chunk):
                r = lo + k * chunk + i
                total = scaled_residual(t, fd, now, r)
                here = now[r]
                if len(pair) == 1:
                    old[r] = here + pair[0] * total
                else:
                    old[r] = here + pair[0] * (here - old[r]) + pair[1] * total
            return carry

        lax.fori_loop(0, (hi - lo) // chunk, rows, 0)

    sweep(t3, fd3, x3b, x3a, 1, 23, 11, smooth_pairs[0])
    given(x3a, 1)
    sweep(t3, fd3, x3a, x3b, 2, 22, 10, smooth_pairs[1])
    sweep(t3, fd3, x3b, x3a, 3, 21, 9, smooth_pairs[2])

    def fine_residual(i):
        return d3[i] * scaled_residual(t3, fd3, x3a, i)

    for i in range(8):
        w3[i] = fine_residual(4 + 2 * i) + fine_residual(5 + 2 * i)
    f4[6:14, 6:10, :] = halve(w3[...], 4)
    f4_copies = []
    for k, (dg, db) in enumerate(FACES):
        f4_copies.append(
            halo(inner(f4, 6, 6), window(f4), dg, db, 4, 4, 6, 6, (8, 4), s_f4.at[k], r_f4.at[k])
        )
    started += f4_copies
    for i in range(16):
        h3[4 + i, 4:12, :] = x3a[4 + i, 4:12, :]
    x3_copies = []
    for copy in ab4_boxes:
        copy.wait_recv()
    ab4_groups = groups4(ab4, s_ab4, r_ab4)
    started += ab4_groups
    for k, db in enumerate((-1, 1)):
        x3_copies.append(
            halo(inner(h3, 4, 4), window(h3), 0, db, 4, 4, 4, 4, (N0, N1), s_x3.at[k], r_x3.at[k])
        )
    started += x3_copies
    late = []
    for k, (db, b_at, b_to, a_at, a_to) in enumerate(((1, 4, 4, 5, 1), (-1, 3, 3, 2, 6))):
        late.append(
            remote(
                bo.at[:, pl.ds(b_at, 1), :], lb.at[:, pl.ds(b_to, 1), :],
                s_late.at[0, k], r_late.at[0, k], device(0, db),
            )
        )
        late.append(
            remote(
                af.at[:, :, pl.ds(a_at, 1), :], lz.at[:, :, pl.ds(a_to, 1), :],
                s_late.at[1, k], r_late.at[1, k], device(0, db),
            )
        )
    started += late

    for copy in abb:
        copy.wait_recv()
    aba = []
    for k, dg in enumerate((2, -2)):
        aba.append(
            remote(
                g5ab.at[:, :, :, pl.ds(sub, 1), :], g5ab.at[:, :, :, pl.ds(sub, 1), :],
                s_aba.at[k], r_aba.at[k], device(dg, 0),
            )
        )
    started += aba

    for copy in ab4_groups:
        copy.wait_recv()
    lanes4 = lax.broadcasted_iota(jnp.int32, (16, 128), 1)
    m4 = inside(4 * b - 6, (16, 128), 0, 4 * NB)

    def masked4(r):
        return jnp.where(m4, ab4[1, r], 0.0) * row_in(r, 8, 6)

    def table4(r, carry):
        bc = masked4(r)
        be, bw = masked4(r + 1), masked4(r - 1)
        bn, bs = pltpu.roll(bc, 15, 0), pltpu.roll(bc, 1, 0)
        bu = jnp.where(lanes4 == 127, 0.0, pltpu.roll(bc, 127, 1))
        bd = jnp.where(lanes4 == 0, 0.0, pltpu.roll(bc, 1, 1))
        c = [0.125 * (bc + v) for v in (be, bw, bn, bs, bu, bd)]
        diag = ab4[0, r] + c[0] + c[1] + c[2] + c[3] + c[4] + c[5]
        inv = jnp.where(m4, 1.0 / diag, 0.0) * row_in(r, 8, 6)
        for n in range(4):
            t4[n, r] = c[n] * inv
        t4[4, r] = jnp.where(lanes4 == 127, 0.0, c[4] * inv)
        t4[5, r] = jnp.where(lanes4 == 0, 0.0, c[5] * inv)
        d4[r] = diag
        inv4[r] = inv
        return carry

    lax.fori_loop(1, 19, table4, 0, unroll=6)

    mine = pl.ds(pl.multiple_of(4 * core, 4), 4)
    partner = (g + 1 - 2 * core, b)

    for copy in f4_copies:
        copy.wait_recv()
    for r in range(2, 18):
        fd = f4[r] * inv4[r]
        fd4[r] = fd
        x4b[r] = fd * (1.0 / smooth_middle)
    sweep(t4, fd4, x4b, x4a, 3, 17, 14, smooth_pairs[0])
    sweep(t4, fd4, x4a, x4b, 4, 16, 12, smooth_pairs[1])
    sweep(t4, fd4, x4b, x4a, 5, 15, 10, smooth_pairs[2])

    for r in range(8):
        w4[r] = d4[6 + r] * scaled_residual(t4, fd4, x4a, 6 + r)
    pack(lambda r: w4[r, 6:10, :], 0)
    packed = 0.125 * dot(z5[...], gather)
    for i in range(4):
        g5f[MID, i, pl.ds(sub, 1), :] = packed[i : i + 1]
    early = len(started)
    fa = []
    for k, dg in enumerate((2, 4, 6)):
        fa.append(
            remote(
                g5f.at[MID, :, pl.ds(sub, 1), :], g5f.at[MID, :, pl.ds(sub, 1), :],
                s_fa.at[k], r_fa.at[k], device(dg, 0),
            )
        )
    started += fa

    forward = []
    for k, (dg, first, size) in enumerate(((2, 0, MID + 1), (-2, MID + 1, MID))):
        aba[k].wait_recv()
        other = 4 * core + lax.rem(chip + (3, 1)[k], 4)
        block = g5ab.at[:, pl.ds(first, size), :, pl.ds(other, 1), :]
        forward.append(remote(block, block, s_aba.at[2 + k], r_aba.at[2 + k], device(dg, 0)))
    started += forward

    for copy in x3_copies:
        copy.wait_recv()
    x3_groups = []
    for k, dg in enumerate((-1, 1)):
        s0, t0, l0 = part(dg, N0, 4, 4)
        x3_groups.append(
            remote(
                h3.at[pl.ds(4 + s0, l0)], h3.at[pl.ds(t0, l0)],
                s_x3.at[2 + k], r_x3.at[2 + k], device(dg, 0),
            )
        )
    started += x3_groups

    p4[0, 6:14, 6:10, :] = f4[6:14, 6:10, :]
    p4[1, 6:14, 6:10, :] = x4a[6:14, 6:10, :]
    for copy in fa:
        copy.wait_recv()
    fb = []
    fb_from = [s * d for d in range(REACH, 0, -1) for s in (-1, 1)]
    for k, db in enumerate(fb_from):
        fb.append(
            remote(
                g5f.at[MID, :, mine, :], g5f.at[MID - db, :, mine, :],
                s_fb.at[k], r_fb.at[k], device(0, db),
            )
        )
    started += fb
    p4_boxes = boxes4(p4, s_p4, r_p4)
    started += p4_boxes

    for copy in forward:
        copy.wait_recv()
    abc = remote(
        g5ab.at[:, :, :, mine, :], g5ab.at[:, :, :, mine, :], s_abc.at[0], r_abc.at[0], partner
    )
    started.append(abc)

    for copy in late:
        copy.wait_recv()

    def widen(r, carry):
        b3[r, 4:5, :] = lb[r, 4:5, :]
        b3[r, 19:20, :] = lb[r, 3:4, :]
        return carry

    def widen2(r, carry):
        a3[r, 1:2, :] = lz[0, r, 1:2, :]
        a3[r, 14:15, :] = lz[0, r, 6:7, :]
        f3[r, 1:2, :] = lz[1, r, 1:2, :]
        f3[r, 14:15, :] = lz[1, r, 6:7, :]
        return carry

    def restart3(r, carry):
        fd3[r] = f3[r] * fd3[r]
        return carry

    lax.fori_loop(0, 26, widen, 0, unroll=13)
    lax.fori_loop(0, 24, widen2, 0, unroll=8)
    lax.fori_loop(0, 24, table3, 0, unroll=4)
    lax.fori_loop(0, 24, restart3, 0, unroll=8)
    for copy in started[:early]:
        copy.wait_send()
    started = started[early:]

    abc.wait_recv()
    lanes5 = lax.broadcasted_iota(jnp.int32, (8, 128), 1)
    subs5 = lax.broadcasted_iota(jnp.int32, (8, 128), 0)
    low = lanes5 < 64
    front = subs5 < 4
    up_end = (lanes5 == 63) | (lanes5 == 127)
    down_end = (lanes5 == 0) | (lanes5 == 64)

    def next_group(v):
        return jnp.where(front, pltpu.roll(v, 4, 0), pltpu.roll(v, 3, 0))

    def last_group(v):
        return jnp.where(front, pltpu.roll(v, 5, 0), pltpu.roll(v, 4, 0))

    def box_in(k):
        at = b + k - MID
        return jnp.where((at >= 0) & (at < NB), 1.0, 0.0).astype(F32)

    def fold_even(get, t, i):
        return pltpu.roll(jnp.where(low, get(2 * MID - t, i), get(t, i)), 64, 1)

    def fold_odd(get, t, i):
        return jnp.where(low, get(t + 1, i), get(2 * MID - 1 - t, i))

    def fold5(t, carry):
        here = (2 * t, 2 * t + 1)
        m5[here[0]] = jnp.where(low, box_in(t), box_in(2 * MID - t))
        m5[here[1]] = jnp.where(low, box_in(t + 1), box_in(2 * MID - 1 - t))
        for i in range(4):
            for n in range(2):
                def get(k, i, n=n):
                    return g5ab[n, k, i]

                for a, fold in zip(here, (fold_even, fold_odd)):
                    value = fold(get, t, i)
                    c5[n, a, i] = value * m5[a] if n else value
        return carry

    lax.fori_loop(0, MID, fold5, 0)
    for i in range(4):
        c5[1, 2 * MID, i] = pltpu.roll(c5[1, 2 * MID - 1, i], 64, 1)

    def table5(a, carry):
        bc = [c5[1, a, i] for i in range(4)]
        mask = m5[a]
        for i in range(4):
            be = bc[i + 1] if i < 3 else jnp.where(subs5 == 7, 0.0, next_group(bc[0]))
            bw = bc[i - 1] if i > 0 else jnp.where(subs5 == 0, 0.0, last_group(bc[3]))
            bu = jnp.where(up_end, 0.0, pltpu.roll(bc[i], 127, 1))
            bd = jnp.where(down_end, 0.0, pltpu.roll(bc[i], 1, 1))
            c = [0.03125 * (bc[i] + v) for v in (be, bw, c5[1, a + 1, i], c5[1, a - 1, i], bu, bd)]
            inv = mask / (c5[0, a, i] + c[0] + c[1] + c[2] + c[3] + c[4] + c[5])
            t5[0, a, i] = c[0] * inv if i < 3 else jnp.where(subs5 == 7, 0.0, c[0] * inv)
            t5[1, a, i] = c[1] * inv if i > 0 else jnp.where(subs5 == 0, 0.0, c[1] * inv)
            t5[2, a, i] = c[2] * inv
            t5[3, a, i] = c[3] * inv
            t5[4, a, i] = jnp.where(up_end, 0.0, c[4] * inv)
            t5[5, a, i] = jnp.where(down_end, 0.0, c[5] * inv)
            inv5[a, i] = inv
        return carry

    lax.fori_loop(1, 2 * MID, table5, 0)


    fc = []
    for k, (first, last) in enumerate(((MID - 3, MID + 3), (1, MID - 4), (MID + 4, SPAN - 2))):
        for copy, db in zip(fb, fb_from):
            if first <= MID - db <= last:
                copy.wait_recv()
        span = pl.ds(first, last - first + 1)
        fc.append(
            remote(g5f.at[span, :, mine, :], g5f.at[span, :, mine, :], s_fc.at[k], r_fc.at[k], partner)
        )
    started += fc
    for copy in p4_boxes:
        copy.wait_recv()
    p4_groups = groups4(p4, s_p4, r_p4)
    started += p4_groups

    bottom_middle, bottom_pairs = coefficients(BOTTOM, BOTTOM_LOW)
    for m, (c1, c2) in enumerate(bottom_pairs):
        ends[m, 0] = F32(c1)
        ends[m, 1] = F32(c2)
    for copy in fc:
        copy.wait_recv()
    for a in range(1, 2 * MID):
        for i in range(4):
            folded = (fold_odd if a % 2 else fold_even)(lambda k, i: g5f[k, i], a // 2, i)
            fd = folded * inv5[a, i]
            fd5[a, i] = fd
            x5b[a, i] = fd * (1.0 / bottom_middle)

    def sweep5(now, old, first, c1, c2):
        for a in range(first, 2 * MID):
            x = [now[a, i] for i in range(4)]
            for i in range(4):
                east = x[i + 1] if i < 3 else next_group(x[0])
                west = x[i - 1] if i > 0 else last_group(x[3])
                inward = now[a + 1, i] if a < 2 * MID - 1 else pltpu.roll(x[i], 64, 1)
                total = fd5[a, i] - x[i]
                total = total + t5[0, a, i] * east + t5[1, a, i] * west
                total = total + t5[2, a, i] * inward + t5[3, a, i] * now[a - 1, i]
                total = total + t5[4, a, i] * pltpu.roll(x[i], 127, 1) + t5[5, a, i] * pltpu.roll(x[i], 1, 1)
                old[a, i] = x[i] + c1 * (x[i] - old[a, i]) + c2 * total

    def two(first):
        def body(k, carry):
            m = first + 2 * k
            sweep5(x5b, x5a, first + 2, ends[m, 0], ends[m, 1])
            sweep5(x5a, x5b, first + 3, ends[m + 1, 0], ends[m + 1, 1])
            return carry

        return body

    for first in range(0, 14, 2):
        two(first)(0, 0)
    sweep5(x5b, x5a, 16, ends[14, 0], ends[14, 1])

    for a in range(10):
        row = a - 3
        group = lax.rem(g + (row // 4) + NG, NG)
        at = 4 * lax.rem(group, 2) + group // 2
        for k in range(4):
            line = jnp.broadcast_to(x5a[16 + k, row % 4, pl.ds(at, 1), :], (2, 128))
            q4[a, 2 * k : 2 * k + 2, :] = line
            q4[a, 14 - 2 * k : 16 - 2 * k, :] = line
    grown = dot(q4[...].reshape(160, 128), spread).reshape(10, 16, 256)
    rows4 = lax.broadcasted_iota(jnp.int32, (16, 128), 0)
    first_half = rows4 < 8
    for copy in p4_groups:
        copy.wait_recv()
    for a in range(10):
        line = jnp.where(first_half, grown[a, :, 0:128], grown[a, :, 128:256])
        for r in (2 * a, 2 * a + 1):
            x4b[r] = jnp.where(m4, p4[1, r] + line, 0.0) * row_in(r, 8, 6)
            if 1 <= r < 19:
                fd4[r] = p4[0, r] * inv4[r]
    sweep(t4, fd4, x4b, x4a, 1, 19, 18, (1.0 / smooth_middle,))
    sweep(t4, fd4, x4a, x4b, 2, 18, 16, smooth_pairs[0])
    sweep(t4, fd4, x4b, x4a, 3, 17, 14, smooth_pairs[1])
    sweep(t4, fd4, x4a, x4b, 4, 16, 12, smooth_pairs[2])

    grown = dot(x4b[4:16, 4:12, :].reshape(96, 128), spread).reshape(12, 8, 256)
    for r in range(12):
        for k in range(2):
            line = grown[r, :, 128 * k : 128 * k + 128]
            u4[k, r, pl.ds(0, 8, stride=2), :] = line
            u4[k, r, pl.ds(1, 8, stride=2), :] = line
    for copy in x3_groups:
        copy.wait_recv()
    for r in range(24):
        row = row_in(r, N0, 4)
        for k in range(2):
            lanes = slice(128 * k, 128 * k + 128)
            x3b[r, :, lanes] = jnp.where(m3c[:, lanes], (h3[r, :, lanes] + u4[k, r // 2]) * row, 0.0)
    sweep(t3, fd3, x3b, x3a, 1, 23, 11, (1.0 / smooth_middle,))
    sweep(t3, fd3, x3a, x3b, 2, 22, 10, smooth_pairs[0])
    sweep(t3, fd3, x3b, x3a, 3, 21, 9, smooth_pairs[1])
    for copy in started:
        copy.wait_send()

    def last(k, carry):
        for i in range(8):
            r = 4 + 8 * k + i
            total = scaled_residual(t3, fd3, x3a, r)
            here = x3a[r]
            line = here + smooth_pairs[2][0] * (here - x3b[r]) + smooth_pairs[2][1] * total
            out[r - 4] = line[4:12]
        return carry

    lax.fori_loop(0, 2, last, 0)


SCRATCH = (
    [pltpu.VMEM(shape, F32) for shape in (
        (26, 8, 256), (2, 24, 8, 256), (6, 24, 8, 256), (24, 8, 256), (2, 24, 8, 256), (2, 24, 8, 256),
        (26, 8, 256), (2, 24, 8, 256),
        (24, 16, 256), (24, 16, 256), (26, 24, 256), (6, 24, 16, 256), (24, 16, 256), (24, 16, 256),
        (24, 16, 256), (24, 16, 256), (24, 16, 256),
        (2, 20, 16, 128), (20, 16, 128), (2, 20, 16, 128), (6, 20, 16, 128), (20, 16, 128), (20, 16, 128),
        (20, 16, 128), (20, 16, 128), (20, 16, 128), (8, 16, 128),
        (8, 256), (2, SPAN, 4, 8, 128), (SPAN, 4, 8, 128),
        (SPAN, 8, 128), (2, SPAN, 4, 8, 128), (6, SPAN, 4, 8, 128), (SPAN, 4, 8, 128),
        (SPAN, 4, 8, 128), (SPAN, 4, 8, 128), (SPAN, 4, 8, 128), (10, 16, 128), (8, 16, 256),
        (2, 12, 16, 128),
    )]
    + [pltpu.SemaphoreType.DMA((3,)), pltpu.SemaphoreType.REGULAR((2,)), pltpu.SMEM((16, 2), F32)]
    + [pltpu.SemaphoreType.DMA(shape) for count in (
        (3, 8), (2,), (2, 2), (6,), (8,), (4,), (6,), (4,), (2 * MID,), (1,), (3,), (2 * REACH,), (3,)
    ) for shape in (count, count)]
)


def cycle(source, alpha, beta):
    return pl.pallas_call(
        kernel,
        out_shape=pltpu.VMEM((N0, N1, N2), F32),
        in_specs=[pl.BlockSpec(memory_space=pl.ANY)] * 3,
        out_specs=pl.BlockSpec(memory_space=pltpu.VMEM),
        scratch_shapes=SCRATCH,
        compiler_params=pltpu.CompilerParams(
            collective_id=0, has_side_effects=True, vmem_limit_bytes=63 << 20
        ),
        name="vcycle",
    )(source, alpha, beta)


def solution(mesh):
    spec = P("grp", "box", None)
    return jax.shard_map(cycle, mesh=mesh, in_specs=(spec,) * 3, out_specs=spec, check_vma=False)
```

```python
import jax
import jax.numpy as jnp
from jax import lax
from jax.experimental import pallas as pl
from jax.experimental.pallas import tpu as pltpu
from jax.sharding import PartitionSpec as P

SMOOTH = 4
BOTTOM = 16
SMOOTH_LOW = 0.25
BOTTOM_LOW = 0.02
UPPER_BOUND = 2.0

MESH = pl.DeviceIdType.MESH
F32 = jnp.float32
NG, NB = 8, 32
N0, N1, N2 = 16, 8, 256
REACH = 9
MID = REACH + 1
SPAN = 2 * MID + 1

FACES = [(dg, db) for db in (-1, 1, 0) for dg in (0, -1, 1) if (dg, db) != (0, 0)]


def coefficients(degree, lower):
    middle = (UPPER_BOUND + lower) / 2.0
    spread = (UPPER_BOUND - lower) / 2.0
    base = middle / spread
    now = 1.0 / base
    pairs = []
    for _ in range(degree - 1):
        after = 1.0 / (2.0 * base - now)
        pairs.append((after * now, 2.0 * after / spread))
        now = after
    return middle, pairs


def part(step, size, width, origin):
    if step == 0:
        return 0, origin, size
    if step == 2:
        return size - (width - size), origin - width, width - size
    if step == -2:
        return 0, origin + 2 * size, width - size
    width = min(width, size)
    if step == 1:
        return size - width, origin - width, width
    return 0, origin + size, width


def kernel(
    source, alpha, beta, out,
    bo, af, to, fdo, xo, xr, lb, lz, f3, a3, b3, t3, d3, fd3, x3a, x3b, h3,
    ab4, f4, p4, t4, inv4, d4, fd4, x4a, x4b, w4,
    z5, g5ab, g5f, m5, c5, t5, inv5, fd5, x5a, x5b, q4, w3, u4,
    own_sem, hello, ends,
    s_p1, r_p1, s_x12, r_x12, s_late, r_late, s_ab4, r_ab4, s_f4, r_f4, s_x3, r_x3, s_p4, r_p4,
    s_aba, r_aba, s_abb, r_abb, s_abc, r_abc, s_fa, r_fa, s_fb, r_fb, s_fc, r_fc,
):
    g, b = lax.axis_index("grp"), lax.axis_index("box")
    core, chip = lax.rem(g, 2), g // 2
    sub = 4 * core + chip

    mine = pl.ds(pl.multiple_of(4 * core, 4), 4)
    partner = (g + 1 - 2 * core, b)

    def device(dg, db):
        return (lax.rem(g + dg + NG, NG), lax.rem(b + db + NB, NB))

    def remote(src, dst, send, recv, target):
        copy = pltpu.make_async_remote_copy(
            src_ref=src, dst_ref=dst, send_sem=send, recv_sem=recv, device_id=target, device_id_type=MESH
        )
        copy.start()
        return copy

    started = []

    own = [
        pltpu.make_async_copy(beta, bo.at[pl.ds(5, N0)], own_sem.at[0]),
        pltpu.make_async_copy(alpha, af.at[0, pl.ds(4, N0)], own_sem.at[1]),
        pltpu.make_async_copy(source, af.at[1, pl.ds(4, N0)], own_sem.at[2]),
    ]
    for copy in own:
        copy.start()

    partners = FACES + [(0, -8), (0, 8)]
    barrier = pltpu.get_barrier_semaphore()
    for dg, db in partners:
        pl.semaphore_signal(barrier, inc=1, device_id=device(dg, db), device_id_type=MESH)

    f4[...] = jnp.zeros_like(f4)
    pl.semaphore_wait(barrier, len(partners))

    def halo(src, dst, dg, db, w0, w1, o0, o1, size, send, recv):
        s0, t0, l0 = part(dg, size[0], w0, o0)
        s1, t1, l1 = part(db, size[1], w1, o1)
        return remote(
            src(s0, l0, s1, l1), dst(t0, l0, t1, l1), send, recv, device(dg, db)
        )

    def window(ref):
        return lambda i, n, j, m: ref.at[pl.ds(i, n), pl.ds(j, m), :]

    def window2(ref):
        return lambda i, n, j, m: ref.at[:, pl.ds(i, n), pl.ds(j, m), :]

    def inner(ref, o0, o1):
        return lambda i, n, j, m: ref.at[pl.ds(o0 + i, n), pl.ds(o1 + j, m), :]

    def inner2(ref, o0, o1):
        return lambda i, n, j, m: ref.at[:, pl.ds(o0 + i, n), pl.ds(o1 + j, m), :]

    along = []
    for n, (src, dst, w, o0) in enumerate(
        ((beta, bo, 5, 5), (alpha, af.at[0], 4, 4), (source, af.at[1], 4, 4))
    ):
        for k, dg in enumerate((-1, 1)):
            s0, t0, l0 = part(dg, N0, w, o0)
            along.append(
                remote(src.at[pl.ds(s0, l0)], dst.at[pl.ds(t0, l0)], s_p1.at[n, k], r_p1.at[n, k], device(dg, 0))
            )
    started += along
    p1 = []
    for n, (src, dst, w0, w1, o0, o1) in enumerate(
        ((beta, b3, 5, 3, 5, 8), (alpha, a3, 4, 2, 4, 4), (source, f3, 4, 2, 4, 4))
    ):
        for k, (dg, db) in enumerate(FACES[:6]):
            p1.append(
                halo(
                    window(src), window(dst), dg, db, w0, w1, o0, o1, (N0, N1),
                    s_p1.at[n, 2 + k], r_p1.at[n, 2 + k],
                )
            )
    started += p1

    def greet(n, peers):
        for dg, db in peers:
            pl.semaphore_signal(hello.at[n], inc=1, device_id=device(dg, db), device_id_type=MESH)

    greet(0, ((0, -1), (0, 1), (-1, 0), (1, 0)))

    rows256 = lax.broadcasted_iota(jnp.int32, (256, 128), 0)
    cols128 = lax.broadcasted_iota(jnp.int32, (256, 128), 1)
    gather = jnp.where(lax.shift_right_logical(rows256, 1) == cols128, 1.0, 0.0).astype(F32)
    rows128 = lax.broadcasted_iota(jnp.int32, (128, 256), 0)
    cols256 = lax.broadcasted_iota(jnp.int32, (128, 256), 1)
    spread = jnp.where(lax.shift_right_logical(cols256, 1) == rows128, 1.0, 0.0).astype(F32)

    def dot(x, matrix):
        return jnp.dot(x, matrix, precision=lax.Precision.HIGHEST, preferred_element_type=F32)

    def halve(pairs, o1):
        n = pairs.shape[1]
        w4[:, 0:n, :] = dot(pairs.reshape(8 * n, 256), gather).reshape(8, n, 128)
        return 0.125 * (w4[:, pl.ds(o1, 4, stride=2), :] + w4[:, pl.ds(o1 + 1, 4, stride=2), :])

    def pack(get, row):
        for i in range(4):
            t = get(2 * i) + get(2 * i + 1)
            z5[pl.ds(row + i, 1), 0:128] = t[0:1] + t[1:2]
            z5[pl.ds(row + i, 1), 128:256] = t[2:3] + t[3:4]

    for copy in own[:2]:
        copy.wait()
    ab4[0, 6:14, 6:10, :] = halve(
        jnp.stack([af[0, 4 + 2 * i] + af[0, 5 + 2 * i] for i in range(8)]), 0
    )
    ab4[1, 6:14, 6:10, :] = halve(
        jnp.stack([bo[5 + 2 * i] + bo[6 + 2 * i] for i in range(8)]), 0
    )
    pl.semaphore_wait(hello.at[0], 4)
    greet(1, ((0, -2), (0, 2), (-2, 0), (2, 0)))
    def inside(start, shape, axis, count):
        at = lax.broadcasted_iota(jnp.int32, shape, axis) + start
        return (at >= 0) & (at < count)

    def row_in(r, size, origin):
        at = size * g + r - origin
        return jnp.where((at >= 0) & (at < size * NG), 1.0, 0.0).astype(F32)

    lanes3 = lax.broadcasted_iota(jnp.int32, (16, 256), 1)
    smooth_middle, smooth_pairs = coefficients(SMOOTH, SMOOTH_LOW)

    def scaled_residual(t, fd, x, r):
        here = x[r]
        n, m = here.shape
        total = fd[r] - here
        total = total + t[0, r] * x[r + 1] + t[1, r] * x[r - 1]
        total = total + t[2, r] * pltpu.roll(here, n - 1, 0) + t[3, r] * pltpu.roll(here, 1, 0)
        return total + t[4, r] * pltpu.roll(here, m - 1, 1) + t[5, r] * pltpu.roll(here, 1, 1)

    def first(r, carry):
        here = row_in(r, N0, 4)
        bc = bo[r + 1] * here
        be = bo[r + 2] * row_in(r + 1, N0, 4)
        bw = bo[r] * row_in(r - 1, N0, 4)
        bn, bs = pltpu.roll(bc, 7, 0), pltpu.roll(bc, 1, 0)
        bu = jnp.where(lanes3[0:8] == 255, 0.0, pltpu.roll(bc, 255, 1))
        bd = jnp.where(lanes3[0:8] == 0, 0.0, pltpu.roll(bc, 1, 1))
        c = [0.5 * (bc + v) for v in (be, bw, bn, bs, bu, bd)]
        inv = here / (af[0, r] + c[0] + c[1] + c[2] + c[3] + c[4] + c[5])
        for n in range(4):
            to[n, r] = c[n] * inv
        to[4, r] = jnp.where(lanes3[0:8] == 255, 0.0, c[4] * inv)
        to[5, r] = jnp.where(lanes3[0:8] == 0, 0.0, c[5] * inv)
        fd = af[1, r] * inv
        fdo[r] = fd
        xo[0, r] = fd * (1.0 / smooth_middle)
        return carry

    def second(r, carry):
        here = xo[0, r]
        total = scaled_residual(to, fdo, xo.at[0], r)
        xo[1, r] = here + smooth_pairs[0][0] * here + smooth_pairs[0][1] * total
        return carry

    own[2].wait()
    for copy in along:
        copy.wait_recv()
    lax.fori_loop(0, 24, first, 0, unroll=6)
    lax.fori_loop(1, 23, second, 0, unroll=11)
    for r in (0, 23):
        xo[1, r] = jnp.zeros_like(xo[1, r])
    x12 = []
    for k, (db, src_at, dst_at) in enumerate(((1, 5, 1), (-1, 2, 6))):
        x12.append(
            remote(
                xo.at[:, :, pl.ds(src_at, 1), :], xr.at[:, :, pl.ds(dst_at, 1), :],
                s_x12.at[k], r_x12.at[k], device(0, db),
            )
        )
    started += x12

    def boxes4(ref, send, recv):
        copies = []
        for k, db in enumerate((-2, 2, -1, 1)):
            copies.append(
                halo(inner2(ref, 6, 6), window2(ref), 0, db, 6, 6, 6, 6, (8, 4), send.at[k], recv.at[k])
            )
        return copies

    def groups4(ref, send, recv):
        copies = []
        for k, dg in enumerate((-1, 1)):
            s0, t0, l0 = part(dg, 8, 6, 6)
            copies.append(
                remote(
                    ref.at[:, pl.ds(6 + s0, l0)], ref.at[:, pl.ds(t0, l0)],
                    send.at[4 + k], recv.at[4 + k], device(dg, 0),
                )
            )
        return copies

    ab4_boxes = boxes4(ab4, s_ab4, r_ab4)
    started += ab4_boxes
    for n in range(2):
        pack(lambda r, n=n: ab4[n, 6 + r, 6:10, :], 4 * n)
    packed = 0.125 * dot(z5[...], gather)
    for n in range(2):
        for i in range(4):
            g5ab[n, MID, i, pl.ds(sub, 1), :] = packed[4 * n + i : 4 * n + i + 1]
    pl.semaphore_wait(hello.at[1], 4)
    abb = []
    for k, db in enumerate([s * d for d in range(MID, 0, -1) for s in (-1, 1)]):
        abb.append(
            remote(
                g5ab.at[:, MID, :, pl.ds(sub, 1), :],
                g5ab.at[:, MID - db, :, pl.ds(sub, 1), :],
                s_abb.at[k], r_abb.at[k], device(0, db),
            )
        )
    started += abb


    x4a[...] = jnp.zeros_like(x4a)
    x5a[...] = jnp.zeros_like(x5a)
    x5b[...] = jnp.zeros_like(x5b)

    def place(r, carry):
        b3[r, 8:16, :] = bo[r]
        return carry

    def place2(r, carry):
        a3[r, 4:12, :] = af[0, r]
        f3[r, 4:12, :] = af[1, r]
        return carry

    lax.fori_loop(0, 26, place, 0, unroll=13)
    lax.fori_loop(0, 24, place2, 0, unroll=8)
    for copy in p1[:12]:
        copy.wait_recv()

    m3c = inside(N1 * b - 4, (16, 256), 0, N1 * NB)
    m3n = inside(N1 * b - 3, (16, 256), 0, N1 * NB)
    m3s = inside(N1 * b - 5, (16, 256), 0, N1 * NB)

    def table3(r, carry):
        here = row_in(r, N0, 4)
        bc = jnp.where(m3c, b3[r + 1, pl.ds(4, 16), :], 0.0) * here
        be = jnp.where(m3c, b3[r + 2, pl.ds(4, 16), :], 0.0) * row_in(r + 1, N0, 4)
        bw = jnp.where(m3c, b3[r, pl.ds(4, 16), :], 0.0) * row_in(r - 1, N0, 4)
        bn = jnp.where(m3n, b3[r + 1, pl.ds(5, 16), :], 0.0) * here
        bs = jnp.where(m3s, b3[r + 1, pl.ds(3, 16), :], 0.0) * here
        bu = jnp.where(lanes3 == 255, 0.0, pltpu.roll(bc, 255, 1))
        bd = jnp.where(lanes3 == 0, 0.0, pltpu.roll(bc, 1, 1))
        c = [0.5 * (bc + v) for v in (be, bw, bn, bs, bu, bd)]
        diag = a3[r] + c[0] + c[1] + c[2] + c[3] + c[4] + c[5]
        inv = jnp.where(m3c, 1.0 / diag, 0.0) * here
        for n in range(4):
            t3[n, r] = c[n] * inv
        t3[4, r] = jnp.where(lanes3 == 255, 0.0, c[4] * inv)
        t3[5, r] = jnp.where(lanes3 == 0, 0.0, c[5] * inv)
        d3[r] = diag
        fd3[r] = inv
        return carry

    def start3(r, carry):
        fd = f3[r] * fd3[r]
        fd3[r] = fd
        x3b[r] = fd * (1.0 / smooth_middle)
        x3a[r] = jnp.zeros_like(fd)
        return carry

    lax.fori_loop(0, 24, table3, 0, unroll=4)
    for copy in p1[12:]:
        copy.wait_recv()
    lax.fori_loop(0, 24, start3, 0, unroll=8)
    below = jnp.where(b > 0, 1.0, 0.0).astype(F32)
    above = jnp.where(b < NB - 1, 1.0, 0.0).astype(F32)

    def given(ref, n):
        def rows(r, carry):
            ref[r, 1:2, :] = xr[n, r, 1:2, :] * below
            ref[r, 14:15, :] = xr[n, r, 6:7, :] * above
            return carry

        lax.fori_loop(0, 24, rows, 0, unroll=8)

    for copy in x12:
        copy.wait_recv()
    given(x3b, 0)

    def sweep(t, fd, now, old, lo, hi, chunk, pair):
        def rows(k, carry):
            for i in range(chunk):
                r = lo + k * chunk + i
                total = scaled_residual(t, fd, now, r)
                here = now[r]
                if len(pair) == 1:
                    old[r] = here + pair[0] * total
                else:
                    old[r] = here + pair[0] * (here - old[r]) + pair[1] * total
            return carry

        lax.fori_loop(0, (hi - lo) // chunk, rows, 0)

    sweep(t3, fd3, x3b, x3a, 1, 23, 11, smooth_pairs[0])
    given(x3a, 1)
    sweep(t3, fd3, x3a, x3b, 2, 22, 10, smooth_pairs[1])
    sweep(t3, fd3, x3b, x3a, 3, 21, 9, smooth_pairs[2])

    def fine_residual(i):
        return d3[i] * scaled_residual(t3, fd3, x3a, i)

    for i in range(8):
        w3[i] = fine_residual(4 + 2 * i) + fine_residual(5 + 2 * i)
    f4[6:14, 6:10, :] = halve(w3[...], 4)
    f4_copies = []
    for k, (dg, db) in enumerate(FACES):
        f4_copies.append(
            halo(inner(f4, 6, 6), window(f4), dg, db, 4, 4, 6, 6, (8, 4), s_f4.at[k], r_f4.at[k])
        )
    started += f4_copies
    for i in range(16):
        h3[4 + i, 4:12, :] = x3a[4 + i, 4:12, :]
    x3_copies = []
    for copy in ab4_boxes:
        copy.wait_recv()
    ab4_groups = groups4(ab4, s_ab4, r_ab4)
    started += ab4_groups
    for k, db in enumerate((-1, 1)):
        x3_copies.append(
            halo(inner(h3, 4, 4), window(h3), 0, db, 4, 4, 4, 4, (N0, N1), s_x3.at[k], r_x3.at[k])
        )
    started += x3_copies
    late = []
    for k, (db, b_at, b_to, a_at, a_to) in enumerate(((1, 4, 4, 5, 1), (-1, 3, 3, 2, 6))):
        late.append(
            remote(
                bo.at[:, pl.ds(b_at, 1), :], lb.at[:, pl.ds(b_to, 1), :],
                s_late.at[0, k], r_late.at[0, k], device(0, db),
            )
        )
        late.append(
            remote(
                af.at[:, :, pl.ds(a_at, 1), :], lz.at[:, :, pl.ds(a_to, 1), :],
                s_late.at[1, k], r_late.at[1, k], device(0, db),
            )
        )
    started += late

    for copy in abb:
        copy.wait_recv()
    abc = []

    def share(at):
        block = g5ab.at[:, :, :, pl.ds(at, 1), :]
        k = len(abc)
        abc.append(remote(block, block, s_abc.at[k], r_abc.at[k], partner))

    aba = []
    for k, dg in enumerate((2, -2)):
        aba.append(
            remote(
                g5ab.at[:, :, :, pl.ds(sub, 1), :], g5ab.at[:, :, :, pl.ds(sub, 1), :],
                s_aba.at[k], r_aba.at[k], device(dg, 0),
            )
        )
    started += aba
    share(sub)

    for copy in ab4_groups:
        copy.wait_recv()
    lanes4 = lax.broadcasted_iota(jnp.int32, (16, 128), 1)
    m4 = inside(4 * b - 6, (16, 128), 0, 4 * NB)

    def masked4(r):
        return jnp.where(m4, ab4[1, r], 0.0) * row_in(r, 8, 6)

    def table4(r, carry):
        bc = masked4(r)
        be, bw = masked4(r + 1), masked4(r - 1)
        bn, bs = pltpu.roll(bc, 15, 0), pltpu.roll(bc, 1, 0)
        bu = jnp.where(lanes4 == 127, 0.0, pltpu.roll(bc, 127, 1))
        bd = jnp.where(lanes4 == 0, 0.0, pltpu.roll(bc, 1, 1))
        c = [0.125 * (bc + v) for v in (be, bw, bn, bs, bu, bd)]
        diag = ab4[0, r] + c[0] + c[1] + c[2] + c[3] + c[4] + c[5]
        inv = jnp.where(m4, 1.0 / diag, 0.0) * row_in(r, 8, 6)
        for n in range(4):
            t4[n, r] = c[n] * inv
        t4[4, r] = jnp.where(lanes4 == 127, 0.0, c[4] * inv)
        t4[5, r] = jnp.where(lanes4 == 0, 0.0, c[5] * inv)
        d4[r] = diag
        inv4[r] = inv
        return carry

    lax.fori_loop(1, 19, table4, 0, unroll=6)


    for copy in f4_copies:
        copy.wait_recv()
    for r in range(2, 18):
        fd = f4[r] * inv4[r]
        fd4[r] = fd
        x4b[r] = fd * (1.0 / smooth_middle)
    sweep(t4, fd4, x4b, x4a, 3, 17, 14, smooth_pairs[0])
    sweep(t4, fd4, x4a, x4b, 4, 16, 12, smooth_pairs[1])
    sweep(t4, fd4, x4b, x4a, 5, 15, 10, smooth_pairs[2])

    for r in range(8):
        w4[r] = d4[6 + r] * scaled_residual(t4, fd4, x4a, 6 + r)
    pack(lambda r: w4[r, 6:10, :], 0)
    packed = 0.125 * dot(z5[...], gather)
    for i in range(4):
        g5f[MID, i, pl.ds(sub, 1), :] = packed[i : i + 1]
    early = len(started)
    fa = []
    for k, dg in enumerate((2, 4, 6)):
        fa.append(
            remote(
                g5f.at[MID, :, pl.ds(sub, 1), :], g5f.at[MID, :, pl.ds(sub, 1), :],
                s_fa.at[k], r_fa.at[k], device(dg, 0),
            )
        )
    started += fa

    forward = []
    for k, (dg, first, size) in enumerate(((2, 0, MID + 1), (-2, MID + 1, MID))):
        aba[k].wait_recv()
        other = 4 * core + lax.rem(chip + (3, 1)[k], 4)
        block = g5ab.at[:, pl.ds(first, size), :, pl.ds(other, 1), :]
        forward.append(remote(block, block, s_aba.at[2 + k], r_aba.at[2 + k], device(dg, 0)))
        share(other)
    started += forward

    for copy in x3_copies:
        copy.wait_recv()
    x3_groups = []
    for k, dg in enumerate((-1, 1)):
        s0, t0, l0 = part(dg, N0, 4, 4)
        x3_groups.append(
            remote(
                h3.at[pl.ds(4 + s0, l0)], h3.at[pl.ds(t0, l0)],
                s_x3.at[2 + k], r_x3.at[2 + k], device(dg, 0),
            )
        )
    started += x3_groups

    p4[0, 6:14, 6:10, :] = f4[6:14, 6:10, :]
    p4[1, 6:14, 6:10, :] = x4a[6:14, 6:10, :]
    for copy in fa:
        copy.wait_recv()
    fb = []
    fb_from = [s * d for d in range(REACH, 0, -1) for s in (-1, 1)]
    for k, db in enumerate(fb_from):
        fb.append(
            remote(
                g5f.at[MID, :, mine, :], g5f.at[MID - db, :, mine, :],
                s_fb.at[k], r_fb.at[k], device(0, db),
            )
        )
    started += fb
    p4_boxes = boxes4(p4, s_p4, r_p4)
    started += p4_boxes

    for copy in forward:
        copy.wait_recv()
    share(4 * core + lax.rem(chip + 2, 4))
    started += abc

    for copy in late:
        copy.wait_recv()

    def widen(r, carry):
        b3[r, 4:5, :] = lb[r, 4:5, :]
        b3[r, 19:20, :] = lb[r, 3:4, :]
        return carry

    def widen2(r, carry):
        a3[r, 1:2, :] = lz[0, r, 1:2, :]
        a3[r, 14:15, :] = lz[0, r, 6:7, :]
        f3[r, 1:2, :] = lz[1, r, 1:2, :]
        f3[r, 14:15, :] = lz[1, r, 6:7, :]
        return carry

    def restart3(r, carry):
        fd3[r] = f3[r] * fd3[r]
        return carry

    lax.fori_loop(0, 26, widen, 0, unroll=13)
    lax.fori_loop(0, 24, widen2, 0, unroll=8)
    lax.fori_loop(0, 24, table3, 0, unroll=4)
    lax.fori_loop(0, 24, restart3, 0, unroll=8)
    for copy in started[:early]:
        copy.wait_send()
    started = started[early:]

    for copy in abc:
        copy.wait_recv()
    lanes5 = lax.broadcasted_iota(jnp.int32, (8, 128), 1)
    subs5 = lax.broadcasted_iota(jnp.int32, (8, 128), 0)
    low = lanes5 < 64
    front = subs5 < 4
    up_end = (lanes5 == 63) | (lanes5 == 127)
    down_end = (lanes5 == 0) | (lanes5 == 64)

    def next_group(v):
        return jnp.where(front, pltpu.roll(v, 4, 0), pltpu.roll(v, 3, 0))

    def last_group(v):
        return jnp.where(front, pltpu.roll(v, 5, 0), pltpu.roll(v, 4, 0))

    def box_in(k):
        at = b + k - MID
        return jnp.where((at >= 0) & (at < NB), 1.0, 0.0).astype(F32)

    def fold_even(get, t, i):
        return pltpu.roll(jnp.where(low, get(2 * MID - t, i), get(t, i)), 64, 1)

    def fold_odd(get, t, i):
        return jnp.where(low, get(t + 1, i), get(2 * MID - 1 - t, i))

    def fold5(t, carry):
        here = (2 * t, 2 * t + 1)
        m5[here[0]] = jnp.where(low, box_in(t), box_in(2 * MID - t))
        m5[here[1]] = jnp.where(low, box_in(t + 1), box_in(2 * MID - 1 - t))
        for i in range(4):
            for n in range(2):
                def get(k, i, n=n):
                    return g5ab[n, k, i]

                for a, fold in zip(here, (fold_even, fold_odd)):
                    value = fold(get, t, i)
                    c5[n, a, i] = value * m5[a] if n else value
        return carry

    lax.fori_loop(0, MID, fold5, 0, unroll=5)
    for i in range(4):
        c5[1, 2 * MID, i] = pltpu.roll(c5[1, 2 * MID - 1, i], 64, 1)

    def table5(a, carry):
        bc = [c5[1, a, i] for i in range(4)]
        mask = m5[a]
        for i in range(4):
            be = bc[i + 1] if i < 3 else jnp.where(subs5 == 7, 0.0, next_group(bc[0]))
            bw = bc[i - 1] if i > 0 else jnp.where(subs5 == 0, 0.0, last_group(bc[3]))
            bu = jnp.where(up_end, 0.0, pltpu.roll(bc[i], 127, 1))
            bd = jnp.where(down_end, 0.0, pltpu.roll(bc[i], 1, 1))
            c = [0.03125 * (bc[i] + v) for v in (be, bw, c5[1, a + 1, i], c5[1, a - 1, i], bu, bd)]
            inv = mask / (c5[0, a, i] + c[0] + c[1] + c[2] + c[3] + c[4] + c[5])
            t5[0, a, i] = c[0] * inv if i < 3 else jnp.where(subs5 == 7, 0.0, c[0] * inv)
            t5[1, a, i] = c[1] * inv if i > 0 else jnp.where(subs5 == 0, 0.0, c[1] * inv)
            t5[2, a, i] = c[2] * inv
            t5[3, a, i] = c[3] * inv
            t5[4, a, i] = jnp.where(up_end, 0.0, c[4] * inv)
            t5[5, a, i] = jnp.where(down_end, 0.0, c[5] * inv)
            inv5[a, i] = inv
        return carry

    lax.fori_loop(1, 2 * MID, table5, 0, unroll=5)


    fc = []
    for k, (first, last) in enumerate(((MID - 3, MID + 3), (1, MID - 4), (MID + 4, SPAN - 2))):
        for copy, db in zip(fb, fb_from):
            if first <= MID - db <= last:
                copy.wait_recv()
        span = pl.ds(first, last - first + 1)
        fc.append(
            remote(g5f.at[span, :, mine, :], g5f.at[span, :, mine, :], s_fc.at[k], r_fc.at[k], partner)
        )
    started += fc
    for copy in p4_boxes:
        copy.wait_recv()
    p4_groups = groups4(p4, s_p4, r_p4)
    started += p4_groups

    bottom_middle, bottom_pairs = coefficients(BOTTOM, BOTTOM_LOW)
    for m, (c1, c2) in enumerate(bottom_pairs):
        ends[m, 0] = F32(c1)
        ends[m, 1] = F32(c2)
    for copy in fc:
        copy.wait_recv()
    for a in range(1, 2 * MID):
        for i in range(4):
            folded = (fold_odd if a % 2 else fold_even)(lambda k, i: g5f[k, i], a // 2, i)
            fd = folded * inv5[a, i]
            fd5[a, i] = fd
            x5b[a, i] = fd * (1.0 / bottom_middle)

    def sweep5(now, old, first, c1, c2):
        for a in range(first, 2 * MID):
            x = [now[a, i] for i in range(4)]
            for i in range(4):
                east = x[i + 1] if i < 3 else next_group(x[0])
                west = x[i - 1] if i > 0 else last_group(x[3])
                inward = now[a + 1, i] if a < 2 * MID - 1 else pltpu.roll(x[i], 64, 1)
                total = fd5[a, i] - x[i]
                total = total + t5[0, a, i] * east + t5[1, a, i] * west
                total = total + t5[2, a, i] * inward + t5[3, a, i] * now[a - 1, i]
                total = total + t5[4, a, i] * pltpu.roll(x[i], 127, 1) + t5[5, a, i] * pltpu.roll(x[i], 1, 1)
                old[a, i] = x[i] + c1 * (x[i] - old[a, i]) + c2 * total

    def two(first):
        def body(k, carry):
            m = first + 2 * k
            sweep5(x5b, x5a, first + 2, ends[m, 0], ends[m, 1])
            sweep5(x5a, x5b, first + 3, ends[m + 1, 0], ends[m + 1, 1])
            return carry

        return body

    for first in range(0, 14, 2):
        two(first)(0, 0)
    sweep5(x5b, x5a, 16, ends[14, 0], ends[14, 1])

    for a in range(10):
        row = a - 3
        group = lax.rem(g + (row // 4) + NG, NG)
        at = 4 * lax.rem(group, 2) + group // 2
        for k in range(4):
            line = jnp.broadcast_to(x5a[16 + k, row % 4, pl.ds(at, 1), :], (2, 128))
            q4[a, 2 * k : 2 * k + 2, :] = line
            q4[a, 14 - 2 * k : 16 - 2 * k, :] = line
    grown = dot(q4[...].reshape(160, 128), spread).reshape(10, 16, 256)
    rows4 = lax.broadcasted_iota(jnp.int32, (16, 128), 0)
    first_half = rows4 < 8
    for copy in p4_groups:
        copy.wait_recv()
    for a in range(10):
        line = jnp.where(first_half, grown[a, :, 0:128], grown[a, :, 128:256])
        for r in (2 * a, 2 * a + 1):
            x4b[r] = jnp.where(m4, p4[1, r] + line, 0.0) * row_in(r, 8, 6)
            if 1 <= r < 19:
                fd4[r] = p4[0, r] * inv4[r]
    sweep(t4, fd4, x4b, x4a, 1, 19, 18, (1.0 / smooth_middle,))
    sweep(t4, fd4, x4a, x4b, 2, 18, 16, smooth_pairs[0])
    sweep(t4, fd4, x4b, x4a, 3, 17, 14, smooth_pairs[1])
    sweep(t4, fd4, x4a, x4b, 4, 16, 12, smooth_pairs[2])

    grown = dot(x4b[4:16, 4:12, :].reshape(96, 128), spread).reshape(12, 8, 256)
    for r in range(12):
        for k in range(2):
            line = grown[r, :, 128 * k : 128 * k + 128]
            u4[k, r, pl.ds(0, 8, stride=2), :] = line
            u4[k, r, pl.ds(1, 8, stride=2), :] = line
    for copy in x3_groups:
        copy.wait_recv()
    for r in range(24):
        row = row_in(r, N0, 4)
        for k in range(2):
            lanes = slice(128 * k, 128 * k + 128)
            x3b[r, :, lanes] = jnp.where(m3c[:, lanes], (h3[r, :, lanes] + u4[k, r // 2]) * row, 0.0)
    sweep(t3, fd3, x3b, x3a, 1, 23, 11, (1.0 / smooth_middle,))
    sweep(t3, fd3, x3a, x3b, 2, 22, 10, smooth_pairs[0])
    sweep(t3, fd3, x3b, x3a, 3, 21, 9, smooth_pairs[1])
    for copy in started:
        copy.wait_send()

    def last(k, carry):
        for i in range(8):
            r = 4 + 8 * k + i
            total = scaled_residual(t3, fd3, x3a, r)
            here = x3a[r]
            line = here + smooth_pairs[2][0] * (here - x3b[r]) + smooth_pairs[2][1] * total
            out[r - 4] = line[4:12]
        return carry

    lax.fori_loop(0, 2, last, 0)


SCRATCH = (
    [pltpu.VMEM(shape, F32) for shape in (
        (26, 8, 256), (2, 24, 8, 256), (6, 24, 8, 256), (24, 8, 256), (2, 24, 8, 256), (2, 24, 8, 256),
        (26, 8, 256), (2, 24, 8, 256),
        (24, 16, 256), (24, 16, 256), (26, 24, 256), (6, 24, 16, 256), (24, 16, 256), (24, 16, 256),
        (24, 16, 256), (24, 16, 256), (24, 16, 256),
        (2, 20, 16, 128), (20, 16, 128), (2, 20, 16, 128), (6, 20, 16, 128), (20, 16, 128), (20, 16, 128),
        (20, 16, 128), (20, 16, 128), (20, 16, 128), (8, 16, 128),
        (8, 256), (2, SPAN, 4, 8, 128), (SPAN, 4, 8, 128),
        (SPAN, 8, 128), (2, SPAN, 4, 8, 128), (6, SPAN, 4, 8, 128), (SPAN, 4, 8, 128),
        (SPAN, 4, 8, 128), (SPAN, 4, 8, 128), (SPAN, 4, 8, 128), (10, 16, 128), (8, 16, 256),
        (2, 12, 16, 128),
    )]
    + [pltpu.SemaphoreType.DMA((3,)), pltpu.SemaphoreType.REGULAR((2,)), pltpu.SMEM((16, 2), F32)]
    + [pltpu.SemaphoreType.DMA(shape) for count in (
        (3, 8), (2,), (2, 2), (6,), (8,), (4,), (6,), (4,), (2 * MID,), (4,), (3,), (2 * REACH,), (3,)
    ) for shape in (count, count)]
)


def cycle(source, alpha, beta):
    return pl.pallas_call(
        kernel,
        out_shape=pltpu.VMEM((N0, N1, N2), F32),
        in_specs=[pl.BlockSpec(memory_space=pl.ANY)] * 3,
        out_specs=pl.BlockSpec(memory_space=pltpu.VMEM),
        scratch_shapes=SCRATCH,
        compiler_params=pltpu.CompilerParams(
            collective_id=0, has_side_effects=True, vmem_limit_bytes=63 << 20
        ),
        name="vcycle",
    )(source, alpha, beta)


def solution(mesh):
    spec = P("grp", "box", None)
    return jax.shard_map(cycle, mesh=mesh, in_specs=(spec,) * 3, out_specs=spec, check_vma=False)
```

```python
import jax
import jax.numpy as jnp
from jax import lax
from jax.experimental import pallas as pl
from jax.experimental.pallas import tpu as pltpu
from jax.sharding import PartitionSpec as P

SMOOTH = 4
BOTTOM = 16
SMOOTH_LOW = 0.25
BOTTOM_LOW = 0.02
UPPER_BOUND = 2.0

MESH = pl.DeviceIdType.MESH
F32 = jnp.float32
NG, NB = 8, 32
N0, N1, N2 = 16, 8, 256
REACH = 9
MID = REACH + 1
SPAN = 2 * MID + 1

FACES = [(dg, db) for db in (-1, 1, 0) for dg in (0, -1, 1) if (dg, db) != (0, 0)]


def coefficients(degree, lower):
    middle = (UPPER_BOUND + lower) / 2.0
    spread = (UPPER_BOUND - lower) / 2.0
    base = middle / spread
    now = 1.0 / base
    pairs = []
    for _ in range(degree - 1):
        after = 1.0 / (2.0 * base - now)
        pairs.append((after * now, 2.0 * after / spread))
        now = after
    return middle, pairs


def part(step, size, width, origin):
    if step == 0:
        return 0, origin, size
    if step == 2:
        return size - (width - size), origin - width, width - size
    if step == -2:
        return 0, origin + 2 * size, width - size
    width = min(width, size)
    if step == 1:
        return size - width, origin - width, width
    return 0, origin + size, width


def kernel(
    source, alpha, beta, out,
    bo, af, to, fdo, xo, xr, lb, lz, f3, a3, b3, t3, d3, fd3, x3a, x3b, h3,
    ab4, f4, p4, t4, inv4, d4, fd4, x4a, x4b, w4,
    z5, g5ab, g5f, m5, c5, t5, inv5, fd5, x5a, x5b, q4, w3, u4,
    own_sem, hello, ends,
    s_p1, r_p1, s_x12, r_x12, s_late, r_late, s_ab4, r_ab4, s_f4, r_f4, s_x3, r_x3, s_p4, r_p4,
    s_aba, r_aba, s_abb, r_abb, s_abc, r_abc, s_fa, r_fa, s_fb, r_fb, s_fc, r_fc,
):
    g, b = lax.axis_index("grp"), lax.axis_index("box")
    core, chip = lax.rem(g, 2), g // 2
    sub = 4 * core + chip

    def device(dg, db):
        return (lax.rem(g + dg + NG, NG), lax.rem(b + db + NB, NB))

    def remote(src, dst, send, recv, target):
        copy = pltpu.make_async_remote_copy(
            src_ref=src, dst_ref=dst, send_sem=send, recv_sem=recv, device_id=target, device_id_type=MESH
        )
        copy.start()
        return copy

    started = []

    own = [
        pltpu.make_async_copy(beta, bo.at[pl.ds(5, N0)], own_sem.at[0]),
        pltpu.make_async_copy(alpha, af.at[0, pl.ds(4, N0)], own_sem.at[1]),
        pltpu.make_async_copy(source, af.at[1, pl.ds(4, N0)], own_sem.at[2]),
    ]
    for copy in own:
        copy.start()

    partners = FACES + [(0, -8), (0, 8)]
    barrier = pltpu.get_barrier_semaphore()
    for dg, db in partners:
        pl.semaphore_signal(barrier, inc=1, device_id=device(dg, db), device_id_type=MESH)

    f4[...] = jnp.zeros_like(f4)
    pl.semaphore_wait(barrier, len(partners))

    def halo(src, dst, dg, db, w0, w1, o0, o1, size, send, recv):
        s0, t0, l0 = part(dg, size[0], w0, o0)
        s1, t1, l1 = part(db, size[1], w1, o1)
        return remote(
            src(s0, l0, s1, l1), dst(t0, l0, t1, l1), send, recv, device(dg, db)
        )

    def window(ref):
        return lambda i, n, j, m: ref.at[pl.ds(i, n), pl.ds(j, m), :]

    def window2(ref):
        return lambda i, n, j, m: ref.at[:, pl.ds(i, n), pl.ds(j, m), :]

    def inner(ref, o0, o1):
        return lambda i, n, j, m: ref.at[pl.ds(o0 + i, n), pl.ds(o1 + j, m), :]

    def inner2(ref, o0, o1):
        return lambda i, n, j, m: ref.at[:, pl.ds(o0 + i, n), pl.ds(o1 + j, m), :]

    along = []
    for n, (src, dst, w, o0) in enumerate(
        ((beta, bo, 5, 5), (alpha, af.at[0], 4, 4), (source, af.at[1], 4, 4))
    ):
        for k, dg in enumerate((-1, 1)):
            s0, t0, l0 = part(dg, N0, w, o0)
            along.append(
                remote(src.at[pl.ds(s0, l0)], dst.at[pl.ds(t0, l0)], s_p1.at[n, k], r_p1.at[n, k], device(dg, 0))
            )
    started += along
    p1 = []
    for n, (src, dst, w0, w1, o0, o1) in enumerate(
        ((beta, b3, 5, 3, 5, 8), (alpha, a3, 4, 2, 4, 4), (source, f3, 4, 2, 4, 4))
    ):
        for k, (dg, db) in enumerate(FACES[:6]):
            p1.append(
                halo(
                    window(src), window(dst), dg, db, w0, w1, o0, o1, (N0, N1),
                    s_p1.at[n, 2 + k], r_p1.at[n, 2 + k],
                )
            )
    started += p1

    def greet(n, peers):
        for dg, db in peers:
            pl.semaphore_signal(hello.at[n], inc=1, device_id=device(dg, db), device_id_type=MESH)

    greet(0, ((0, -1), (0, 1), (-1, 0), (1, 0)))

    rows256 = lax.broadcasted_iota(jnp.int32, (256, 128), 0)
    cols128 = lax.broadcasted_iota(jnp.int32, (256, 128), 1)
    gather = jnp.where(lax.shift_right_logical(rows256, 1) == cols128, 1.0, 0.0).astype(F32)
    rows128 = lax.broadcasted_iota(jnp.int32, (128, 256), 0)
    cols256 = lax.broadcasted_iota(jnp.int32, (128, 256), 1)
    spread = jnp.where(lax.shift_right_logical(cols256, 1) == rows128, 1.0, 0.0).astype(F32)

    def dot(x, matrix):
        return jnp.dot(x, matrix, precision=lax.Precision.HIGHEST, preferred_element_type=F32)

    def halve(pairs, o1):
        n = pairs.shape[1]
        w4[:, 0:n, :] = dot(pairs.reshape(8 * n, 256), gather).reshape(8, n, 128)
        return 0.125 * (w4[:, pl.ds(o1, 4, stride=2), :] + w4[:, pl.ds(o1 + 1, 4, stride=2), :])

    def pack(get, row):
        for i in range(4):
            t = get(2 * i) + get(2 * i + 1)
            z5[pl.ds(row + i, 1), 0:128] = t[0:1] + t[1:2]
            z5[pl.ds(row + i, 1), 128:256] = t[2:3] + t[3:4]

    for copy in own[:2]:
        copy.wait()
    ab4[0, 6:14, 6:10, :] = halve(
        jnp.stack([af[0, 4 + 2 * i] + af[0, 5 + 2 * i] for i in range(8)]), 0
    )
    ab4[1, 6:14, 6:10, :] = halve(
        jnp.stack([bo[5 + 2 * i] + bo[6 + 2 * i] for i in range(8)]), 0
    )
    pl.semaphore_wait(hello.at[0], 4)
    greet(1, ((0, -2), (0, 2), (-2, 0), (2, 0)))
    def inside(start, shape, axis, count):
        at = lax.broadcasted_iota(jnp.int32, shape, axis) + start
        return (at >= 0) & (at < count)

    def row_in(r, size, origin):
        at = size * g + r - origin
        return jnp.where((at >= 0) & (at < size * NG), 1.0, 0.0).astype(F32)

    lanes3 = lax.broadcasted_iota(jnp.int32, (16, 256), 1)
    smooth_middle, smooth_pairs = coefficients(SMOOTH, SMOOTH_LOW)

    def scaled_residual(t, fd, x, r):
        here = x[r]
        n, m = here.shape
        total = fd[r] - here
        total = total + t[0, r] * x[r + 1] + t[1, r] * x[r - 1]
        total = total + t[2, r] * pltpu.roll(here, n - 1, 0) + t[3, r] * pltpu.roll(here, 1, 0)
        return total + t[4, r] * pltpu.roll(here, m - 1, 1) + t[5, r] * pltpu.roll(here, 1, 1)

    def first(r, carry):
        here = row_in(r, N0, 4)
        bc = bo[r + 1] * here
        be = bo[r + 2] * row_in(r + 1, N0, 4)
        bw = bo[r] * row_in(r - 1, N0, 4)
        bn, bs = pltpu.roll(bc, 7, 0), pltpu.roll(bc, 1, 0)
        bu = jnp.where(lanes3[0:8] == 255, 0.0, pltpu.roll(bc, 255, 1))
        bd = jnp.where(lanes3[0:8] == 0, 0.0, pltpu.roll(bc, 1, 1))
        c = [0.5 * (bc + v) for v in (be, bw, bn, bs, bu, bd)]
        inv = here / (af[0, r] + c[0] + c[1] + c[2] + c[3] + c[4] + c[5])
        for n in range(4):
            to[n, r] = c[n] * inv
        to[4, r] = jnp.where(lanes3[0:8] == 255, 0.0, c[4] * inv)
        to[5, r] = jnp.where(lanes3[0:8] == 0, 0.0, c[5] * inv)
        fd = af[1, r] * inv
        fdo[r] = fd
        xo[0, r] = fd * (1.0 / smooth_middle)
        return carry

    def second(r, carry):
        here = xo[0, r]
        total = scaled_residual(to, fdo, xo.at[0], r)
        xo[1, r] = here + smooth_pairs[0][0] * here + smooth_pairs[0][1] * total
        return carry

    own[2].wait()
    for copy in along:
        copy.wait_recv()
    lax.fori_loop(0, 24, first, 0, unroll=6)
    lax.fori_loop(1, 23, second, 0, unroll=11)
    for r in (0, 23):
        xo[1, r] = jnp.zeros_like(xo[1, r])
    x12 = []
    for k, (db, src_at, dst_at) in enumerate(((1, 5, 1), (-1, 2, 6))):
        x12.append(
            remote(
                xo.at[:, :, pl.ds(src_at, 1), :], xr.at[:, :, pl.ds(dst_at, 1), :],
                s_x12.at[k], r_x12.at[k], device(0, db),
            )
        )
    started += x12

    def boxes4(ref, send, recv):
        copies = []
        for k, db in enumerate((-2, 2, -1, 1)):
            copies.append(
                halo(inner2(ref, 6, 6), window2(ref), 0, db, 6, 6, 6, 6, (8, 4), send.at[k], recv.at[k])
            )
        return copies

    def groups4(ref, send, recv):
        copies = []
        for k, dg in enumerate((-1, 1)):
            s0, t0, l0 = part(dg, 8, 6, 6)
            copies.append(
                remote(
                    ref.at[:, pl.ds(6 + s0, l0)], ref.at[:, pl.ds(t0, l0)],
                    send.at[4 + k], recv.at[4 + k], device(dg, 0),
                )
            )
        return copies

    ab4_boxes = boxes4(ab4, s_ab4, r_ab4)
    started += ab4_boxes
    for n in range(2):
        pack(lambda r, n=n: ab4[n, 6 + r, 6:10, :], 4 * n)
    packed = 0.125 * dot(z5[...], gather)
    for n in range(2):
        for i in range(4):
            g5ab[n, MID, i, pl.ds(sub, 1), :] = packed[4 * n + i : 4 * n + i + 1]
    pl.semaphore_wait(hello.at[1], 4)
    abb = []
    for k, db in enumerate([s * d for d in range(MID, 0, -1) for s in (-1, 1)]):
        abb.append(
            remote(
                g5ab.at[:, MID, :, pl.ds(sub, 1), :],
                g5ab.at[:, MID - db, :, pl.ds(sub, 1), :],
                s_abb.at[k], r_abb.at[k], device(0, db),
            )
        )
    started += abb


    x4a[...] = jnp.zeros_like(x4a)
    x5a[...] = jnp.zeros_like(x5a)
    x5b[...] = jnp.zeros_like(x5b)

    def place(r, carry):
        b3[r, 8:16, :] = bo[r]
        return carry

    def place2(r, carry):
        a3[r, 4:12, :] = af[0, r]
        f3[r, 4:12, :] = af[1, r]
        return carry

    lax.fori_loop(0, 26, place, 0, unroll=13)
    lax.fori_loop(0, 24, place2, 0, unroll=8)
    for copy in p1[:12]:
        copy.wait_recv()

    m3c = inside(N1 * b - 4, (16, 256), 0, N1 * NB)
    m3n = inside(N1 * b - 3, (16, 256), 0, N1 * NB)
    m3s = inside(N1 * b - 5, (16, 256), 0, N1 * NB)

    def table3(r, carry):
        here = row_in(r, N0, 4)
        bc = jnp.where(m3c, b3[r + 1, pl.ds(4, 16), :], 0.0) * here
        be = jnp.where(m3c, b3[r + 2, pl.ds(4, 16), :], 0.0) * row_in(r + 1, N0, 4)
        bw = jnp.where(m3c, b3[r, pl.ds(4, 16), :], 0.0) * row_in(r - 1, N0, 4)
        bn = jnp.where(m3n, b3[r + 1, pl.ds(5, 16), :], 0.0) * here
        bs = jnp.where(m3s, b3[r + 1, pl.ds(3, 16), :], 0.0) * here
        bu = jnp.where(lanes3 == 255, 0.0, pltpu.roll(bc, 255, 1))
        bd = jnp.where(lanes3 == 0, 0.0, pltpu.roll(bc, 1, 1))
        c = [0.5 * (bc + v) for v in (be, bw, bn, bs, bu, bd)]
        diag = a3[r] + c[0] + c[1] + c[2] + c[3] + c[4] + c[5]
        inv = jnp.where(m3c, 1.0 / diag, 0.0) * here
        for n in range(4):
            t3[n, r] = c[n] * inv
        t3[4, r] = jnp.where(lanes3 == 255, 0.0, c[4] * inv)
        t3[5, r] = jnp.where(lanes3 == 0, 0.0, c[5] * inv)
        d3[r] = diag
        fd3[r] = inv
        return carry

    def start3(r, carry):
        fd = f3[r] * fd3[r]
        fd3[r] = fd
        x3b[r] = fd * (1.0 / smooth_middle)
        x3a[r] = jnp.zeros_like(fd)
        return carry

    lax.fori_loop(0, 24, table3, 0, unroll=4)
    for copy in p1[12:]:
        copy.wait_recv()
    lax.fori_loop(0, 24, start3, 0, unroll=8)
    below = jnp.where(b > 0, 1.0, 0.0).astype(F32)
    above = jnp.where(b < NB - 1, 1.0, 0.0).astype(F32)

    def given(ref, n):
        def rows(r, carry):
            ref[r, 1:2, :] = xr[n, r, 1:2, :] * below
            ref[r, 14:15, :] = xr[n, r, 6:7, :] * above
            return carry

        lax.fori_loop(0, 24, rows, 0, unroll=8)

    for copy in x12:
        copy.wait_recv()
    given(x3b, 0)

    def sweep(t, fd, now, old, lo, hi, chunk, pair):
        def rows(k, carry):
            for i in range(chunk):
                r = lo + k * chunk + i
                total = scaled_residual(t, fd, now, r)
                here = now[r]
                if len(pair) == 1:
                    old[r] = here + pair[0] * total
                else:
                    old[r] = here + pair[0] * (here - old[r]) + pair[1] * total
            return carry

        lax.fori_loop(0, (hi - lo) // chunk, rows, 0)

    sweep(t3, fd3, x3b, x3a, 1, 23, 11, smooth_pairs[0])
    given(x3a, 1)
    sweep(t3, fd3, x3a, x3b, 2, 22, 10, smooth_pairs[1])
    sweep(t3, fd3, x3b, x3a, 3, 21, 9, smooth_pairs[2])

    def fine_residual(i):
        return d3[i] * scaled_residual(t3, fd3, x3a, i)

    for i in range(8):
        w3[i] = fine_residual(4 + 2 * i) + fine_residual(5 + 2 * i)
    f4[6:14, 6:10, :] = halve(w3[...], 4)
    f4_copies = []
    for k, (dg, db) in enumerate(FACES):
        f4_copies.append(
            halo(inner(f4, 6, 6), window(f4), dg, db, 4, 4, 6, 6, (8, 4), s_f4.at[k], r_f4.at[k])
        )
    started += f4_copies
    for i in range(16):
        h3[4 + i, 4:12, :] = x3a[4 + i, 4:12, :]
    x3_copies = []
    for copy in ab4_boxes:
        copy.wait_recv()
    ab4_groups = groups4(ab4, s_ab4, r_ab4)
    started += ab4_groups
    for copy in abb:
        copy.wait_recv()
    aba = []
    for k, dg in enumerate((2, -2)):
        aba.append(
            remote(
                g5ab.at[:, :, :, pl.ds(sub, 1), :], g5ab.at[:, :, :, pl.ds(sub, 1), :],
                s_aba.at[k], r_aba.at[k], device(dg, 0),
            )
        )
    started += aba
    for k, db in enumerate((-1, 1)):
        x3_copies.append(
            halo(inner(h3, 4, 4), window(h3), 0, db, 4, 4, 4, 4, (N0, N1), s_x3.at[k], r_x3.at[k])
        )
    started += x3_copies
    late = []
    for k, (db, b_at, b_to, a_at, a_to) in enumerate(((1, 4, 4, 5, 1), (-1, 3, 3, 2, 6))):
        late.append(
            remote(
                bo.at[:, pl.ds(b_at, 1), :], lb.at[:, pl.ds(b_to, 1), :],
                s_late.at[0, k], r_late.at[0, k], device(0, db),
            )
        )
        late.append(
            remote(
                af.at[:, :, pl.ds(a_at, 1), :], lz.at[:, :, pl.ds(a_to, 1), :],
                s_late.at[1, k], r_late.at[1, k], device(0, db),
            )
        )
    started += late


    for copy in ab4_groups:
        copy.wait_recv()
    lanes4 = lax.broadcasted_iota(jnp.int32, (16, 128), 1)
    m4 = inside(4 * b - 6, (16, 128), 0, 4 * NB)

    def masked4(r):
        return jnp.where(m4, ab4[1, r], 0.0) * row_in(r, 8, 6)

    def table4(r, carry):
        bc = masked4(r)
        be, bw = masked4(r + 1), masked4(r - 1)
        bn, bs = pltpu.roll(bc, 15, 0), pltpu.roll(bc, 1, 0)
        bu = jnp.where(lanes4 == 127, 0.0, pltpu.roll(bc, 127, 1))
        bd = jnp.where(lanes4 == 0, 0.0, pltpu.roll(bc, 1, 1))
        c = [0.125 * (bc + v) for v in (be, bw, bn, bs, bu, bd)]
        diag = ab4[0, r] + c[0] + c[1] + c[2] + c[3] + c[4] + c[5]
        inv = jnp.where(m4, 1.0 / diag, 0.0) * row_in(r, 8, 6)
        for n in range(4):
            t4[n, r] = c[n] * inv
        t4[4, r] = jnp.where(lanes4 == 127, 0.0, c[4] * inv)
        t4[5, r] = jnp.where(lanes4 == 0, 0.0, c[5] * inv)
        d4[r] = diag
        inv4[r] = inv
        return carry

    lax.fori_loop(1, 19, table4, 0, unroll=6)

    mine = pl.ds(pl.multiple_of(4 * core, 4), 4)
    partner = (g + 1 - 2 * core, b)

    for copy in f4_copies:
        copy.wait_recv()
    for r in range(2, 18):
        fd = f4[r] * inv4[r]
        fd4[r] = fd
        x4b[r] = fd * (1.0 / smooth_middle)
    sweep(t4, fd4, x4b, x4a, 3, 17, 14, smooth_pairs[0])
    sweep(t4, fd4, x4a, x4b, 4, 16, 12, smooth_pairs[1])
    sweep(t4, fd4, x4b, x4a, 5, 15, 10, smooth_pairs[2])

    for r in range(8):
        w4[r] = d4[6 + r] * scaled_residual(t4, fd4, x4a, 6 + r)
    pack(lambda r: w4[r, 6:10, :], 0)
    packed = 0.125 * dot(z5[...], gather)
    for i in range(4):
        g5f[MID, i, pl.ds(sub, 1), :] = packed[i : i + 1]
    early = len(started)
    fa = []
    for k, dg in enumerate((2, 4, 6)):
        fa.append(
            remote(
                g5f.at[MID, :, pl.ds(sub, 1), :], g5f.at[MID, :, pl.ds(sub, 1), :],
                s_fa.at[k], r_fa.at[k], device(dg, 0),
            )
        )
    started += fa

    forward = []
    for k, (dg, first, size) in enumerate(((2, 0, MID + 1), (-2, MID + 1, MID))):
        aba[k].wait_recv()
        other = 4 * core + lax.rem(chip + (3, 1)[k], 4)
        block = g5ab.at[:, pl.ds(first, size), :, pl.ds(other, 1), :]
        forward.append(remote(block, block, s_aba.at[2 + k], r_aba.at[2 + k], device(dg, 0)))
    started += forward

    for copy in x3_copies:
        copy.wait_recv()
    x3_groups = []
    for k, dg in enumerate((-1, 1)):
        s0, t0, l0 = part(dg, N0, 4, 4)
        x3_groups.append(
            remote(
                h3.at[pl.ds(4 + s0, l0)], h3.at[pl.ds(t0, l0)],
                s_x3.at[2 + k], r_x3.at[2 + k], device(dg, 0),
            )
        )
    started += x3_groups

    p4[0, 6:14, 6:10, :] = f4[6:14, 6:10, :]
    p4[1, 6:14, 6:10, :] = x4a[6:14, 6:10, :]
    for copy in fa:
        copy.wait_recv()
    fb = []
    fb_from = [s * d for d in range(REACH, 0, -1) for s in (-1, 1)]
    for k, db in enumerate(fb_from):
        fb.append(
            remote(
                g5f.at[MID, :, mine, :], g5f.at[MID - db, :, mine, :],
                s_fb.at[k], r_fb.at[k], device(0, db),
            )
        )
    started += fb
    p4_boxes = boxes4(p4, s_p4, r_p4)
    started += p4_boxes

    for copy in forward:
        copy.wait_recv()
    abc = remote(
        g5ab.at[:, :, :, mine, :], g5ab.at[:, :, :, mine, :], s_abc.at[0], r_abc.at[0], partner
    )
    started.append(abc)

    for copy in late:
        copy.wait_recv()

    def widen(r, carry):
        b3[r, 4:5, :] = lb[r, 4:5, :]
        b3[r, 19:20, :] = lb[r, 3:4, :]
        return carry

    def widen2(r, carry):
        a3[r, 1:2, :] = lz[0, r, 1:2, :]
        a3[r, 14:15, :] = lz[0, r, 6:7, :]
        f3[r, 1:2, :] = lz[1, r, 1:2, :]
        f3[r, 14:15, :] = lz[1, r, 6:7, :]
        return carry

    def restart3(r, carry):
        fd3[r] = f3[r] * fd3[r]
        return carry

    lax.fori_loop(0, 26, widen, 0, unroll=13)
    lax.fori_loop(0, 24, widen2, 0, unroll=8)
    lax.fori_loop(0, 24, table3, 0, unroll=4)
    lax.fori_loop(0, 24, restart3, 0, unroll=8)
    for copy in started[:early]:
        copy.wait_send()
    started = started[early:]

    abc.wait_recv()
    lanes5 = lax.broadcasted_iota(jnp.int32, (8, 128), 1)
    subs5 = lax.broadcasted_iota(jnp.int32, (8, 128), 0)
    low = lanes5 < 64
    front = subs5 < 4
    up_end = (lanes5 == 63) | (lanes5 == 127)
    down_end = (lanes5 == 0) | (lanes5 == 64)

    def next_group(v):
        return jnp.where(front, pltpu.roll(v, 4, 0), pltpu.roll(v, 3, 0))

    def last_group(v):
        return jnp.where(front, pltpu.roll(v, 5, 0), pltpu.roll(v, 4, 0))

    def box_in(k):
        at = b + k - MID
        return jnp.where((at >= 0) & (at < NB), 1.0, 0.0).astype(F32)

    def fold_even(get, t, i):
        return pltpu.roll(jnp.where(low, get(2 * MID - t, i), get(t, i)), 64, 1)

    def fold_odd(get, t, i):
        return jnp.where(low, get(t + 1, i), get(2 * MID - 1 - t, i))

    def fold5(t, carry):
        here = (2 * t, 2 * t + 1)
        m5[here[0]] = jnp.where(low, box_in(t), box_in(2 * MID - t))
        m5[here[1]] = jnp.where(low, box_in(t + 1), box_in(2 * MID - 1 - t))
        for i in range(4):
            for n in range(2):
                def get(k, i, n=n):
                    return g5ab[n, k, i]

                for a, fold in zip(here, (fold_even, fold_odd)):
                    value = fold(get, t, i)
                    c5[n, a, i] = value * m5[a] if n else value
        return carry

    lax.fori_loop(0, MID, fold5, 0)
    for i in range(4):
        c5[1, 2 * MID, i] = pltpu.roll(c5[1, 2 * MID - 1, i], 64, 1)

    def table5(a, carry):
        bc = [c5[1, a, i] for i in range(4)]
        mask = m5[a]
        for i in range(4):
            be = bc[i + 1] if i < 3 else jnp.where(subs5 == 7, 0.0, next_group(bc[0]))
            bw = bc[i - 1] if i > 0 else jnp.where(subs5 == 0, 0.0, last_group(bc[3]))
            bu = jnp.where(up_end, 0.0, pltpu.roll(bc[i], 127, 1))
            bd = jnp.where(down_end, 0.0, pltpu.roll(bc[i], 1, 1))
            c = [0.03125 * (bc[i] + v) for v in (be, bw, c5[1, a + 1, i], c5[1, a - 1, i], bu, bd)]
            inv = mask / (c5[0, a, i] + c[0] + c[1] + c[2] + c[3] + c[4] + c[5])
            t5[0, a, i] = c[0] * inv if i < 3 else jnp.where(subs5 == 7, 0.0, c[0] * inv)
            t5[1, a, i] = c[1] * inv if i > 0 else jnp.where(subs5 == 0, 0.0, c[1] * inv)
            t5[2, a, i] = c[2] * inv
            t5[3, a, i] = c[3] * inv
            t5[4, a, i] = jnp.where(up_end, 0.0, c[4] * inv)
            t5[5, a, i] = jnp.where(down_end, 0.0, c[5] * inv)
            inv5[a, i] = inv
        return carry

    lax.fori_loop(1, 2 * MID, table5, 0)


    fc = []
    for k, (first, last) in enumerate(((MID - 3, MID + 3), (1, MID - 4), (MID + 4, SPAN - 2))):
        for copy, db in zip(fb, fb_from):
            if first <= MID - db <= last:
                copy.wait_recv()
        span = pl.ds(first, last - first + 1)
        fc.append(
            remote(g5f.at[span, :, mine, :], g5f.at[span, :, mine, :], s_fc.at[k], r_fc.at[k], partner)
        )
    started += fc
    for copy in p4_boxes:
        copy.wait_recv()
    p4_groups = groups4(p4, s_p4, r_p4)
    started += p4_groups

    bottom_middle, bottom_pairs = coefficients(BOTTOM, BOTTOM_LOW)
    for m, (c1, c2) in enumerate(bottom_pairs):
        ends[m, 0] = F32(c1)
        ends[m, 1] = F32(c2)
    for copy in fc:
        copy.wait_recv()
    for a in range(1, 2 * MID):
        for i in range(4):
            folded = (fold_odd if a % 2 else fold_even)(lambda k, i: g5f[k, i], a // 2, i)
            fd = folded * inv5[a, i]
            fd5[a, i] = fd
            x5b[a, i] = fd * (1.0 / bottom_middle)

    def sweep5(now, old, first, c1, c2):
        for a in range(first, 2 * MID):
            x = [now[a, i] for i in range(4)]
            for i in range(4):
                east = x[i + 1] if i < 3 else next_group(x[0])
                west = x[i - 1] if i > 0 else last_group(x[3])
                inward = now[a + 1, i] if a < 2 * MID - 1 else pltpu.roll(x[i], 64, 1)
                total = fd5[a, i] - x[i]
                total = total + t5[0, a, i] * east + t5[1, a, i] * west
                total = total + t5[2, a, i] * inward + t5[3, a, i] * now[a - 1, i]
                total = total + t5[4, a, i] * pltpu.roll(x[i], 127, 1) + t5[5, a, i] * pltpu.roll(x[i], 1, 1)
                old[a, i] = x[i] + c1 * (x[i] - old[a, i]) + c2 * total

    def two(first):
        def body(k, carry):
            m = first + 2 * k
            sweep5(x5b, x5a, first + 2, ends[m, 0], ends[m, 1])
            sweep5(x5a, x5b, first + 3, ends[m + 1, 0], ends[m + 1, 1])
            return carry

        return body

    for first in range(0, 14, 2):
        two(first)(0, 0)
    sweep5(x5b, x5a, 16, ends[14, 0], ends[14, 1])

    for a in range(10):
        row = a - 3
        group = lax.rem(g + (row // 4) + NG, NG)
        at = 4 * lax.rem(group, 2) + group // 2
        for k in range(4):
            line = jnp.broadcast_to(x5a[16 + k, row % 4, pl.ds(at, 1), :], (2, 128))
            q4[a, 2 * k : 2 * k + 2, :] = line
            q4[a, 14 - 2 * k : 16 - 2 * k, :] = line
    grown = dot(q4[...].reshape(160, 128), spread).reshape(10, 16, 256)
    rows4 = lax.broadcasted_iota(jnp.int32, (16, 128), 0)
    first_half = rows4 < 8
    for copy in p4_groups:
        copy.wait_recv()
    for a in range(10):
        line = jnp.where(first_half, grown[a, :, 0:128], grown[a, :, 128:256])
        for r in (2 * a, 2 * a + 1):
            x4b[r] = jnp.where(m4, p4[1, r] + line, 0.0) * row_in(r, 8, 6)
            if 1 <= r < 19:
                fd4[r] = p4[0, r] * inv4[r]
    sweep(t4, fd4, x4b, x4a, 1, 19, 18, (1.0 / smooth_middle,))
    sweep(t4, fd4, x4a, x4b, 2, 18, 16, smooth_pairs[0])
    sweep(t4, fd4, x4b, x4a, 3, 17, 14, smooth_pairs[1])
    sweep(t4, fd4, x4a, x4b, 4, 16, 12, smooth_pairs[2])

    grown = dot(x4b[4:16, 4:12, :].reshape(96, 128), spread).reshape(12, 8, 256)
    for r in range(12):
        for k in range(2):
            line = grown[r, :, 128 * k : 128 * k + 128]
            u4[k, r, pl.ds(0, 8, stride=2), :] = line
            u4[k, r, pl.ds(1, 8, stride=2), :] = line
    for copy in x3_groups:
        copy.wait_recv()
    for r in range(24):
        row = row_in(r, N0, 4)
        for k in range(2):
            lanes = slice(128 * k, 128 * k + 128)
            x3b[r, :, lanes] = jnp.where(m3c[:, lanes], (h3[r, :, lanes] + u4[k, r // 2]) * row, 0.0)
    sweep(t3, fd3, x3b, x3a, 1, 23, 11, (1.0 / smooth_middle,))
    sweep(t3, fd3, x3a, x3b, 2, 22, 10, smooth_pairs[0])
    sweep(t3, fd3, x3b, x3a, 3, 21, 9, smooth_pairs[1])
    for copy in started:
        copy.wait_send()

    def last(k, carry):
        for i in range(8):
            r = 4 + 8 * k + i
            total = scaled_residual(t3, fd3, x3a, r)
            here = x3a[r]
            line = here + smooth_pairs[2][0] * (here - x3b[r]) + smooth_pairs[2][1] * total
            out[r - 4] = line[4:12]
        return carry

    lax.fori_loop(0, 2, last, 0)


SCRATCH = (
    [pltpu.VMEM(shape, F32) for shape in (
        (26, 8, 256), (2, 24, 8, 256), (6, 24, 8, 256), (24, 8, 256), (2, 24, 8, 256), (2, 24, 8, 256),
        (26, 8, 256), (2, 24, 8, 256),
        (24, 16, 256), (24, 16, 256), (26, 24, 256), (6, 24, 16, 256), (24, 16, 256), (24, 16, 256),
        (24, 16, 256), (24, 16, 256), (24, 16, 256),
        (2, 20, 16, 128), (20, 16, 128), (2, 20, 16, 128), (6, 20, 16, 128), (20, 16, 128), (20, 16, 128),
        (20, 16, 128), (20, 16, 128), (20, 16, 128), (8, 16, 128),
        (8, 256), (2, SPAN, 4, 8, 128), (SPAN, 4, 8, 128),
        (SPAN, 8, 128), (2, SPAN, 4, 8, 128), (6, SPAN, 4, 8, 128), (SPAN, 4, 8, 128),
        (SPAN, 4, 8, 128), (SPAN, 4, 8, 128), (SPAN, 4, 8, 128), (10, 16, 128), (8, 16, 256),
        (2, 12, 16, 128),
    )]
    + [pltpu.SemaphoreType.DMA((3,)), pltpu.SemaphoreType.REGULAR((2,)), pltpu.SMEM((16, 2), F32)]
    + [pltpu.SemaphoreType.DMA(shape) for count in (
        (3, 8), (2,), (2, 2), (6,), (8,), (4,), (6,), (4,), (2 * MID,), (1,), (3,), (2 * REACH,), (3,)
    ) for shape in (count, count)]
)


def cycle(source, alpha, beta):
    return pl.pallas_call(
        kernel,
        out_shape=pltpu.VMEM((N0, N1, N2), F32),
        in_specs=[pl.BlockSpec(memory_space=pl.ANY)] * 3,
        out_specs=pl.BlockSpec(memory_space=pltpu.VMEM),
        scratch_shapes=SCRATCH,
        compiler_params=pltpu.CompilerParams(
            collective_id=0, has_side_effects=True, vmem_limit_bytes=63 << 20
        ),
        name="vcycle",
    )(source, alpha, beta)


def solution(mesh):
    spec = P("grp", "box", None)
    return jax.shard_map(cycle, mesh=mesh, in_specs=(spec,) * 3, out_specs=spec, check_vma=False)
```
